256 devices in a mesh: dp: 8 (over z), expert: 32 (over y, x, core).
Axes of the slice: x: 4, y: 4, z: 8, core: 2. Of those that a mesh axis runs over, the one named last changes fastest.
Arguments:
- queries: bfloat16 [512, 32, 576], P(('dp', 'expert')), may hold values from -32 to 32
- new_latent: bfloat16 [512, 576], P(('dp', 'expert')), may hold values from -4 to 4
- pool_pages: bfloat16 [1536, 576, 128], P(('dp', 'expert')), may hold values from -4 to 4
- page_owner: int32 [8, 32, 2, 8], P(None, 'expert'), may hold values from 0 to 7, as said below
- page_slot: int32 [8, 32, 2, 8], P(None, 'expert'), may hold values from 0 to 5
- lengths: int32 [512], P(('dp', 'expert')), may hold values from 128 to 1024, as said below
- residual: bfloat16 [512, 7168], P('dp', 'expert'), may hold values from -20 to 20
- value_weight: bfloat16 [32, 512, 128], replicated, may hold values from -1 to 1
- output_weight: bfloat16 [4096, 7168], P(None, 'expert'), may hold values from -0.09375 to 0.09375
- norm_gain: float32 [7168], P('expert'), may hold values from 0.25 to 1.75
- expert_ids: int32 [512, 8], P('dp'), may hold values from 0 to 31, all different within a row; in each aligned block of 64 rows (0 to 63, 64 to 127, ...) at most 24 rows name the same one
- route_gates: float32 [512, 8], P('dp'), may hold values from 0.05 to 0.4
- expert_in: bfloat16 [32, 7168, 2, 1024], P('dp', 'expert'), may hold values from -0.0625 to 0.0625
- expert_out: bfloat16 [32, 1024, 7168], P('dp', None, 'expert'), may hold values from -0.1875 to 0.1875
Outputs:
- mixed: bfloat16 [512, 7168], P('dp', 'expert')
The draws below stay inside these ranges and needn't reach their ends.
Inputs may be any that keep to these rules, and one draw needn't show every extreme that they name: `expert_ids`: in each aligned block of 64 rows (the rows of one index of dp) a row names 8 different experts and no expert is named by more than 24 rows. `page_owner`: among the 16 page entries of the rows of one device, no index of dp is named more than 3 times, and in every such set one index is named exactly 3 times. `lengths`: in every attention group some row has exactly 1024 tokens and some row exactly 128.
All inputs are finite; a program needn't handle non-finite values.
Results may differ from the reference program's by a relative error of at most 0.0075.
Values may be sent and summed in bfloat16 or wider, within the bound.
A program may use at most 128 MiB of HBM per device.

```python
import math
from functools import partial
import jax
import jax.numpy as jnp
import numpy as np
from jax import lax

D = 7168
HEADS = 32
KVR = 512
ROPE = 64
DV = 128
PAGE = 128
FF = 1024
TOP = 8
ROWS_DEV = 2
MAXP = 8
LAT = 576
GROUPS = 8
COLUMNS = 32
GROUP = 64
TOKENS = 512
EXPERTS = 32
CAPX = 24
CAPP = 3
P_DEV = 6
POOL = 1536


def page_owners(key):
    base_key = jax.random.fold_in(key, 101)
    device_keys = jax.random.split(base_key, GROUPS * COLUMNS)
    requests = ROWS_DEV * MAXP
    pool_owner = jnp.arange(GROUPS * CAPP, dtype=jnp.int32) // CAPP

    def one_device(device_key):
        busy_key, order_key, place_key = jax.random.split(device_key, 3)
        busiest = jax.random.randint(busy_key, (), 0, GROUPS)
        priority = jax.random.permutation(order_key, GROUPS * CAPP).astype(jnp.int32)
        priority = priority - GROUPS * CAPP * (pool_owner == busiest).astype(jnp.int32)
        chosen = pool_owner[jnp.argsort(priority, stable=True)[:requests]]
        return chosen[jax.random.permutation(place_key, requests)]
    return jax.vmap(one_device)(device_keys).reshape(GROUPS, COLUMNS, ROWS_DEV, MAXP)


def page_locals(key):
    return jax.random.randint(jax.random.fold_in(key, 303), (GROUPS, COLUMNS, ROWS_DEV, MAXP), 0, P_DEV)


def pool_values(key):
    pool_data = jnp.clip(jax.random.normal(jax.random.fold_in(key, 202), (POOL, LAT, PAGE), jnp.float32), -4.0, 4.0)
    second = pool_data[:, :, 1]
    pool_data = pool_data.at[:, :, 1].set(second)
    return jnp.clip(pool_data, -4.0, 4.0)


def draw_pool_pages(key, part):
    return pool_values(key).astype(jnp.bfloat16)


def draw_page_owner(key, part):
    return page_owners(key)


def draw_page_slot(key, part):
    return page_locals(key)


def draw_queries(key, part):
    own_key = jax.random.fold_in(key, 5)
    return jnp.clip(0.5 * jax.random.normal(own_key, (TOKENS, HEADS, LAT), jnp.float32), -2.0, 2.0).astype(jnp.bfloat16)


def draw_lengths(key, part):
    key = jax.random.fold_in(key, 404)
    spans_key, longest_key = jax.random.split(key)
    row_spans = jax.random.randint(spans_key, (GROUPS, GROUP), PAGE, MAXP * PAGE + 1)
    longest = jax.random.randint(longest_key, (GROUPS, 1), 0, GROUP)
    positions = jnp.arange(GROUP, dtype=jnp.int32)[None, :]
    row_spans = jnp.where(positions == longest, MAXP * PAGE, row_spans)
    row_spans = jnp.where(positions == (longest + 1) % GROUP, PAGE, row_spans)
    return row_spans.reshape(TOKENS)


def draw_residual(key, part):
    key = jax.random.fold_in(key, 505)
    value_key, spread_key = jax.random.split(key, 2)
    col_ramp = jnp.exp(0.5 * jnp.log(3.0) * jnp.arange(D, dtype=jnp.float32) / D)
    spread = jnp.exp(jnp.log(3.2) * jax.random.uniform(spread_key, (D,), jnp.float32))
    base_values = jnp.clip(jax.random.normal(value_key, (TOKENS, D), jnp.float32), -4.0, 4.0)
    return (0.5 * base_values * col_ramp[None, :] * spread[None, :]).astype(jnp.bfloat16)


def block_scale(key, extent, cuts, low, top_value):
    gain = 1.0
    for axis_at, blocks in cuts:
        heights = jax.random.uniform(jax.random.fold_in(jax.random.fold_in(key, 6), axis_at), (blocks,), jnp.float32, low / len(cuts), top_value / len(cuts))
        gain = gain * jnp.repeat(jnp.exp(heights), extent[axis_at] // blocks).reshape((-1,) + (1,) * (len(extent) - 1 - axis_at))
    return gain


def routed_block(stream_key, own, number, rows, number_of, top, reach, skew):
    ranking = jax.random.permutation(stream_key, number_of)
    crowded, ordinary = shares(number_of, rows * top, reach, skew, True), shares(number_of, rows * top, reach, skew, False)
    places = jnp.arange(number_of)

    def named(sizes, rotation):
        used = int((sizes > 0).sum())
        fixed = max(1, used // 4)
        moved = fixed + (places - fixed + rotation * (used - fixed)) % max(1, number_of - fixed)
        return jnp.zeros((number_of,), jnp.int32).at[ranking[jnp.where(places < fixed, places, moved)]].set(jnp.asarray(sizes, jnp.int32))

    sizes = jnp.where(number % 4 == 0, named(crowded, number // 4), named(ordinary, number - number // 4 - 1))
    mixed = jax.random.permutation(jax.random.fold_in(own, 3), number_of)
    source_of, sink = mixed[0:number_of // 2 * 2:2], mixed[1:number_of // 2 * 2:2]
    margin = jnp.minimum(sizes[source_of] - 1, reach - sizes[sink]) // 2
    margin = jnp.where((source_of == ranking[0]) | (sink == ranking[0]) | (sizes[sink] == 0), 0, jnp.maximum(margin, 0))
    moved = jax.random.randint(jax.random.fold_in(own, 4), (number_of // 2,), 0, 1 << 20) % (margin + 1)
    sizes = sizes.at[source_of].add(-moved).at[sink].add(moved)
    items = jnp.searchsorted(jnp.cumsum(sizes), jnp.arange(rows * top), side="right").astype(jnp.int32)
    table = items.reshape(top, rows).T
    table = table[jax.random.permutation(jax.random.fold_in(own, 1), rows)]
    rotation = jax.random.randint(jax.random.fold_in(own, 2), (rows, 1), 0, top)
    return jnp.take_along_axis(table, (jnp.arange(top)[None, :] + rotation) % top, axis=1)


def shares(amount, total, bound, skew, full):
    portions = [(1 << 20) // math.isqrt(standing ** skew) + 1 for standing in range(1, amount + 1)]
    largest = bound if full else min(bound, max(-(-total // amount), total * portions[0] // sum(portions)))
    least = 1 if total - largest >= amount - 1 else 0
    counts, surplus = [largest] + [least] * (amount - 1), total - largest - least * (amount - 1)
    while surplus > 0:
        candidates = [i for i in range(1, amount) if counts[i] < largest] or [i for i in range(1, amount) if counts[i] < bound]
        pool, remaining = sum([portions[i] for i in candidates]), surplus
        for i in candidates:
            extra = min(bound - counts[i], max(1, remaining * portions[i] // pool), surplus)
            counts[i] = counts[i] + extra
            surplus = surplus - extra
    return np.array(counts)


def noise(rng, dims, width, bound, cuts=(), kind=jnp.bfloat16):
    result = jax.random.normal(rng, dims, jnp.float32) * width
    if len(cuts) > 0:
        result = block_scale(rng, dims, cuts, -0.22, 0.18) * result
    return jnp.clip(result, min=-bound, max=bound).astype(kind)


def setup_inputs(seed: int = 0) -> dict:
    splits = jax.random.split(jax.random.key(seed), 15)
    queries = draw_queries(jax.random.fold_in(splits[14], 71), 0)
    new_latent = noise(splits[1], (TOKENS, LAT), 1.0, 4.0, ((0, 256),))
    pool_pages = draw_pool_pages(jax.random.fold_in(splits[14], 71), 0)
    page_owner = draw_page_owner(jax.random.fold_in(splits[14], 71), 0)
    page_slot = draw_page_slot(jax.random.fold_in(splits[14], 71), 0)
    lengths = draw_lengths(jax.random.fold_in(splits[14], 71), 0)
    residual = draw_residual(jax.random.fold_in(splits[14], 71), 0)
    value_weight = noise(splits[7], (HEADS, KVR, DV), (KVR // 16) ** -0.5, 1.0)
    output_weight = noise(splits[8], (HEADS * DV, D), (HEADS * DV) ** -0.5, 0.09375, ((1, 32),))
    norm_gain = jnp.clip(1.0 + 0.15 * jax.random.normal(splits[9], (D,), jnp.float32), 0.25, 1.75)
    expert_ids_keys = jax.random.split(jax.random.fold_in(splits[10], 1), TOKENS // GROUP)
    expert_ids_turns = jax.random.permutation(jax.random.fold_in(splits[10], 3), TOKENS // GROUP)
    expert_ids = jax.vmap(lambda own, number: routed_block(jax.random.fold_in(splits[10], 2), own, number, GROUP, EXPERTS, TOP, CAPX, 2))(expert_ids_keys, expert_ids_turns).reshape((TOKENS, TOP))
    route_gates = jnp.clip(jnp.exp(math.log(0.4) - 2.0794415 * jax.random.uniform(splits[11], (TOKENS, TOP), jnp.float32) ** block_scale(splits[11], (TOKENS, TOP), ((0, 8),), -0.2, 0.2)), 0.05, 0.4)
    expert_in = noise(splits[12], (EXPERTS, D, 2, FF), D ** -0.5, 0.0625, ((0, 8), (1, 32)))
    expert_out = noise(splits[13], (EXPERTS, FF, D), FF ** -0.5, 0.1875, ((0, 8), (2, 32)))
    return dict(queries=queries, new_latent=new_latent, pool_pages=pool_pages, page_owner=page_owner, page_slot=page_slot, lengths=lengths, residual=residual, value_weight=value_weight, output_weight=output_weight, norm_gain=norm_gain, expert_ids=expert_ids, route_gates=route_gates, expert_in=expert_in, expert_out=expert_out)


epsilon = 1e-06

def route_tables(expert_ids, experts, capacity):
    group_rows, chosen = expert_ids.shape
    flattened = expert_ids.reshape(-1)
    matches = (flattened[:, None] == jnp.arange(experts, dtype=jnp.int32)[None, :]).astype(jnp.int32)
    earlier = lax.optimization_barrier(jnp.sum((jnp.cumsum(matches, axis=0) - matches) * matches, axis=1))
    target_index = (flattened * capacity + earlier).astype(jnp.int32)
    source_rows = jnp.arange(group_rows * chosen, dtype=jnp.int32) // chosen
    source_table = jnp.full((experts * capacity,), group_rows, jnp.int32).at[target_index].set(source_rows)
    return (target_index.reshape(group_rows, chosen), source_table)

def attend(operands, pool_pages):
    query_row, new_row, page_index, length = operands
    page_keys = pool_pages[page_index]
    score_scale = (DV + ROPE) ** (-0.5)
    keys_wide = page_keys.astype(jnp.float32)
    scores = jnp.einsum('hc,pct->hpt', query_row.astype(jnp.float32), keys_wide) * score_scale
    self_score = jnp.einsum('hc,c->h', query_row.astype(jnp.float32), new_row.astype(jnp.float32)) * score_scale
    position = jnp.arange(MAXP, dtype=jnp.int32)[:, None] * PAGE + jnp.arange(PAGE, dtype=jnp.int32)[None, :]
    valid = position < length
    scores = jnp.where(valid[None], scores, -jnp.inf)
    highest = jnp.maximum(lax.optimization_barrier(jnp.max(scores, axis=(1, 2))), self_score)
    expo = jnp.exp(scores - highest[:, None, None])
    self_expo = jnp.exp(self_score - highest)
    denominator = lax.optimization_barrier(jnp.sum(expo, axis=(1, 2))) + self_expo
    weights = (expo / denominator[:, None, None]).astype(jnp.bfloat16)
    self_weight = (self_expo / denominator).astype(jnp.bfloat16)
    summed = jnp.einsum('hpt,pct->hc', weights.astype(jnp.float32), keys_wide)
    summed = summed + self_weight.astype(jnp.float32)[:, None] * new_row.astype(jnp.float32)[None, :]
    return summed[:, :KVR].astype(jnp.bfloat16)

def reference(queries, new_latent, pool_pages, page_owner, page_slot, lengths, residual, value_weight, output_weight, norm_gain, expert_ids, route_gates, expert_in, expert_out):
    column = jnp.arange(COLUMNS, dtype=jnp.int32)[None, :, None, None]
    page_index = ((page_owner * COLUMNS + column) * P_DEV + page_slot).reshape(TOKENS, MAXP).astype(jnp.int32)
    latent_out = lax.map(partial(attend, pool_pages=pool_pages), (queries, new_latent, page_index, lengths))
    head_values = jnp.einsum('thc,hcv->thv', latent_out.astype(jnp.float32), value_weight.astype(jnp.float32))
    head_values = head_values.astype(jnp.bfloat16).reshape(TOKENS, HEADS * DV)
    projected = jnp.dot(head_values, output_weight, preferred_element_type=jnp.float32)
    resid = (residual.astype(jnp.float32) + projected).astype(jnp.bfloat16)
    values_wide = resid.astype(jnp.float32)
    inverse = lax.rsqrt(lax.optimization_barrier(jnp.sum(values_wide * values_wide, axis=1)) / D + epsilon)
    scaled = (values_wide * norm_gain[None, :]).astype(jnp.bfloat16)
    grouped_ids = expert_ids.reshape(GROUPS, GROUP, TOP)
    targets, tables = jax.vmap(partial(route_tables, experts=EXPERTS, capacity=CAPX))(grouped_ids)
    offsets = jnp.arange(GROUPS, dtype=jnp.int32)[:, None] * GROUP
    global_rows = jnp.where(tables == GROUP, TOKENS, tables + offsets).astype(jnp.int32)
    per_expert = global_rows.reshape(GROUPS, EXPERTS, CAPX).transpose(1, 0, 2).reshape(EXPERTS, GROUPS * CAPX)
    scaled_pad = jnp.concatenate([scaled, jnp.zeros((1, D), jnp.bfloat16)], axis=0)
    inverse_pad = jnp.concatenate([inverse, jnp.zeros((1,), jnp.float32)], axis=0)

    def expert_step(operands):
        indices, weight_in, weight_out = operands
        gate_up = jnp.dot(scaled_pad[indices], weight_in.reshape(D, 2 * FF), preferred_element_type=jnp.float32)
        gate_up = gate_up.reshape(-1, 2, FF) * inverse_pad[indices][:, None, None]
        hidden = (jax.nn.silu(gate_up[:, 0]) * gate_up[:, 1]).astype(jnp.bfloat16)
        return jnp.dot(hidden, weight_out, preferred_element_type=jnp.float32).astype(jnp.bfloat16)
    outputs = lax.map(expert_step, (per_expert, expert_in, expert_out))
    expert_index = targets // CAPX
    slot_index = targets % CAPX
    group_index = jnp.arange(GROUPS, dtype=jnp.int32)[:, None, None]
    picked = outputs[expert_index, group_index * CAPX + slot_index]
    gates = route_gates.reshape(GROUPS, GROUP, TOP)
    combined = lax.optimization_barrier(jnp.sum(gates[..., None] * picked.astype(jnp.float32), axis=2)).reshape(TOKENS, D)
    return (values_wide + combined).astype(jnp.bfloat16)
```

```python
import functools
import jax
import jax.numpy as jnp
from jax import lax
from jax.experimental import pallas as pl
from jax.experimental.pallas import tpu as pltpu
from jax.sharding import PartitionSpec as P

D = 7168
KVR = 512
ROPE = 64
DV = 128
TOP = 8
EPS = 1e-06
MESH = pl.DeviceIdType.MESH
F32 = jnp.float32
BF16 = jnp.bfloat16
NEG = -1e30


def iota(shape, dim):
    return lax.broadcasted_iota(jnp.int32, shape, dim)


def mm(a, b):
    return jnp.dot(a, b, preferred_element_type=F32)


def mm_nt(a, b):
    return lax.dot_general(a, b, (((1,), (1,)), ((), ())), preferred_element_type=F32)


def kernel(
    G, C, ELOC, CAPX,
    q_hbm, nl_ref, pool_hbm, owner_ref, slot_ref, len_ref, res_ref, wv_hbm, wo_hbm, gain_ref,
    ids_ref, gates_ref, win_hbm, wout_hbm,
    out_ref,
    kc, vt, nlp, q_all, sml_s, sml_r, perm, perm_t, o_all, o_hm, hv_hm, hv_s, lse_s, hv_r, lse_r,
    hva, xmat, wv, wo, win, wg, wout, xall, xsib, sq_s, sq_r, inv_s, inv_r,
    sel, sel_t, gcol, part, prs, hid, vown, vsib, zsib_s, zsib_r, zs, zr, zown,
    lsem, s_q, r_q, s_sml, r_sml, s_hv, r_hv, s_lse, r_lse, s_x, r_x, s_inv, r_inv, s_z, r_z,
    s_hva, r_hva, s_sq, r_sq, s_prs, r_prs, s_hid, r_hid, s_fw, r_fw, s_w, r_w,
):
    g = lax.axis_index("dp")
    k = lax.axis_index("expert")
    core = lax.rem(k, 2)
    chip = lax.div(k, 2)
    sib = k + 1 - 2 * core
    NC = C // 2
    ROWS, H, LAT = q_all.shape[1:]
    NS = pool_hbm.shape[0]
    PAGE = pool_hbm.shape[2]
    RH = ROWS * H
    GROUP = C * ROWS
    W = res_ref.shape[1]
    FF = win_hbm.shape[3]
    FH = FF // 2
    ESL = G * CAPX
    RCH = ELOC * ESL // NC
    CPE = NC // ELOC
    NR = G * ROWS

    def dp_peer(d):
        half = lax.div(d + 1, 2)
        off = half * (2 * lax.rem(d, 2) - 1)
        return lax.rem(g + off + G, G)

    def ex_peer(d):
        return lax.rem(k + d, C)

    def chip_peer(d):
        return lax.rem(chip + d, NC)

    def rcopy(src, dst, ss, rs, dev):
        return pltpu.make_async_remote_copy(
            src_ref=src, dst_ref=dst, send_sem=ss, recv_sem=rs, device_id=dev, device_id_type=MESH
        )

    def loop(lo, hi, fn):
        lax.fori_loop(lo, hi, lambda i, c: (fn(i), c)[1], 0)

    def exp_dev(kk):
        return (g, kk)

    def dp_dev(j):
        return (j, k)

    locals_ = []
    for s in range(NS):
        locals_.append(
            pltpu.make_async_copy(pool_hbm.at[s], kc.at[:, pl.ds(s * PAGE, PAGE)], lsem.at[s])
        )
    c_q = pltpu.make_async_copy(q_hbm, q_all.at[g], lsem.at[NS])
    c_win = pltpu.make_async_copy(
        win_hbm.at[:, :, :, pl.ds(pl.multiple_of(core * FH, FH), FH)], win.at[0], lsem.at[NS + 1]
    )
    c_wv = pltpu.make_async_copy(wv_hbm, wv, lsem.at[NS + 2])
    c_wo = pltpu.make_async_copy(wo_hbm, wo, lsem.at[NS + 3])
    c_wout = pltpu.make_async_copy(
        wout_hbm.at[:, :, pl.ds(pl.multiple_of(core * FH, FH), FH)], wout.at[0], lsem.at[NS + 4]
    )
    c_q.start()
    for c in locals_:
        c.start()
    for c in (c_win, c_wv, c_wo, c_wout):
        c.start()

    barrier = pltpu.get_barrier_semaphore()

    def sig_dp(d):
        pl.semaphore_signal(barrier, inc=1, device_id=dp_dev(lax.rem(g + d, G)), device_id_type=MESH)

    def sig_ex(d):
        pl.semaphore_signal(barrier, inc=1, device_id=exp_dev(ex_peer(d)), device_id_type=MESH)

    loop(1, G, sig_dp)
    loop(1, C, sig_ex)

    ids = ids_ref[...]
    gates = gates_ref[...]
    e_iota = iota((G * ELOC, GROUP), 0)
    named = jnp.zeros((G * ELOC, GROUP), F32)
    gval = jnp.zeros((G * ELOC, GROUP), F32)
    for t in range(TOP):
        hit = ids[t : t + 1, :] == e_iota
        named = named + hit.astype(F32)
        gval = gval + jnp.where(hit, gates[t : t + 1, :], 0.0)
    tri = (iota((GROUP, GROUP), 0) < iota((GROUP, GROUP), 1)).astype(BF16)
    rank = mm(named.astype(BF16), tri)
    code = jnp.where(named > 0, rank, -1.0)
    lane = iota((8, 128), 0)
    lens = jnp.where(lane == 0, len_ref[0], len_ref[1]).astype(F32)
    sml_s[...] = jnp.zeros_like(sml_s)
    for j in range(G):
        sml_s[j, 0:ELOC, 0:GROUP] = code[j * ELOC : (j + 1) * ELOC]
        sml_s[j, ELOC : 2 * ELOC, 0:GROUP] = gval[j * ELOC : (j + 1) * ELOC]
        sml_s[j, 8:16, :] = lens
    sml_r[g] = sml_s[g]

    c_q.wait()
    pl.semaphore_wait(barrier, G - 1 + C - 1)

    def send_q(d):
        j = dp_peer(d)
        rcopy(sml_s.at[j], sml_r.at[g], s_sml.at[j], r_sml.at[g], dp_dev(j)).start()
        rcopy(q_all.at[g], q_all.at[g], s_q.at[j], r_q.at[g], dp_dev(j)).start()

    loop(1, G, send_q)

    other = pl.multiple_of((1 - core) * FH, FH)
    w1 = rcopy(win_hbm.at[:, :, :, pl.ds(other, FH)], win.at[1], s_w.at[0], r_w.at[0], exp_dev(sib))
    w2 = rcopy(wout_hbm.at[:, :, pl.ds(other, FH)], wout.at[1], s_w.at[1], r_w.at[1], exp_dev(sib))
    w1.start()
    w2.start()

    N2 = NR * H
    pr = iota((N2, 1), 0)
    perm[...] = (iota((N2, N2), 1) == lax.rem(pr, NR) * H + lax.div(pr, NR)).astype(BF16)
    perm_t[...] = (iota((N2, N2), 1) == lax.rem(pr, H) * NR + lax.div(pr, H)).astype(BF16)
    nl = nl_ref[...].astype(F32)
    nrow = iota((128, LAT), 0)
    nacc = jnp.zeros((128, LAT), F32)
    for s in range(ROWS):
        nacc = jnp.where(nrow == s, nl[s : s + 1, :], nacc)
    nlp[...] = nacc.astype(BF16)
    for c in locals_:
        c.wait()
    vt[...] = kc[0:KVR, :].T

    scale = (DV + ROPE) ** (-0.5)
    NT = NS * PAGE

    def attend(src, own):
        q = q_all[src].reshape(RH, LAT)
        sc = mm(q, kc[...]) * scale
        lid = iota((1, NT), 1)
        slot_lane = lax.div(lid, PAGE)
        tpos = lax.rem(lid, PAGE).astype(F32)
        rows = []
        lv = sml_r[src, 8:16, :]
        for s in range(ROWS):
            ln = lv[s : s + 1, 0:1]
            cnt = jnp.zeros((1, NT), F32)
            for p in range(owner_ref.shape[3]):
                here = jnp.where(owner_ref[src, 0, s, p] == g, slot_ref[src, 0, s, p], -1)
                ok = jnp.logical_and(slot_lane == here, tpos + float(p * PAGE) < ln)
                cnt = cnt + ok.astype(F32)
            rows.append(jnp.broadcast_to(cnt, (H, NT)))
        cnt = jnp.concatenate(rows, axis=0)
        scm = jnp.where(cnt > 0, sc, NEG)
        top = jnp.max(scm, axis=1, keepdims=True)
        if own:
            cs = (iota((RH, 128), 1) == lax.div(iota((RH, 128), 0), H)).astype(F32)
            ss = jnp.where(cs > 0, mm_nt(q, nlp[...]) * scale, NEG)
            top = jnp.maximum(top, jnp.max(ss, axis=1, keepdims=True))
        p = cnt * jnp.exp(scm - top)
        den = jnp.sum(p, axis=1, keepdims=True)
        acc = mm(p.astype(BF16), vt[...])
        if own:
            pself = cs * jnp.exp(ss - top)
            den = den + jnp.sum(pself, axis=1, keepdims=True)
            acc = acc + mm(pself.astype(BF16), nlp[:, 0:KVR])
        has = den > 0
        inv_den = jnp.where(has, 1.0 / jnp.where(has, den, 1.0), 0.0)
        lse = jnp.where(has, top + jnp.log(jnp.where(has, den, 1.0)), NEG)
        o_all[pl.ds(pl.multiple_of(src * RH, RH), RH), :] = (acc * inv_den).astype(BF16)
        row = jnp.broadcast_to(lse, (RH, 128)).T[0:8]
        lse_s[src] = jnp.concatenate([row, row], axis=1)

    attend(g, True)

    c_win.wait()
    rcopy(win.at[1], win.at[1], s_w.at[0], r_w.at[0], exp_dev(sib)).wait_recv()
    col = iota((W, 2 * W), 1)
    two = 2 * iota((W, 2 * W), 0)
    pick_g = (col == two).astype(BF16)
    pick_u = (col == two + 1).astype(BF16)

    def split(i):
        e = lax.div(i, 2)
        o = lax.rem(i, 2)
        w = win[o, e].reshape(2 * W, FH)
        wg[e, o, :, 0:FH] = mm(pick_g, w).astype(BF16)
        wg[e, o, :, FH : 2 * FH] = mm(pick_u, w).astype(BF16)

    loop(0, 2 * ELOC, split)

    def chunk(d):
        src = dp_peer(d)
        rcopy(sml_r.at[src], sml_r.at[src], s_sml.at[src], r_sml.at[src], dp_dev(src)).wait_recv()
        rcopy(q_all.at[src], q_all.at[src], s_q.at[src], r_q.at[src], dp_dev(src)).wait_recv()
        attend(src, False)

    loop(1, G, chunk)

    o_hm[...] = mm(perm[...], o_all[...]).astype(BF16)
    c_wv.wait()
    HB = 8

    def project(b):
        for i in range(HB):
            h = b * HB + i
            at = pl.ds(pl.multiple_of(h * NR, NR), NR)
            hv_hm[at, :] = mm(o_hm[at, :], wv[h]).astype(BF16)

    loop(0, H // HB, project)
    hv_s[...] = mm(perm_t[...], hv_hm[...]).astype(BF16).reshape(G, RH, DV)
    hv_r[g] = hv_s[g]
    lse_r[g] = lse_s[g]

    def send_hv(d):
        j = dp_peer(d)
        rcopy(lse_s.at[j], lse_r.at[g], s_lse.at[j], r_lse.at[g], dp_dev(j)).start()
        rcopy(hv_s.at[j], hv_r.at[g], s_hv.at[j], r_hv.at[g], dp_dev(j)).start()

    loop(1, G, send_hv)

    siota = iota((ESL, G * GROUP), 0).astype(F32)
    for e in range(ELOC):
        codes = []
        gvals = []
        for j in range(G):
            cj = sml_r[j, e : e + 1, 0:GROUP]
            codes.append(jnp.where(cj >= 0, cj + float(j * CAPX), -1.0))
            gvals.append(sml_r[j, ELOC + e : ELOC + e + 1, 0:GROUP])
        crow = jnp.concatenate(codes, axis=1)
        grow = jnp.concatenate(gvals, axis=1)
        hit = siota == crow
        sel[e] = hit.astype(F32).astype(BF16)
        gs = jnp.sum(jnp.where(hit, grow, 0.0), axis=1, keepdims=True)
        gcol[e] = jnp.broadcast_to(gs, (ESL, 128))
    sel_t[...] = sel[...].reshape(ELOC * ESL, G * GROUP).T

    def wait_hv(d):
        j = dp_peer(d)
        rcopy(lse_r.at[j], lse_r.at[j], s_lse.at[j], r_lse.at[j], dp_dev(j)).wait_recv()
        rcopy(hv_r.at[j], hv_r.at[j], s_hv.at[j], r_hv.at[j], dp_dev(j)).wait_recv()

    loop(1, G, wait_hv)
    riota = iota((8, 128), 0)
    ls = jnp.full((8, 128), NEG, F32)
    for j in range(G):
        ls = jnp.where(riota == j, lse_r[j], ls)
    wts = jnp.exp(ls - jnp.max(ls, axis=0, keepdims=True))
    wts = wts / jnp.sum(wts, axis=0, keepdims=True)
    wcol = wts.T
    comb = jnp.zeros((RH, DV), F32)
    for j in range(G):
        comb = comb + wcol[0:RH, j : j + 1] * hv_r[j].astype(F32)
    hva[k] = comb.astype(BF16)

    def send_hva(d):
        j = ex_peer(d)
        rcopy(hva.at[k], hva.at[k], s_hva.at[j], r_hva.at[k], exp_dev(j)).start()

    loop(1, C, send_hva)
    c_wo.wait()

    def wait_hva(d):
        j = ex_peer(d)
        rcopy(hva.at[j], hva.at[j], s_hva.at[j], r_hva.at[j], exp_dev(j)).wait_recv()

    loop(1, C, wait_hva)

    for b in range(C // G):
        blk = mm(perm[...], hva[b * G : (b + 1) * G].reshape(N2, DV)).astype(BF16)
        for h in range(H):
            xmat[b * NR : (b + 1) * NR, h * DV : (h + 1) * DV] = blk[h * NR : (h + 1) * NR]
    proj = mm_nt(xmat[...], wo[...])
    resid = (res_ref[...].astype(F32) + proj).astype(BF16).astype(F32)
    xall[g] = (resid * gain_ref[...].reshape(1, W)).astype(BF16)

    def send_x(d):
        j = dp_peer(d)
        rcopy(xall.at[g], xall.at[g], s_x.at[j], r_x.at[g], dp_dev(j)).start()

    def fwd(j):
        rcopy(xall.at[j], xsib.at[j], s_fw.at[j], r_fw.at[j], exp_dev(sib)).start()

    loop(1, G, send_x)
    fwd(g)
    sq = jnp.sum(resid * resid, axis=1, keepdims=True)
    sq_row = jnp.broadcast_to(sq, (GROUP, 128)).T[0:8]
    sq_s[...] = jnp.concatenate([sq_row] * (128 // GROUP), axis=1)
    sq_r[k] = sq_s[...]

    def send_sq(d):
        j = ex_peer(d)
        rcopy(sq_s, sq_r.at[k], s_sq.at[j], r_sq.at[k], exp_dev(j)).start()

    loop(1, C, send_sq)

    def pass_x(d):
        j = dp_peer(d)
        rcopy(xall.at[j], xall.at[j], s_x.at[j], r_x.at[j], dp_dev(j)).wait_recv()
        fwd(j)

    loop(1, G, pass_x)

    def wait_fw(j):
        rcopy(xsib.at[j], xsib.at[j], s_fw.at[j], r_fw.at[j], exp_dev(sib)).wait_recv()

    loop(0, G, wait_fw)

    e0 = lax.div(chip, CPE)

    def part_step(i):
        e = lax.rem(e0 + i, ELOC)
        xo = mm(sel[e], xall[...].reshape(G * GROUP, W)).astype(BF16)
        xs = mm(sel[e], xsib[...].reshape(G * GROUP, W)).astype(BF16)
        at = pl.ds(pl.multiple_of(e * ESL, 16), ESL)
        for f in range(2):
            cols = slice(f * FH, (f + 1) * FH)
            part[at, cols] = (mm(xo, wg[e, 0, :, cols]) + mm(xs, wg[e, 1, :, cols])).astype(BF16)

        def send(t):
            c = e * CPE + lax.rem(chip + t, CPE)

            @pl.when(c != chip)
            def _():
                rcopy(
                    part.at[pl.ds(pl.multiple_of(c * RCH, 16), RCH)], prs.at[chip],
                    s_prs.at[c], r_prs.at[chip], exp_dev(2 * c + core),
                ).start()

        loop(0, CPE, send)

    loop(0, ELOC, part_step)
    mine = pl.ds(pl.multiple_of(chip * RCH, 16), RCH)
    prs[chip] = part[mine, :]

    def wait_sq(d):
        j = ex_peer(d)
        rcopy(sq_r.at[j], sq_r.at[j], s_sq.at[j], r_sq.at[j], exp_dev(j)).wait_recv()

    loop(1, C, wait_sq)
    inv_s[...] = lax.rsqrt(jnp.sum(sq_r[...], axis=0) / D + EPS)
    inv_r[g] = inv_s[...]

    def send_inv(d):
        j = dp_peer(d)
        rcopy(inv_s, inv_r.at[g], s_inv.at[j], r_inv.at[g], dp_dev(j)).start()

    loop(1, G, send_inv)

    def wait_inv(d):
        j = dp_peer(d)
        rcopy(inv_r.at[j], inv_r.at[j], s_inv.at[j], r_inv.at[j], dp_dev(j)).wait_recv()

    loop(1, G, wait_inv)
    irow = jnp.concatenate([inv_r[j, 0:1, 0:GROUP] for j in range(G)], axis=1)
    my_sel = sel[lax.div(chip, CPE), pl.ds(pl.multiple_of(lax.rem(chip, CPE) * RCH, 16), RCH), :]
    icol = jnp.sum(my_sel.astype(F32) * irow, axis=1, keepdims=True)

    def wait_prs(d):
        c = chip_peer(d)
        rcopy(prs.at[c], prs.at[c], s_prs.at[c], r_prs.at[c], exp_dev(2 * c + core)).wait_recv()

    loop(1, NC, wait_prs)
    tot = prs[0].astype(F32)
    for c in range(1, NC):
        tot = tot + prs[c].astype(F32)
    tot = tot * icol
    ga = tot[:, 0:FH]
    hid[mine, :] = (ga / (1.0 + jnp.exp(-ga)) * tot[:, FH : 2 * FH]).astype(BF16)

    def send_hid(d):
        c = chip_peer(d)
        rcopy(hid.at[mine], hid.at[mine], s_hid.at[c], r_hid.at[chip], exp_dev(2 * c + core)).start()

    loop(1, NC, send_hid)
    c_wout.wait()
    rcopy(wout.at[1], wout.at[1], s_w.at[1], r_w.at[1], exp_dev(sib)).wait_recv()

    def wait_hid(d):
        c = chip_peer(d)
        at = pl.ds(pl.multiple_of(c * RCH, 16), RCH)
        rcopy(hid.at[at], hid.at[at], s_hid.at[c], r_hid.at[c], exp_dev(2 * c + core)).wait_recv()

    loop(1, NC, wait_hid)

    def down(e):
        at = pl.ds(pl.multiple_of(e * ESL, 16), ESL)
        he = hid[at, :]
        gs = gcol[e, :, 0:1]
        vsib[at, :] = (mm_nt(he, wout[1, e]) * gs).astype(BF16)
        vown[at, :] = (mm_nt(he, wout[0, e]) * gs).astype(BF16)

    loop(0, ELOC, down)
    zsib_s[...] = mm(sel_t[...], vsib[...]).astype(BF16)
    zc = rcopy(zsib_s, zsib_r, s_w.at[2], r_w.at[2], exp_dev(sib))
    zc.start()
    zown[...] = mm(sel_t[...], vown[...])
    zc.wait_recv()
    zsum = zown[...] + zsib_r[...].astype(F32)
    zown[...] = zsum
    zs[...] = zsum.astype(BF16).reshape(G, GROUP, W)

    def send_z(d):
        j = dp_peer(d)
        rcopy(zs.at[j], zr.at[g], s_z.at[j], r_z.at[g], dp_dev(j)).start()

    loop(1, G, send_z)
    zr[g] = jnp.zeros((GROUP, W), BF16)
    total = resid + zown[pl.ds(pl.multiple_of(g * GROUP, GROUP), GROUP), :]

    def wait_z(d):
        j = dp_peer(d)
        rcopy(zr.at[j], zr.at[j], s_z.at[j], r_z.at[j], dp_dev(j)).wait_recv()

    loop(1, G, wait_z)
    for j in range(G):
        total = total + zr[j].astype(F32)
    out_ref[...] = total.astype(BF16)

    w1.wait_send()
    w2.wait_send()
    zc.wait_send()

    def drain_dp(d):
        j = dp_peer(d)
        dev = dp_dev(j)
        rcopy(sml_s.at[j], sml_r.at[g], s_sml.at[j], r_sml.at[g], dev).wait_send()
        rcopy(q_all.at[g], q_all.at[g], s_q.at[j], r_q.at[g], dev).wait_send()
        rcopy(lse_s.at[j], lse_r.at[g], s_lse.at[j], r_lse.at[g], dev).wait_send()
        rcopy(hv_s.at[j], hv_r.at[g], s_hv.at[j], r_hv.at[g], dev).wait_send()
        rcopy(xall.at[g], xall.at[g], s_x.at[j], r_x.at[g], dev).wait_send()
        rcopy(inv_s, inv_r.at[g], s_inv.at[j], r_inv.at[g], dev).wait_send()
        rcopy(zs.at[j], zr.at[g], s_z.at[j], r_z.at[g], dev).wait_send()

    loop(1, G, drain_dp)

    def drain_ex(d):
        j = ex_peer(d)
        dev = exp_dev(j)
        rcopy(hva.at[k], hva.at[k], s_hva.at[j], r_hva.at[k], dev).wait_send()
        rcopy(sq_s, sq_r.at[k], s_sq.at[j], r_sq.at[k], dev).wait_send()

    loop(1, C, drain_ex)

    def drain_fw(j):
        rcopy(xall.at[j], xsib.at[j], s_fw.at[j], r_fw.at[j], exp_dev(sib)).wait_send()

    loop(0, G, drain_fw)

    def drain_ch(d):
        c = chip_peer(d)
        dev = exp_dev(2 * c + core)
        at = pl.ds(pl.multiple_of(c * RCH, 16), RCH)
        rcopy(part.at[at], prs.at[chip], s_prs.at[c], r_prs.at[chip], dev).wait_send()
        rcopy(hid.at[mine], hid.at[mine], s_hid.at[c], r_hid.at[chip], dev).wait_send()

    loop(1, NC, drain_ch)


def body(
    queries, new_latent, pool_pages, page_owner, page_slot, lengths, residual, value_weight,
    output_weight, norm_gain, expert_ids, route_gates, expert_in, expert_out,
):
    G = lax.axis_size("dp")
    C = lax.axis_size("expert")
    ROWS, H, LAT = queries.shape
    NS, _, PAGE = pool_pages.shape
    GROUP, W = residual.shape
    ELOC, _, _, FF = expert_in.shape
    FH = FF // 2
    NC = C // 2
    RH = ROWS * H
    capacity = min(GROUP, (3 * GROUP * TOP + 2 * G * ELOC - 1) // (2 * G * ELOC))
    ESL = G * capacity
    SLOTS = ELOC * ESL
    RCH = SLOTS // NC
    N2 = G * RH
    ROWN = G * GROUP

    def v(shape, dtype=BF16):
        return pltpu.VMEM(shape, dtype)

    dma = lambda n: pltpu.SemaphoreType.DMA((n,))
    scratch = [
        v((LAT, NS * PAGE)), v((NS * PAGE, KVR)), v((128, LAT)), v((G, ROWS, H, LAT)),
        v((G, 16, 128), F32), v((G, 16, 128), F32), v((N2, N2)), v((N2, N2)),
        v((N2, KVR)), v((N2, KVR)), v((N2, DV)), v((G, RH, DV)), v((G, 8, 128), F32),
        v((G, RH, DV)), v((G, 8, 128), F32),
        v((C, RH, DV)), v((GROUP, H * DV)), v((H, KVR, DV)), v((W, H * DV)),
        v((2, ELOC, W, 2, FH)), v((ELOC, 2, W, FF)), v((2, ELOC, W, FH)),
        v((G, GROUP, W)), v((G, GROUP, W)), v((8, 128), F32), v((C, 8, 128), F32),
        v((8, 128), F32), v((G, 8, 128), F32),
        v((ELOC, ESL, ROWN)), v((ROWN, SLOTS)), v((ELOC, ESL, 128), F32),
        v((SLOTS, FF)), v((NC, RCH, FF)), v((SLOTS, FH)), v((SLOTS, W)), v((SLOTS, W)),
        v((ROWN, W)), v((ROWN, W)), v((G, GROUP, W)), v((G, GROUP, W)), v((ROWN, W), F32),
        dma(NS + 5),
    ]
    for n in (G, G, G, G, G, G, G, C, C, NC, NC, G, 3):
        scratch += [dma(n), dma(n)]
    vm = pl.BlockSpec(memory_space=pltpu.VMEM)
    sm = pl.BlockSpec(memory_space=pltpu.SMEM)
    hbm = pl.BlockSpec(memory_space=pl.ANY)
    return pl.pallas_call(
        functools.partial(kernel, G, C, ELOC, capacity),
        out_shape=jax.ShapeDtypeStruct((GROUP, W), BF16),
        in_specs=[hbm, vm, hbm, sm, sm, sm, vm, hbm, hbm, vm, vm, vm, hbm, hbm],
        out_specs=vm,
        scratch_shapes=scratch,
        compiler_params=pltpu.CompilerParams(
            collective_id=0, has_side_effects=True, vmem_limit_bytes=56 << 20
        ),
        cost_estimate=pl.CostEstimate(flops=4 << 30, bytes_accessed=16 << 20, transcendentals=1 << 20),
        name="decode_step",
    )(
        queries, new_latent, pool_pages, page_owner, page_slot, lengths, residual, value_weight,
        output_weight.T, norm_gain, expert_ids.T, route_gates.T, expert_in,
        jnp.swapaxes(expert_out, 1, 2),
    )


def solution(mesh):
    in_specs = (
        P(("dp", "expert"), None, None),
        P(("dp", "expert"), None),
        P(("dp", "expert"), None, None),
        P(None, "expert", None, None),
        P(None, "expert", None, None),
        P(("dp", "expert")),
        P("dp", "expert"),
        P(),
        P(None, "expert"),
        P("expert"),
        P("dp", None),
        P("dp", None),
        P("dp", "expert", None, None),
        P("dp", None, "expert"),
    )
    return jax.shard_map(
        body, mesh=mesh, in_specs=in_specs, out_specs=P("dp", "expert"), check_vma=False
    )
```

```python
import functools
import jax
import jax.numpy as jnp
from jax import lax
from jax.experimental import pallas as pl
from jax.experimental.pallas import tpu as pltpu
from jax.sharding import PartitionSpec as P

D = 7168
KVR = 512
ROPE = 64
DV = 128
TOP = 8
EPS = 1e-06
MESH = pl.DeviceIdType.MESH
F32 = jnp.float32
BF16 = jnp.bfloat16
NEG = -1e30


def iota(shape, dim):
    return lax.broadcasted_iota(jnp.int32, shape, dim)


def mm(a, b):
    return jnp.dot(a, b, preferred_element_type=F32)


def mm_nt(a, b):
    return lax.dot_general(a, b, (((1,), (1,)), ((), ())), preferred_element_type=F32)


def kernel(
    G, C, ELOC, CAPX,
    q_hbm, nl_ref, pool_hbm, owner_ref, slot_ref, len_ref, res_ref, wv_hbm, wo_hbm, gain_ref,
    ids_ref, gates_ref, win_hbm, wout_hbm,
    out_ref,
    kc, vt, nlp, q_in, q_all, sml_s, sml_r, perm, perm_t, o_all, o_hm, hv_hm, hv_s, lse_s, hv_r,
    lse_r, hva, xmat, wv, wo, win, wg, wout, xall, xsib, sq_s, sq_r, inv_s, inv_r,
    sel, sel_t, gcol, part, in1, out1, b2, in2, hid, vown, vsib, zsib_s, zsib_r, zs, zr, zown,
    lsem, s_q, r_q, s_sml, r_sml, s_hv, r_hv, s_lse, r_lse, s_x, r_x, s_inv, r_inv, s_z, r_z,
    s_hva, r_hva, s_sq, r_sq, s_p1, r_p1, s_p2, r_p2, s_hid, r_hid, s_fw, r_fw, s_w, r_w,
):
    g = lax.axis_index("dp")
    k = lax.axis_index("expert")
    core = lax.rem(k, 2)
    chip = lax.div(k, 2)
    sib = k + 1 - 2 * core
    cx = lax.rem(chip, 4)
    cy = lax.div(chip, 4)
    ROWS, H, LAT = q_in.shape
    NS = pool_hbm.shape[0]
    PAGE = pool_hbm.shape[2]
    RH = ROWS * H
    GROUP = C * ROWS
    W = res_ref.shape[1]
    FF = win_hbm.shape[3]
    FH = FF // 2
    ESL = G * CAPX
    QR = ESL // 4
    QF = FH // 4
    NR = G * ROWS

    def dp_peer(d):
        half = lax.div(G + 1 - d, 2)
        off = half * (1 - 2 * lax.rem(G + 1 - d, 2))
        return lax.rem(g + off + G, G)

    def at_dp(off):
        return lax.rem(g + off + G, G)

    def ex_peer(d):
        return lax.rem(k + d, C)

    def at_chip(ox, oy):
        x = lax.rem(cx + ox + 4, 4)
        y = lax.rem(cy + oy + 4, 4)
        return x, y, (g, 2 * (4 * y + x) + core)

    def rcopy(src, dst, ss, rs, dev):
        return pltpu.make_async_remote_copy(
            src_ref=src, dst_ref=dst, send_sem=ss, recv_sem=rs, device_id=dev, device_id_type=MESH
        )

    def loop(lo, hi, fn):
        lax.fori_loop(lo, hi, lambda i, c: (fn(i), c)[1], 0)

    def exp_dev(kk):
        return (g, kk)

    def dp_dev(j):
        return (j, k)

    locals_ = []
    for s in range(NS):
        locals_.append(
            pltpu.make_async_copy(pool_hbm.at[s], kc.at[:, pl.ds(s * PAGE, PAGE)], lsem.at[s])
        )
    c_q = pltpu.make_async_copy(q_hbm, q_in, lsem.at[NS])
    c_win = pltpu.make_async_copy(
        win_hbm.at[:, :, :, pl.ds(pl.multiple_of(core * FH, FH), FH)], win.at[0], lsem.at[NS + 1]
    )
    c_wv = pltpu.make_async_copy(wv_hbm, wv, lsem.at[NS + 2])
    c_wo = pltpu.make_async_copy(wo_hbm, wo, lsem.at[NS + 3])
    c_wout = pltpu.make_async_copy(
        wout_hbm.at[:, :, pl.ds(pl.multiple_of(core * FH, FH), FH)], wout.at[0], lsem.at[NS + 4]
    )
    c_q.start()
    for c in locals_:
        c.start()
    for c in (c_win, c_wv, c_wo, c_wout):
        c.start()

    barrier = pltpu.get_barrier_semaphore()

    def sig_dp(d):
        pl.semaphore_signal(barrier, inc=1, device_id=dp_dev(lax.rem(g + d, G)), device_id_type=MESH)

    def sig_ex(d):
        pl.semaphore_signal(barrier, inc=1, device_id=exp_dev(ex_peer(d)), device_id_type=MESH)

    loop(1, G, sig_dp)
    loop(1, C, sig_ex)

    ids = ids_ref[...]
    gates = gates_ref[...]
    e_iota = iota((G * ELOC, GROUP), 0)
    named = jnp.zeros((G * ELOC, GROUP), F32)
    gval = jnp.zeros((G * ELOC, GROUP), F32)
    for t in range(TOP):
        hit = ids[t : t + 1, :] == e_iota
        named = named + hit.astype(F32)
        gval = gval + jnp.where(hit, gates[t : t + 1, :], 0.0)
    tri = (iota((GROUP, GROUP), 0) < iota((GROUP, GROUP), 1)).astype(BF16)
    rank = mm(named.astype(BF16), tri)
    code = jnp.where(named > 0, rank, -1.0)
    sml_s[...] = jnp.zeros_like(sml_s)
    for j in range(G):
        sml_s[j, 0:ELOC, 0:GROUP] = code[j * ELOC : (j + 1) * ELOC]
        sml_s[j, ELOC : 2 * ELOC, 0:GROUP] = gval[j * ELOC : (j + 1) * ELOC]
    sml_r[g] = sml_s[g]

    N2 = NR * H
    pr = iota((N2, 1), 0)
    perm[...] = (iota((N2, N2), 1) == lax.rem(pr, NR) * H + lax.div(pr, NR)).astype(BF16)
    perm_t[...] = (iota((N2, N2), 1) == lax.rem(pr, H) * NR + lax.div(pr, H)).astype(BF16)
    nl = nl_ref[...].astype(F32)
    nrow = iota((128, LAT), 0)
    nacc = jnp.zeros((128, LAT), F32)
    for s in range(ROWS):
        nacc = jnp.where(nrow == s, nl[s : s + 1, :], nacc)
    nlp[...] = nacc.astype(BF16)

    c_q.wait()
    for r in range(ROWS):
        n = len_ref[r]
        li = iota((H, q_all.shape[3] - LAT), 1)
        tail = jnp.where(li == 0, lax.div(n, 32), jnp.where(li == 1, lax.rem(n, 32), 0))
        q_all[g, r] = jnp.concatenate([q_in[r], tail.astype(F32).astype(BF16)], axis=1)
    pl.semaphore_wait(barrier, G - 1 + C - 1)

    def q_copy(i, src, off, row=None):
        j = at_dp(off)
        if row is None:
            return rcopy(q_all.at[src], q_all.at[src], s_q.at[i], r_q.at[src], dp_dev(j))
        return rcopy(
            q_all.at[src, row], q_all.at[src, row], s_q.at[i], r_q.at[G + row], dp_dev(j)
        )

    q_sends = [q_copy(0, g, 2), q_copy(1, g, -2), q_copy(2, g, 1), q_copy(3, g, -1)]
    for c in q_sends:
        c.start()

    other = pl.multiple_of((1 - core) * FH, FH)
    w1 = rcopy(win_hbm.at[:, :, :, pl.ds(other, FH)], win.at[1], s_w.at[0], r_w.at[0], exp_dev(sib))
    w2 = rcopy(wout_hbm.at[:, :, pl.ds(other, FH)], wout.at[1], s_w.at[1], r_w.at[1], exp_dev(sib))
    w1.start()
    w2.start()

    for c in locals_:
        c.wait()
    vt[...] = kc[0:KVR, :].T

    scale = (DV + ROPE) ** (-0.5)
    NT = NS * PAGE

    def attend(src, own):
        qx = q_all[src].reshape(RH, q_all.shape[3])
        q = qx[:, 0:LAT]
        sc = mm(q, kc[...]) * scale
        lid = iota((1, NT), 1)
        slot_lane = lax.div(lid, PAGE)
        tpos = lax.rem(lid, PAGE).astype(F32)
        rows = []
        for s in range(ROWS):
            lv = qx[s * H : s * H + 8, LAT : LAT + 2].astype(F32)
            ln = lv[0:1, 0:1] * 32.0 + lv[0:1, 1:2]
            cnt = jnp.zeros((1, NT), F32)
            for p in range(owner_ref.shape[3]):
                here = jnp.where(owner_ref[src, 0, s, p] == g, slot_ref[src, 0, s, p], -1)
                ok = jnp.logical_and(slot_lane == here, tpos + float(p * PAGE) < ln)
                cnt = cnt + ok.astype(F32)
            rows.append(jnp.broadcast_to(cnt, (H, NT)))
        cnt = jnp.concatenate(rows, axis=0)
        scm = jnp.where(cnt > 0, sc, NEG)
        top = jnp.max(scm, axis=1, keepdims=True)
        if own:
            cs = (iota((RH, 128), 1) == lax.div(iota((RH, 128), 0), H)).astype(F32)
            ss = jnp.where(cs > 0, mm_nt(q, nlp[...]) * scale, NEG)
            top = jnp.maximum(top, jnp.max(ss, axis=1, keepdims=True))
        p = cnt * jnp.exp(scm - top)
        den = jnp.sum(p, axis=1, keepdims=True)
        acc = mm(p.astype(BF16), vt[...])
        if own:
            pself = cs * jnp.exp(ss - top)
            den = den + jnp.sum(pself, axis=1, keepdims=True)
            acc = acc + mm(pself.astype(BF16), nlp[:, 0:KVR])
        has = den > 0
        inv_den = jnp.where(has, 1.0 / jnp.where(has, den, 1.0), 0.0)
        lse = jnp.where(has, top + jnp.log(jnp.where(has, den, 1.0)), NEG)
        o_all[pl.ds(pl.multiple_of(src * RH, RH), RH), :] = (acc * inv_den).astype(BF16)
        row = jnp.broadcast_to(lse, (RH, 128)).T[0:1]
        lse_s[src] = jnp.concatenate([row, row], axis=1)

    attend(g, True)

    for i, off in ((0, -2), (1, 2)):
        src = at_dp(off)
        q_copy(i, src, off).wait_recv()
        for c in (q_copy(4 + i, src, 1 - 2 * i), q_copy(6 + i, src, 2 - 4 * i, row=i)):
            c.start()
            q_sends.append(c)

    def send_sml(d):
        j = dp_peer(d)
        rcopy(sml_s.at[j], sml_r.at[g], s_sml.at[j], r_sml.at[g], dp_dev(j)).start()

    loop(1, G, send_sml)

    def ring(d):
        n = lax.div(d, 2)
        m = jnp.where(n == 0, 2, jnp.where(n == 1, 1, n + 1))
        return at_dp(jnp.where(lax.rem(d, 2) == 0, -m, m))

    def near(d):
        attend(ring(d), False)

    def chunk(d):
        src = ring(d)
        rcopy(q_all.at[src], q_all.at[src], s_q.at[0], r_q.at[src], dp_dev(src)).wait_recv()
        attend(src, False)

    loop(0, 2, near)
    loop(2, G - 2, chunk)
    far = at_dp(G // 2)
    for r in range(ROWS):
        rcopy(q_all.at[far, r], q_all.at[far, r], s_q.at[0], r_q.at[G + r], dp_dev(far)).wait_recv()
    attend(far, False)

    o_hm[...] = mm(perm[...], o_all[...]).astype(BF16)
    c_wv.wait()
    HB = 8

    def project(b):
        for i in range(HB):
            h = b * HB + i
            at = pl.ds(pl.multiple_of(h * NR, NR), NR)
            hv_hm[at, :] = mm(o_hm[at, :], wv[h]).astype(BF16)

    loop(0, H // HB, project)
    hv_s[...] = mm(perm_t[...], hv_hm[...]).astype(BF16).reshape(G, RH, DV)
    hv_r[g] = hv_s[g]
    lse_r[g] = lse_s[g]

    def send_hv(d):
        j = dp_peer(d)
        rcopy(lse_s.at[j], lse_r.at[g], s_lse.at[j], r_lse.at[g], dp_dev(j)).start()
        rcopy(hv_s.at[j], hv_r.at[g], s_hv.at[j], r_hv.at[g], dp_dev(j)).start()

    loop(1, G, send_hv)

    def wait_sml(d):
        j = dp_peer(d)
        rcopy(sml_r.at[j], sml_r.at[j], s_sml.at[j], r_sml.at[j], dp_dev(j)).wait_recv()

    loop(1, G, wait_sml)
    siota = iota((ESL, G * GROUP), 0).astype(F32)
    for e in range(ELOC):
        codes = []
        gvals = []
        for j in range(G):
            cj = sml_r[j, e : e + 1, 0:GROUP]
            codes.append(jnp.where(cj >= 0, cj + float(j * CAPX), -1.0))
            gvals.append(sml_r[j, ELOC + e : ELOC + e + 1, 0:GROUP])
        crow = jnp.concatenate(codes, axis=1)
        grow = jnp.concatenate(gvals, axis=1)
        hit = siota == crow
        sel[e] = hit.astype(F32).astype(BF16)
        gs = jnp.sum(jnp.where(hit, grow, 0.0), axis=1, keepdims=True)
        gcol[e] = jnp.broadcast_to(gs, (ESL, 128))
    sel_t[...] = sel[...].reshape(ELOC * ESL, G * GROUP).T

    def wait_hv(d):
        j = dp_peer(d)
        rcopy(lse_r.at[j], lse_r.at[j], s_lse.at[j], r_lse.at[j], dp_dev(j)).wait_recv()
        rcopy(hv_r.at[j], hv_r.at[j], s_hv.at[j], r_hv.at[j], dp_dev(j)).wait_recv()

    loop(1, G, wait_hv)
    riota = iota((8, 128), 0)
    ls = jnp.full((8, 128), NEG, F32)
    for j in range(G):
        ls = jnp.where(riota == j, lse_r[j], ls)
    wts = jnp.exp(ls - jnp.max(ls, axis=0, keepdims=True))
    wts = wts / jnp.sum(wts, axis=0, keepdims=True)
    wcol = wts.T
    comb = jnp.zeros((RH, DV), F32)
    for j in range(G):
        comb = comb + wcol[0:RH, j : j + 1] * hv_r[j].astype(F32)
    hva[k] = comb.astype(BF16)

    def send_hva(d):
        j = ex_peer(d)
        rcopy(hva.at[k], hva.at[k], s_hva.at[j], r_hva.at[k], exp_dev(j)).start()

    loop(1, C, send_hva)

    c_win.wait()
    rcopy(win.at[1], win.at[1], s_w.at[0], r_w.at[0], exp_dev(sib)).wait_recv()
    col = iota((W, 2 * W), 1)
    two = 2 * iota((W, 2 * W), 0)
    pick_g = (col == two).astype(BF16)
    pick_u = (col == two + 1).astype(BF16)

    def split(i):
        e = lax.div(i, 2)
        o = lax.rem(i, 2)
        w = win[o, e].reshape(2 * W, FH)
        wgate = mm(pick_g, w).astype(BF16)
        wup = mm(pick_u, w).astype(BF16)
        for f in range(4):
            wg[e, o, :, 2 * f * QF : (2 * f + 1) * QF] = wgate[:, f * QF : (f + 1) * QF]
            wg[e, o, :, (2 * f + 1) * QF : 2 * (f + 1) * QF] = wup[:, f * QF : (f + 1) * QF]

    loop(0, 2 * ELOC, split)

    c_wo.wait()

    def wait_hva(d):
        j = ex_peer(d)
        rcopy(hva.at[j], hva.at[j], s_hva.at[j], r_hva.at[j], exp_dev(j)).wait_recv()

    loop(1, C, wait_hva)

    for b in range(C // G):
        blk = mm(perm[...], hva[b * G : (b + 1) * G].reshape(N2, DV)).astype(BF16)
        for h in range(H):
            xmat[b * NR : (b + 1) * NR, h * DV : (h + 1) * DV] = blk[h * NR : (h + 1) * NR]
    proj = mm_nt(xmat[...], wo[...])
    resid = (res_ref[...].astype(F32) + proj).astype(BF16).astype(F32)
    xall[g] = (resid * gain_ref[...].reshape(1, W)).astype(BF16)

    def send_x(d):
        j = dp_peer(d)
        rcopy(xall.at[g], xall.at[g], s_x.at[j], r_x.at[g], dp_dev(j)).start()

    def fwd(j):
        rcopy(xall.at[j], xsib.at[j], s_fw.at[j], r_fw.at[j], exp_dev(sib)).start()

    loop(1, G, send_x)
    fwd(g)
    sq = jnp.sum(resid * resid, axis=1, keepdims=True)
    sq_row = jnp.broadcast_to(sq, (GROUP, 128)).T[0:1]
    sq_s[...] = jnp.concatenate([sq_row] * (128 // GROUP), axis=1)
    sq_r[k] = sq_s[...]

    def send_sq(d):
        j = ex_peer(d)
        rcopy(sq_s, sq_r.at[k], s_sq.at[j], r_sq.at[k], exp_dev(j)).start()

    loop(1, C, send_sq)

    def pass_x(d):
        j = dp_peer(d)
        rcopy(xall.at[j], xall.at[j], s_x.at[j], r_x.at[j], dp_dev(j)).wait_recv()
        fwd(j)

    loop(1, G, pass_x)

    def wait_fw(j):
        rcopy(xsib.at[j], xsib.at[j], s_fw.at[j], r_fw.at[j], exp_dev(sib)).wait_recv()

    loop(0, G, wait_fw)

    def wait_sq(d):
        j = ex_peer(d)
        rcopy(sq_r.at[j], sq_r.at[j], s_sq.at[j], r_sq.at[j], exp_dev(j)).wait_recv()

    loop(1, C, wait_sq)
    inv_s[...] = lax.rsqrt(jnp.sum(sq_r[...], axis=0) / D + EPS)
    inv_r[g] = inv_s[...]

    def send_inv(d):
        j = dp_peer(d)
        rcopy(inv_s, inv_r.at[g], s_inv.at[j], r_inv.at[g], dp_dev(j)).start()

    loop(1, G, send_inv)

    place = (cx, cy)

    def along(h, off):
        return at_chip(off, 0)[2] if h == 0 else at_chip(0, off)[2]

    def across(h, off):
        return at_chip(0, off)[2] if h == 0 else at_chip(off, 0)[2]

    def ring1(h, slot, src):
        n = 6 * h + slot
        return rcopy(src, in1.at[h, slot], s_p1.at[n], r_p1.at[n], along(h, 1 if slot < 3 else -1))

    def block(e):
        return pl.ds(pl.multiple_of(e * ESL, 16), ESL)

    def part_step(i):
        e = lax.rem(cx + 2 + 3 * i, 4)
        xo = mm(sel[e], xall[...].reshape(G * GROUP, W)).astype(BF16)
        xs = mm(sel[e], xsib[...].reshape(G * GROUP, W)).astype(BF16)
        for f in range(4):
            cols = slice(2 * f * QF, 2 * (f + 1) * QF)
            part[f, block(e)] = (mm(xo, wg[e, 0, :, cols]) + mm(xs, wg[e, 1, :, cols])).astype(BF16)
        for h in range(2):
            role = lax.rem(e - place[h] + 4, 4)

            @pl.when(role == 2)
            def _():
                ring1(h, 0, part.at[2 * h, block(e)]).start()
                ring1(h, 3, part.at[2 * h + 1, block(e)]).start()

            @pl.when(role == 1)
            def _():
                ring1(h, 1, part.at[2 * h + 1, block(e)]).start()

            @pl.when(role == 3)
            def _():
                ring1(h, 4, part.at[2 * h, block(e)]).start()

    loop(0, 4, part_step)

    for h in range(2):
        for i in range(2):
            to = lax.rem(place[h] + (1, 3)[i], 4)
            ring1(h, 3 * i, in1.at[h, 3 * i]).wait_recv()
            mixed = part[2 * h + i, block(to)].astype(F32) + in1[h, 3 * i].astype(F32)
            out1[h, i] = mixed.astype(BF16)
            ring1(h, 2 + 3 * i, out1.at[h, i]).start()

    def rows2(p):
        return pl.ds(pl.multiple_of(p * QR, 16), QR)

    def ring2(h, off):
        to = lax.rem(place[1 - h] + off, 4)
        n = 3 * h + off - 1
        return rcopy(
            b2.at[h, :, rows2(to)], in2.at[h, 4 - off], s_p2.at[n], r_p2.at[n], across(h, off)
        )

    for h in range(2):
        for i in range(2):
            ring1(h, 4 - 3 * i, in1.at[h, 4 - 3 * i]).wait_recv()
            ring1(h, 2 + 3 * i, in1.at[h, 2 + 3 * i]).wait_recv()
            own = part[2 * h + i, block(place[h])].astype(F32)
            got = in1[h, 4 - 3 * i].astype(F32) + in1[h, 2 + 3 * i].astype(F32)
            b2[h, i] = (own + got).astype(BF16)
        for off in (2, 1, 3):
            ring2(h, off).start()
        in2[h, 0] = b2[h, :, rows2(place[1 - h])]

    def wait_inv(d):
        j = dp_peer(d)
        rcopy(inv_r.at[j], inv_r.at[j], s_inv.at[j], r_inv.at[j], dp_dev(j)).wait_recv()

    loop(1, G, wait_inv)
    irow = jnp.concatenate([inv_r[j, 0:1, 0:GROUP] for j in range(G)], axis=1)

    def hid_rows(h, x, y):
        p = (x, y)
        return pl.ds(pl.multiple_of(p[h] * ESL + p[1 - h] * QR, 16), QR)

    for h in range(2):
        mine = sel[place[h], rows2(place[1 - h]), :]
        icol = jnp.sum(mine.astype(F32) * irow, axis=1, keepdims=True)
        for off in (1, 3, 2):
            ring2(h, off).wait_recv()
        for i in range(2):
            tot = in2[h, 0, i].astype(F32)
            for j in range(1, 4):
                tot = tot + in2[h, j, i].astype(F32)
            tot = tot * icol
            ga = tot[:, 0:QF]
            hv = ga / (1.0 + jnp.exp(-ga)) * tot[:, QF : 2 * QF]
            hid[2 * h + i, hid_rows(h, cx, cy)] = hv.astype(BF16)

    def hid_send(n, h, src_x, src_y, dev):
        ref = hid.at[pl.ds(2 * h, 2), hid_rows(h, src_x, src_y)]
        return rcopy(ref, ref, s_hid.at[n], r_hid.at[2 * (4 * src_y + src_x) + h], dev)

    def hid_quarter(n, f, src_x, src_y, dev):
        ref = hid.at[f, hid_rows(f // 2, src_x, src_y)]
        return rcopy(ref, ref, s_hid.at[n], r_hid.at[32 + f], dev)

    around = [(1, 1), (1, -1), (-1, 1), (-1, -1), (1, 0), (-1, 0), (0, 1), (0, -1)]
    hid_sends = []

    def begin(c):
        c.start()
        hid_sends.append(c)

    for ox, oy in around:
        for h in range(2):
            begin(hid_send(len(hid_sends), h, cx, cy, at_chip(ox, oy)[2]))
    for ox, oy in around:
        sx, sy, dev = at_chip(ox, oy)
        for h in range(2):
            hid_send(0, h, sx, sy, dev).wait_recv()
        if ox != 0 and oy != 0:
            f = (ox > 0) + 2 * (oy > 0)
            begin(hid_quarter(len(hid_sends), f, sx, sy, at_chip(-ox, -oy)[2]))
        if ox != 0:
            begin(hid_send(len(hid_sends), int(ox > 0), sx, sy, at_chip(-ox, 0)[2]))
        if oy != 0:
            begin(hid_send(len(hid_sends), int(oy > 0), sx, sy, at_chip(0, -oy)[2]))
    c_wout.wait()
    rcopy(wout.at[1], wout.at[1], s_w.at[1], r_w.at[1], exp_dev(sib)).wait_recv()
    for ox, oy in ((2, 0), (2, 1), (2, -1), (0, 2), (1, 2), (-1, 2)):
        sx, sy, dev = at_chip(ox, oy)
        for h in range(2):
            hid_send(0, h, sx, sy, dev).wait_recv()
    sx, sy, dev = at_chip(2, 2)
    for f in range(4):
        hid_quarter(0, f, sx, sy, dev).wait_recv()

    def down(e):
        at = pl.ds(pl.multiple_of(e * ESL, 16), ESL)
        he = jnp.concatenate([hid[f, at] for f in range(4)], axis=1)
        gs = gcol[e, :, 0:1]
        vsib[at, :] = (mm_nt(he, wout[1, e]) * gs).astype(BF16)
        vown[at, :] = (mm_nt(he, wout[0, e]) * gs).astype(BF16)

    loop(0, ELOC, down)
    zsib_s[...] = mm(sel_t[...], vsib[...]).astype(BF16)
    zc = rcopy(zsib_s, zsib_r, s_w.at[2], r_w.at[2], exp_dev(sib))
    zc.start()
    zown[...] = mm(sel_t[...], vown[...])
    zc.wait_recv()
    zsum = zown[...] + zsib_r[...].astype(F32)
    zown[...] = zsum
    zs[...] = zsum.astype(BF16).reshape(G, GROUP, W)

    def send_z(d):
        j = dp_peer(d)
        rcopy(zs.at[j], zr.at[g], s_z.at[j], r_z.at[g], dp_dev(j)).start()

    loop(1, G, send_z)
    zr[g] = jnp.zeros((GROUP, W), BF16)
    total = resid + zown[pl.ds(pl.multiple_of(g * GROUP, GROUP), GROUP), :]

    def wait_z(d):
        j = dp_peer(d)
        rcopy(zr.at[j], zr.at[j], s_z.at[j], r_z.at[j], dp_dev(j)).wait_recv()

    loop(1, G, wait_z)
    for j in range(G):
        total = total + zr[j].astype(F32)
    out_ref[...] = total.astype(BF16)

    w1.wait_send()
    w2.wait_send()
    zc.wait_send()

    def drain_dp(d):
        j = dp_peer(d)
        dev = dp_dev(j)
        rcopy(sml_s.at[j], sml_r.at[g], s_sml.at[j], r_sml.at[g], dev).wait_send()
        rcopy(lse_s.at[j], lse_r.at[g], s_lse.at[j], r_lse.at[g], dev).wait_send()
        rcopy(hv_s.at[j], hv_r.at[g], s_hv.at[j], r_hv.at[g], dev).wait_send()
        rcopy(xall.at[g], xall.at[g], s_x.at[j], r_x.at[g], dev).wait_send()
        rcopy(inv_s, inv_r.at[g], s_inv.at[j], r_inv.at[g], dev).wait_send()
        rcopy(zs.at[j], zr.at[g], s_z.at[j], r_z.at[g], dev).wait_send()

    loop(1, G, drain_dp)

    def drain_ex(d):
        j = ex_peer(d)
        dev = exp_dev(j)
        rcopy(hva.at[k], hva.at[k], s_hva.at[j], r_hva.at[k], dev).wait_send()
        rcopy(sq_s, sq_r.at[k], s_sq.at[j], r_sq.at[k], dev).wait_send()

    loop(1, C, drain_ex)

    def drain_fw(j):
        rcopy(xall.at[j], xsib.at[j], s_fw.at[j], r_fw.at[j], exp_dev(sib)).wait_send()

    loop(0, G, drain_fw)

    for c in q_sends + hid_sends:
        c.wait_send()
    for h in range(2):
        for slot in range(6):
            ring1(h, slot, in1.at[h, slot]).wait_send()
        for off in (1, 2, 3):
            ring2(h, off).wait_send()


def body(
    queries, new_latent, pool_pages, page_owner, page_slot, lengths, residual, value_weight,
    output_weight, norm_gain, expert_ids, route_gates, expert_in, expert_out,
):
    G = lax.axis_size("dp")
    C = lax.axis_size("expert")
    ROWS, H, LAT = queries.shape
    NS, _, PAGE = pool_pages.shape
    GROUP, W = residual.shape
    ELOC, _, _, FF = expert_in.shape
    FH = FF // 2
    RH = ROWS * H
    capacity = min(GROUP, (3 * GROUP * TOP + 2 * G * ELOC - 1) // (2 * G * ELOC))
    ESL = G * capacity
    SLOTS = ELOC * ESL
    BLK, QR, QC = SLOTS // 4, SLOTS // 16, FF // 4
    N2 = G * RH
    ROWN = G * GROUP

    def v(shape, dtype=BF16):
        return pltpu.VMEM(shape, dtype)

    dma = lambda n: pltpu.SemaphoreType.DMA((n,))
    scratch = [
        v((LAT, NS * PAGE)), v((NS * PAGE, KVR)), v((128, LAT)), v((ROWS, H, LAT)),
        v((G, ROWS, H, -(-(LAT + 2) // 128) * 128)),
        v((G, 8, 128), F32), v((G, 8, 128), F32), v((N2, N2)), v((N2, N2)),
        v((N2, KVR)), v((N2, KVR)), v((N2, DV)), v((G, RH, DV)), v((G, 1, 128), F32),
        v((G, RH, DV)), v((G, 1, 128), F32),
        v((C, RH, DV)), v((GROUP, H * DV)), v((H, KVR, DV)), v((W, H * DV)),
        v((2, ELOC, W, 2, FH)), v((ELOC, 2, W, FF)), v((2, ELOC, W, FH)),
        v((G, GROUP, W)), v((G, GROUP, W)), v((1, 128), F32), v((C, 1, 128), F32),
        v((1, 128), F32), v((G, 1, 128), F32),
        v((ELOC, ESL, ROWN)), v((ROWN, SLOTS)), v((ELOC, ESL, 128), F32),
        v((4, SLOTS, QC)), v((2, 6, BLK, QC)), v((2, 2, BLK, QC)), v((2, 2, BLK, QC)),
        v((2, 4, 2, QR, QC)), v((4, SLOTS, QC // 2)), v((SLOTS, W)), v((SLOTS, W)),
        v((ROWN, W)), v((ROWN, W)), v((G, GROUP, W)), v((G, GROUP, W)), v((ROWN, W), F32),
        dma(NS + 5),
    ]
    for n in (G + 2, G, G, G, G, G, G, C, C, 12, 6, C + 4, G, 3):
        scratch += [dma(n), dma(n)]
    vm = pl.BlockSpec(memory_space=pltpu.VMEM)
    sm = pl.BlockSpec(memory_space=pltpu.SMEM)
    hbm = pl.BlockSpec(memory_space=pl.ANY)
    return pl.pallas_call(
        functools.partial(kernel, G, C, ELOC, capacity),
        out_shape=jax.ShapeDtypeStruct((GROUP, W), BF16),
        in_specs=[hbm, vm, hbm, sm, sm, sm, vm, hbm, hbm, vm, vm, vm, hbm, hbm],
        out_specs=vm,
        scratch_shapes=scratch,
        compiler_params=pltpu.CompilerParams(
            collective_id=0, has_side_effects=True, vmem_limit_bytes=56 << 20
        ),
        cost_estimate=pl.CostEstimate(flops=4 << 30, bytes_accessed=16 << 20, transcendentals=1 << 20),
        name="decode_step",
    )(
        queries, new_latent, pool_pages, page_owner, page_slot, lengths, residual, value_weight,
        output_weight.T, norm_gain, expert_ids.T, route_gates.T, expert_in,
        jnp.swapaxes(expert_out, 1, 2),
    )


def solution(mesh):
    in_specs = (
        P(("dp", "expert"), None, None),
        P(("dp", "expert"), None),
        P(("dp", "expert"), None, None),
        P(None, "expert", None, None),
        P(None, "expert", None, None),
        P(("dp", "expert")),
        P("dp", "expert"),
        P(),
        P(None, "expert"),
        P("expert"),
        P("dp", None),
        P("dp", None),
        P("dp", "expert", None, None),
        P("dp", None, "expert"),
    )
    return jax.shard_map(
        body, mesh=mesh, in_specs=in_specs, out_specs=P("dp", "expert"), check_vma=False
    )
```

```python
import functools
import jax
import jax.numpy as jnp
from jax import lax
from jax.experimental import pallas as pl
from jax.experimental.pallas import tpu as pltpu
from jax.sharding import PartitionSpec as P

D = 7168
KVR = 512
ROPE = 64
DV = 128
TOP = 8
EPS = 1e-06
MESH = pl.DeviceIdType.MESH
F32 = jnp.float32
BF16 = jnp.bfloat16
NEG = -1e30
WAVES = ((0, 1, -1, 2), (-2, 3, -3, 4))
POS = {off: 4 * w + t for w in range(2) for t, off in enumerate(WAVES[w])}
BACK = {off: POS[4 if off == 4 else -off] for off in POS}


def iota(shape, dim):
    return lax.broadcasted_iota(jnp.int32, shape, dim)


def mm(a, b):
    return jnp.dot(a, b, preferred_element_type=F32)


def mm_nt(a, b):
    return lax.dot_general(a, b, (((1,), (1,)), ((), ())), preferred_element_type=F32)


def kernel(
    G, C, ELOC, CAPX,
    q_hbm, nl_hbm, pool_hbm, owner_hbm, slot_hbm, len_hbm, res_hbm, wv_hbm, wo_hbm, gain_hbm,
    ids_hbm, gates_hbm, win_hbm, wout_hbm,
    out_ref,
    nl_ref, owner_ref, slot_ref, len_ref, res_ref, gain_ref, ids_ref, gates_ref,
    kc, vt, nlp, q_in, q_all, sml_s, sml_r, perm, perm_t, o_all, o_hm, hv_hm, hv_s, lse_s, hv_r,
    lse_r, hva, xmat, wv, wo, win, wg, wout, xall, xsib, sq_s, sq_r, inv_s, inv_r,
    sel, sel_t, gcol, part, in1, out1, b2, in2, hid, vown, vsib, zsib_s, zsib_r, zs, zr, zown,
    lsem, sent, heard, r_q, r_x, r_hva, r_p1, r_p2, r_hid,
):
    g = lax.axis_index("dp")
    k = lax.axis_index("expert")
    core = lax.rem(k, 2)
    chip = lax.div(k, 2)
    sib = k + 1 - 2 * core
    cx = lax.rem(chip, 4)
    cy = lax.div(chip, 4)
    ROWS, H, LAT = q_in.shape
    NS = pool_hbm.shape[0]
    PAGE = pool_hbm.shape[2]
    RH = ROWS * H
    GROUP = C * ROWS
    W = res_ref.shape[1]
    FF = win_hbm.shape[3]
    FH = FF // 2
    ESL = 4 * CAPX
    QR = ESL // 2
    QF = FH // 4
    NR = G * ROWS

    def dp_peer(d):
        half = lax.div(G + 1 - d, 2)
        off = half * (1 - 2 * lax.rem(G + 1 - d, 2))
        return lax.rem(g + off + G, G)

    def at_dp(off):
        return lax.rem(g + off + G, G)

    def ex_peer(d):
        return lax.rem(k + d, C)

    def at_chip(ox, oy):
        x = lax.rem(cx + ox + 4, 4)
        y = lax.rem(cy + oy + 4, 4)
        return x, y, (g, 2 * (4 * y + x) + core)

    s_q, s_sml, s_hv, s_lse, s_hva, s_x, s_fw, s_sq = (sent.at[i] for i in range(8))
    s_inv, s_p1, s_p2, s_hid, s_win, s_wout, s_zsib, s_z = (sent.at[8 + i] for i in range(8))
    r_sml, r_hv, r_lse, r_inv, r_z, r_sq, r_win, r_wout = (heard.at[i] for i in range(8))
    r_fwd, r_sib, r_zsib = (heard.at[8], heard.at[9]), heard.at[10], (heard.at[11], heard.at[12])

    def rcopy(src, dst, ss, rs, dev):
        return pltpu.make_async_remote_copy(
            src_ref=src, dst_ref=dst, send_sem=ss, recv_sem=rs, device_id=dev, device_id_type=MESH
        )

    def sent_all(ref, sem):
        rcopy(ref, ref, sem, sem, exp_dev(sib)).wait_send()

    def heard_all(ref, sem):
        rcopy(ref, ref, sem, sem, exp_dev(sib)).wait_recv()

    def loop(lo, hi, fn):
        lax.fori_loop(lo, hi, lambda i, c: (fn(i), c)[1], 0)

    def exp_dev(kk):
        return (g, kk)

    def dp_dev(j):
        return (j, k)

    locals_ = []
    for s in range(NS):
        locals_.append(
            pltpu.make_async_copy(pool_hbm.at[s], kc.at[:, pl.ds(s * PAGE, PAGE)], lsem.at[0])
        )
    c_q = pltpu.make_async_copy(q_hbm, q_in, lsem.at[1])
    c_win = pltpu.make_async_copy(
        win_hbm.at[:, :, :, pl.ds(pl.multiple_of(core * FH, FH), FH)], win.at[0], lsem.at[2]
    )
    c_wv = pltpu.make_async_copy(wv_hbm, wv, lsem.at[3])
    c_wo = pltpu.make_async_copy(wo_hbm, wo, lsem.at[4])
    c_wout = pltpu.make_async_copy(
        wout_hbm.at[:, :, pl.ds(pl.multiple_of(core * FH, FH), FH)], wout.at[0], lsem.at[5]
    )
    c_q.start()
    small = []
    for i, (a, b) in enumerate(
        (
            (ids_hbm, ids_ref), (gates_hbm, gates_ref), (len_hbm, len_ref), (nl_hbm, nl_ref),
            (owner_hbm, owner_ref), (slot_hbm, slot_ref), (res_hbm, res_ref), (gain_hbm, gain_ref),
        )
    ):
        small.append(pltpu.make_async_copy(a, b, lsem.at[6 + i]))
        small[-1].start()
    for c in locals_:
        c.start()
    for c in (c_win, c_wv, c_wo, c_wout):
        c.start()

    barrier = pltpu.get_barrier_semaphore()

    def sig_dp(d):
        pl.semaphore_signal(barrier, inc=1, device_id=dp_dev(lax.rem(g + d, G)), device_id_type=MESH)

    def sig_ex(d):
        pl.semaphore_signal(barrier, inc=1, device_id=exp_dev(ex_peer(d)), device_id_type=MESH)

    loop(1, G, sig_dp)
    loop(1, C, sig_ex)

    for c in small:
        c.wait()
    ids = ids_ref[...]
    gates = gates_ref[...]
    e_iota = iota((G * ELOC, GROUP), 0)
    named = jnp.zeros((G * ELOC, GROUP), F32)
    gval = jnp.zeros((G * ELOC, GROUP), F32)
    for t in range(TOP):
        hit = ids[t : t + 1, :] == e_iota
        named = named + hit.astype(F32)
        gval = gval + jnp.where(hit, gates[t : t + 1, :], 0.0)
    tri = (iota((GROUP, GROUP), 0) < iota((GROUP, GROUP), 1)).astype(BF16)
    rank = mm(named.astype(BF16), tri)
    code = jnp.where(named > 0, rank, -1.0)
    sml_s[...] = jnp.zeros_like(sml_s)
    for j in range(G):
        sml_s[j, 0:ELOC, 0:GROUP] = code[j * ELOC : (j + 1) * ELOC]
        sml_s[j, ELOC : 2 * ELOC, 0:GROUP] = gval[j * ELOC : (j + 1) * ELOC]
    sml_r[0] = sml_s[g]

    N2 = NR * H
    pr = iota((N2, 1), 0)
    perm[...] = (iota((N2, N2), 1) == lax.rem(pr, NR) * H + lax.div(pr, NR)).astype(BF16)
    perm_t[...] = (iota((N2, N2), 1) == lax.rem(pr, H) * NR + lax.div(pr, H)).astype(BF16)
    nl = nl_ref[...].astype(F32)
    nrow = iota((128, LAT), 0)
    nacc = jnp.zeros((128, LAT), F32)
    for s in range(ROWS):
        nacc = jnp.where(nrow == s, nl[s : s + 1, :], nacc)
    nlp[...] = nacc.astype(BF16)

    c_q.wait()
    for r in range(ROWS):
        n = len_ref[r]
        li = iota((H, q_all.shape[3] - LAT), 1)
        tail = jnp.where(li == 0, lax.div(n, 32), jnp.where(li == 1, lax.rem(n, 32), 0))
        q_all[g, r] = jnp.concatenate([q_in[r], tail.astype(F32).astype(BF16)], axis=1)
    pl.semaphore_wait(barrier, G - 1 + C - 1)

    def q_copy(src, off, row=None):
        ref = q_all.at[src] if row is None else q_all.at[src, row]
        return rcopy(ref, ref, s_q, r_q.at[src], dp_dev(at_dp(off)))

    for off in (2, -2, 1, -1):
        q_copy(g, off).start()

    other = pl.multiple_of((1 - core) * FH, FH)
    w1 = rcopy(win_hbm.at[:, :, :, pl.ds(other, FH)], win.at[1], s_win, r_win, exp_dev(sib))
    w2 = rcopy(wout_hbm.at[:, :, pl.ds(other, FH)], wout.at[1], s_wout, r_wout, exp_dev(sib))
    w1.start()
    w2.start()

    pltpu.make_async_copy(kc, kc, lsem.at[0]).wait()
    vt[...] = kc[0:KVR, :].T

    scale = (DV + ROPE) ** (-0.5)
    NT = NS * PAGE

    def attend(src, own):
        qx = q_all[src].reshape(RH, q_all.shape[3])
        q = qx[:, 0:LAT]
        sc = mm(q, kc[...]) * scale
        lid = iota((1, NT), 1)
        slot_lane = lax.div(lid, PAGE)
        tpos = lax.rem(lid, PAGE).astype(F32)
        rows = []
        for s in range(ROWS):
            lv = qx[s * H : s * H + 8, LAT : LAT + 2].astype(F32)
            ln = lv[0:1, 0:1] * 32.0 + lv[0:1, 1:2]
            cnt = jnp.zeros((1, NT), F32)
            for p in range(owner_ref.shape[3]):
                here = jnp.where(owner_ref[src, 0, s, p] == g, slot_ref[src, 0, s, p], -1)
                ok = jnp.logical_and(slot_lane == here, tpos + float(p * PAGE) < ln)
                cnt = cnt + ok.astype(F32)
            rows.append(jnp.broadcast_to(cnt, (H, NT)))
        cnt = jnp.concatenate(rows, axis=0)
        scm = jnp.where(cnt > 0, sc, NEG)
        top = jnp.max(scm, axis=1, keepdims=True)
        if own:
            cs = (iota((RH, 128), 1) == lax.div(iota((RH, 128), 0), H)).astype(F32)
            ss = jnp.where(cs > 0, mm_nt(q, nlp[...]) * scale, NEG)
            top = jnp.maximum(top, jnp.max(ss, axis=1, keepdims=True))
        p = cnt * jnp.exp(scm - top)
        den = jnp.sum(p, axis=1, keepdims=True)
        acc = mm(p.astype(BF16), vt[...])
        if own:
            pself = cs * jnp.exp(ss - top)
            den = den + jnp.sum(pself, axis=1, keepdims=True)
            acc = acc + mm(pself.astype(BF16), nlp[:, 0:KVR])
        has = den > 0
        inv_den = jnp.where(has, 1.0 / jnp.where(has, den, 1.0), 0.0)
        lse = jnp.where(has, top + jnp.log(jnp.where(has, den, 1.0)), NEG)
        o_all[pl.ds(pl.multiple_of(src * RH, RH), RH), :] = (acc * inv_den).astype(BF16)
        row = jnp.broadcast_to(lse, (RH, 128)).T[0:1]
        lse_s[src] = jnp.concatenate([row, row], axis=1)

    attend(g, True)

    col = iota((W, 2 * W), 1)
    two = 2 * iota((W, 2 * W), 0)
    pick_g = (col == two).astype(BF16)
    pick_u = (col == two + 1).astype(BF16)

    def split(o, e):
        w = win[o, e].reshape(2 * W, FH)
        wgate = mm(pick_g, w).astype(BF16)
        wup = mm(pick_u, w).astype(BF16)
        for f in range(4):
            wg[e, o, :, 2 * f * QF : (2 * f + 1) * QF] = wgate[:, f * QF : (f + 1) * QF]
            wg[e, o, :, (2 * f + 1) * QF : 2 * (f + 1) * QF] = wup[:, f * QF : (f + 1) * QF]

    c_win.wait()
    loop(0, ELOC, lambda e: split(0, e))

    for i, off in ((0, -2), (1, 2)):
        src = at_dp(off)
        q_copy(src, off).wait_recv()
        q_copy(src, 1 - 2 * i).start()
        q_copy(src, 2 - 4 * i, row=i).start()

    def sml_copy(off, n):
        j = at_dp(off)
        return rcopy(sml_s.at[j], sml_r.at[n], s_sml, r_sml, dp_dev(j))

    others = [4, -3, 3, -2, 2, -1, 1]
    for off in others:
        sml_copy(off, BACK[off]).start()

    def ring(d):
        n = lax.div(d, 2)
        m = jnp.where(n == 0, 2, jnp.where(n == 1, 1, n + 1))
        return at_dp(jnp.where(lax.rem(d, 2) == 0, -m, m))

    def near(d):
        attend(ring(d), False)

    def chunk(d):
        src = ring(d)
        heard_all(q_all.at[src], r_q.at[src])
        attend(src, False)

    loop(0, 2, near)
    loop(2, G - 2, chunk)
    far = at_dp(G // 2)
    heard_all(q_all.at[far], r_q.at[far])
    attend(far, False)

    o_hm[...] = mm(perm[...], o_all[...]).astype(BF16)
    c_wv.wait()
    HB = 8

    def project(b):
        for i in range(HB):
            h = b * HB + i
            at = pl.ds(pl.multiple_of(h * NR, NR), NR)
            hv_hm[at, :] = mm(o_hm[at, :], wv[h]).astype(BF16)

    loop(0, H // HB, project)
    hv_s[...] = mm(perm_t[...], hv_hm[...]).astype(BF16).reshape(G, RH, DV)
    hv_r[g] = hv_s[g]
    lse_r[g] = lse_s[g]

    def send_hv(d):
        j = dp_peer(d)
        rcopy(lse_s.at[j], lse_r.at[g], s_lse, r_lse, dp_dev(j)).start()
        rcopy(hv_s.at[j], hv_r.at[g], s_hv, r_hv, dp_dev(j)).start()

    loop(1, G, send_hv)

    heard_all(win.at[1], r_win)
    loop(0, ELOC, lambda e: split(1, e))
    heard_all(sml_r.at[pl.ds(1, G - 1)], r_sml)
    siota = iota((ESL, 4 * GROUP), 0).astype(F32)
    for w in range(2):
        for e in range(ELOC):
            codes = []
            gvals = []
            for t in range(4):
                cj = sml_r[4 * w + t, e : e + 1, 0:GROUP]
                codes.append(jnp.where(cj >= 0, cj + float(t * CAPX), -1.0))
                gvals.append(sml_r[4 * w + t, ELOC + e : ELOC + e + 1, 0:GROUP])
            hit = siota == jnp.concatenate(codes, axis=1)
            sel[w, e] = hit.astype(F32).astype(BF16)
            gs = jnp.where(hit, jnp.concatenate(gvals, axis=1), 0.0)
            gcol[w, e] = jnp.broadcast_to(jnp.sum(gs, axis=1, keepdims=True), (ESL, 128))
        sel_t[w] = sel[w].reshape(ELOC * ESL, 4 * GROUP).T

    heard_all(lse_r.at[pl.ds(0, G - 1)], r_lse)
    heard_all(hv_r.at[pl.ds(0, G - 1)], r_hv)
    riota = iota((8, 128), 0)
    ls = jnp.full((8, 128), NEG, F32)
    for j in range(G):
        ls = jnp.where(riota == j, lse_r[j], ls)
    wts = jnp.exp(ls - jnp.max(ls, axis=0, keepdims=True))
    wts = wts / jnp.sum(wts, axis=0, keepdims=True)
    wcol = wts.T
    comb = jnp.zeros((RH, DV), F32)
    for j in range(G):
        comb = comb + wcol[0:RH, j : j + 1] * hv_r[j].astype(F32)
    hva[k] = comb.astype(BF16)

    plane = [(2, 2), (2, 1), (2, -1), (1, 2), (-1, 2), (2, 0), (0, 2)]
    plane += [(1, 1), (1, -1), (-1, 1), (-1, -1), (1, 0), (-1, 0), (0, 1), (0, -1)]
    for ox, oy in plane:
        rcopy(hva.at[k], hva.at[k], s_hva, r_hva.at[chip], at_chip(ox, oy)[2]).start()
    rcopy(hva.at[k], hva.at[k], s_hva, r_sib, exp_dev(sib)).start()
    for ox, oy in plane[::-1]:
        sx, sy, dev = at_chip(ox, oy)
        c = 4 * sy + sx
        got = hva.at[2 * c + core]
        heard_all(got, r_hva.at[c])
        rcopy(got, got, s_hva, r_sib, exp_dev(sib)).start()
    c_wo.wait()
    heard_all(hva.at[pl.ds(0, C // 2)], r_sib)

    for b in range(C // G):
        blk = mm(perm[...], hva[b * G : (b + 1) * G].reshape(N2, DV)).astype(BF16)
        for h in range(H):
            xmat[b * NR : (b + 1) * NR, h * DV : (h + 1) * DV] = blk[h * NR : (h + 1) * NR]
    proj = mm_nt(xmat[...], wo[...])
    resid = (res_ref[...].astype(F32) + proj).astype(BF16).astype(F32)
    xall[0, 0] = (resid * gain_ref[...]).astype(BF16)

    def x_copy(off, n):
        ref = xall.at[n // 4, n % 4]
        return rcopy(xall.at[0, 0], ref, s_x, r_x.at[n], dp_dev(at_dp(off)))

    def fwd(n):
        src, dst = xall.at[n // 4, n % 4], xsib.at[n // 4, n % 4]
        return rcopy(src, dst, s_fw, r_fwd[n // 4], exp_dev(sib))

    for off in (-1, 1, -2, 4, -3, 3, 2):
        x_copy(off, BACK[off]).start()
    fwd(0).start()
    sq = jnp.sum(resid * resid, axis=1, keepdims=True)
    sq_row = jnp.broadcast_to(sq, (GROUP, 128)).T[0:1]
    sq_s[...] = jnp.concatenate([sq_row] * (128 // GROUP), axis=1)
    sq_r[k] = sq_s[...]

    def send_sq(d):
        j = ex_peer(d)
        rcopy(sq_s, sq_r.at[k], s_sq, r_sq, exp_dev(j)).start()

    loop(1, C, send_sq)

    def get_x(w):
        for off in sorted(WAVES[w], key=abs):
            if off != 0:
                x_copy(off, POS[off]).wait_recv()
                fwd(POS[off]).start()
        heard_all(xsib.at[w], r_fwd[w])

    place = (cx, cy)

    def along(h, off):
        return at_chip(off, 0)[2] if h == 0 else at_chip(0, off)[2]

    def across(h, off):
        return at_chip(0, off)[2] if h == 0 else at_chip(off, 0)[2]

    def ring1(w, h, slot, src):
        sem = r_p1.at[3 * (2 * w + h) + min(slot, 2)]
        return rcopy(src, in1.at[w, h, slot], s_p1, sem, along(h, 1 if slot in (0, 2, 3) else -1))

    def block(e):
        return pl.ds(pl.multiple_of(e * ESL, 16), ESL)

    def partials(w):
        def step(i):
            e = lax.rem(cx + 2 + 3 * i, 4)
            xo = mm(sel[w, e], xall[w].reshape(4 * GROUP, W)).astype(BF16)
            xs = mm(sel[w, e], xsib[w].reshape(4 * GROUP, W)).astype(BF16)
            for f in range(4):
                cols = slice(2 * f * QF, 2 * (f + 1) * QF)
                both = mm(xo, wg[e, 0, :, cols]) + mm(xs, wg[e, 1, :, cols])
                part[w, f, block(e)] = both.astype(BF16)
            for h in range(2):
                role = lax.rem(e - place[h] + 4, 4)

                @pl.when(role == 2)
                def _():
                    ring1(w, h, 0, part.at[w, 2 * h, block(e)]).start()
                    ring1(w, h, 1, part.at[w, 2 * h + 1, block(e)]).start()

                @pl.when(role == 1)
                def _():
                    ring1(w, h, 2, part.at[w, 2 * h + 1, block(e)]).start()

                @pl.when(role == 3)
                def _():
                    ring1(w, h, 4, part.at[w, 2 * h, block(e)]).start()

        loop(0, 4, step)

    def relay(w):
        for h in range(2):
            for i in range(2):
                to = lax.rem(place[h] + (1, 3)[i], 4)
                ring1(w, h, i, in1.at[w, h, i]).wait_recv()
                passed = part[w, 2 * h + i, block(to)].astype(F32) + in1[w, h, i].astype(F32)
                out1[w, h, i] = passed.astype(BF16)
                ring1(w, h, 3 + 2 * i, out1.at[w, h, i]).start()

    def rows2(p):
        return pl.ds(pl.multiple_of(lax.div(p, 2) * QR, 16), QR)

    def ring2(w, h, off):
        to = lax.rem(place[1 - h] + off, 4)
        src = b2.at[w, h, lax.rem(to, 2), rows2(to)]
        return rcopy(src, in2.at[w, h, 4 - off], s_p2, r_p2.at[2 * w + h], across(h, off))

    def second(w):
        for h in range(2):
            heard_all(in1.at[w, h, pl.ds(2, 4)], r_p1.at[3 * (2 * w + h) + 2])
            for i in range(2):
                own = part[w, 2 * h + i, block(place[h])].astype(F32)
                got = in1[w, h, 4 - 2 * i].astype(F32) + in1[w, h, 3 + 2 * i].astype(F32)
                b2[w, h, i] = (own + got).astype(BF16)
            for off in (2, 1, 3):
                ring2(w, h, off).start()
            p = place[1 - h]
            in2[w, h, 0] = b2[w, h, lax.rem(p, 2), rows2(p)]

    def piece(w, h, x, y):
        p = (x, y)
        at = p[h] * ESL + lax.div(p[1 - h], 2) * QR
        return w, 2 * h + lax.rem(p[1 - h], 2), pl.ds(pl.multiple_of(at, 16), QR)

    around = [(1, 1), (1, -1), (-1, 1), (-1, -1), (1, 0), (-1, 0), (0, 1), (0, -1)]

    def hid_copy(w, h, sx, sy, n, dev):
        ref = hid.at[piece(w, h, sx, sy)]
        return rcopy(ref, ref, s_hid, r_hid.at[9 * w + n], dev)

    def hidden(w):
        irow = jnp.concatenate([inv_r[4 * w + t, 0:1, 0:GROUP] for t in range(4)], axis=1)
        for h in range(2):
            mine = sel[w, place[h], rows2(place[1 - h]), :]
            icol = jnp.sum(mine.astype(F32) * irow, axis=1, keepdims=True)
            heard_all(in2.at[w, h, pl.ds(1, 3)], r_p2.at[2 * w + h])
            tot = in2[w, h, 0].astype(F32)
            for j in range(1, 4):
                tot = tot + in2[w, h, j].astype(F32)
            tot = tot * icol
            ga = tot[:, 0:QF]
            hv = ga / (1.0 + jnp.exp(-ga)) * tot[:, QF : 2 * QF]
            hid[piece(w, h, cx, cy)] = hv.astype(BF16)
            for ox, oy in around:
                n = around.index((-ox, -oy))
                hid_copy(w, h, cx, cy, n, at_chip(ox, oy)[2]).start()

    def spread(w):
        for n, (ox, oy) in enumerate(around):
            sx, sy, _ = at_chip(ox, oy)
            heard_all(hid.at[w, pl.ds(0, 2), pl.ds(0, QR)], r_hid.at[9 * w + n])
            if ox == oy:
                hid_copy(w, int(ox > 0), sx, sy, 8, at_chip(-ox, -oy)[2]).start()
            if ox != 0:
                hid_copy(w, int(ox > 0), sx, sy, 8, at_chip(-ox, 0)[2]).start()
            if oy != 0:
                hid_copy(w, int(oy > 0), sx, sy, 8, at_chip(0, -oy)[2]).start()

    def down(w):
        heard_all(hid.at[w, pl.ds(0, 2), pl.ds(0, 7 * QR)], r_hid.at[9 * w + 8])

        def step(e):
            at = block(e)
            he = jnp.concatenate([hid[w, f, at] for f in range(4)], axis=1)
            gs = gcol[w, e, :, 0:1]
            vsib[w, at, :] = (mm_nt(he, wout[1, e]) * gs).astype(BF16)
            vown[w, at, :] = (mm_nt(he, wout[0, e]) * gs).astype(BF16)

        loop(0, ELOC, step)
        zsib_s[w] = mm(sel_t[w], vsib[w]).astype(BF16)
        zsib_copy(w).start()
        zown[w] = mm(sel_t[w], vown[w])

    def zsib_copy(w):
        return rcopy(zsib_s.at[w], zsib_r.at[w], s_zsib, r_zsib[w], exp_dev(sib))

    def z_copy(off, n):
        ref = zs.at[POS[off] // 4, POS[off] % 4]
        return rcopy(ref, zr.at[n], s_z, r_z, dp_dev(at_dp(off)))

    def give_back(w):
        zsib_copy(w).wait_recv()
        zsum = zown[w] + zsib_r[w].astype(F32)
        zown[w] = zsum
        zs[w] = zsum.astype(BF16).reshape(4, GROUP, W)
        for off in sorted(WAVES[w], key=lambda o: -abs(o)):
            if off != 0:
                z_copy(off, BACK[off]).start()

    get_x(0)
    partials(0)

    heard_all(sq_r.at[pl.ds(0, C - 1)], r_sq)
    inv_s[...] = lax.rsqrt(jnp.sum(sq_r[...], axis=0) / D + EPS)
    inv_r[0] = inv_s[...]

    def inv_copy(off, n):
        return rcopy(inv_s, inv_r.at[n], s_inv, r_inv, dp_dev(at_dp(off)))

    for off in others:
        inv_copy(off, BACK[off]).start()
    get_x(1)
    partials(1)
    relay(0)
    second(0)
    relay(1)
    heard_all(inv_r.at[pl.ds(1, G - 1)], r_inv)
    hidden(0)
    second(1)
    spread(0)
    hidden(1)
    c_wout.wait()
    heard_all(wout.at[1], r_wout)
    down(0)
    spread(1)
    give_back(0)
    down(1)
    give_back(1)
    total = resid + zown[0, 0:GROUP, :]

    w1.wait_send()
    w2.wait_send()
    seven = pl.ds(0, G - 1)
    sent_all(q_all.at[seven], s_q)
    sent_all(sml_r.at[seven], s_sml)
    sent_all(hv_r.at[seven], s_hv)
    sent_all(lse_r.at[seven], s_lse)
    sent_all(hva.at[pl.ds(0, C - 1)], s_hva)
    sent_all(zr.at[seven], s_x)
    sent_all(zr, s_fw)
    sent_all(sq_r.at[pl.ds(0, C - 1)], s_sq)
    sent_all(inv_r.at[seven], s_inv)
    sent_all(in1, s_p1)
    sent_all(in2.at[:, :, pl.ds(0, 3)], s_p2)
    sent_all(wv.at[pl.ds(0, 30), pl.ds(0, 2 * QR)], s_hid)
    sent_all(zsib_r, s_zsib)

    heard_all(zr.at[pl.ds(1, G - 1)], r_z)
    for n in range(1, G):
        total = total + zr[n].astype(F32)
    out_ref[...] = total.astype(BF16)
    sent_all(zr.at[seven], s_z)


def body(
    queries, new_latent, pool_pages, page_owner, page_slot, lengths, residual, value_weight,
    output_weight, norm_gain, expert_ids, route_gates, expert_in, expert_out,
):
    G = lax.axis_size("dp")
    C = lax.axis_size("expert")
    ROWS, H, LAT = queries.shape
    NS, _, PAGE = pool_pages.shape
    GROUP, W = residual.shape
    ELOC, _, _, FF = expert_in.shape
    FH = FF // 2
    RH = ROWS * H
    capacity = min(GROUP, (3 * GROUP * TOP + 2 * G * ELOC - 1) // (2 * G * ELOC))
    ESL = 4 * capacity
    SLOTS = ELOC * ESL
    QR, QC = ESL // 2, FF // 4
    N2 = G * RH
    HALF = 4 * GROUP

    def v(shape, dtype=BF16):
        return pltpu.VMEM(shape, dtype)

    dma = lambda n: pltpu.SemaphoreType.DMA((n,))
    scratch = [
        v(new_latent.shape), pltpu.SMEM(page_owner.shape, jnp.int32),
        pltpu.SMEM(page_slot.shape, jnp.int32), pltpu.SMEM(lengths.shape, jnp.int32),
        v((GROUP, W)), v((1, W), F32), v((TOP, GROUP), jnp.int32), v((TOP, GROUP), F32),
        v((LAT, NS * PAGE)), v((NS * PAGE, KVR)), v((128, LAT)), v((ROWS, H, LAT)),
        v((G, ROWS, H, -(-(LAT + 2) // 128) * 128)),
        v((G, 8, 128), F32), v((G, 8, 128), F32), v((N2, N2)), v((N2, N2)),
        v((N2, KVR)), v((N2, KVR)), v((N2, DV)), v((G, RH, DV)), v((G, 1, 128), F32),
        v((G, RH, DV)), v((G, 1, 128), F32),
        v((C, RH, DV)), v((GROUP, H * DV)), v((H, KVR, DV)), v((W, H * DV)),
        v((2, ELOC, W, 2, FH)), v((ELOC, 2, W, FF)), v((2, ELOC, W, FH)),
        v((2, 4, GROUP, W)), v((2, 4, GROUP, W)), v((1, 128), F32), v((C, 1, 128), F32),
        v((1, 128), F32), v((G, 1, 128), F32),
        v((2, ELOC, ESL, HALF)), v((2, HALF, SLOTS)), v((2, ELOC, ESL, 128), F32),
        v((2, 4, SLOTS, QC)), v((2, 2, 6, ESL, QC)), v((2, 2, 2, ESL, QC)), v((2, 2, 2, ESL, QC)),
        v((2, 2, 4, QR, QC)), v((2, 4, SLOTS, QC // 2)), v((2, SLOTS, W)), v((2, SLOTS, W)),
        v((2, HALF, W)), v((2, HALF, W)), v((2, 4, GROUP, W)), v((G, GROUP, W)),
        v((2, HALF, W), F32),
        dma(14), dma(16), dma(13), dma(G), dma(G), dma(C // 2), dma(12), dma(4), dma(18),
    ]
    vm = pl.BlockSpec(memory_space=pltpu.VMEM)
    hbm = pl.BlockSpec(memory_space=pl.ANY)
    return pl.pallas_call(
        functools.partial(kernel, G, C, ELOC, capacity),
        out_shape=jax.ShapeDtypeStruct((GROUP, W), BF16),
        in_specs=[hbm] * 14,
        out_specs=vm,
        scratch_shapes=scratch,
        compiler_params=pltpu.CompilerParams(
            collective_id=0, has_side_effects=True, vmem_limit_bytes=56 << 20
        ),
        cost_estimate=pl.CostEstimate(flops=4 << 30, bytes_accessed=16 << 20, transcendentals=1 << 20),
        name="decode_step",
    )(
        queries, new_latent, pool_pages, page_owner, page_slot, lengths, residual, value_weight,
        output_weight.T, norm_gain.reshape(1, W), expert_ids.T, route_gates.T, expert_in,
        jnp.swapaxes(expert_out, 1, 2),
    )


def solution(mesh):
    in_specs = (
        P(("dp", "expert"), None, None),
        P(("dp", "expert"), None),
        P(("dp", "expert"), None, None),
        P(None, "expert", None, None),
        P(None, "expert", None, None),
        P(("dp", "expert")),
        P("dp", "expert"),
        P(),
        P(None, "expert"),
        P("expert"),
        P("dp", None),
        P("dp", None),
        P("dp", "expert", None, None),
        P("dp", None, "expert"),
    )
    return jax.shard_map(
        body, mesh=mesh, in_specs=in_specs, out_specs=P("dp", "expert"), check_vma=False
    )
```

```python
import functools
import jax
import jax.numpy as jnp
from jax import lax
from jax.experimental import pallas as pl
from jax.experimental.pallas import tpu as pltpu
from jax.sharding import PartitionSpec as P

D = 7168
KVR = 512
ROPE = 64
DV = 128
TOP = 8
EPS = 1e-06
MESH = pl.DeviceIdType.MESH
F32 = jnp.float32
BF16 = jnp.bfloat16
NEG = -1e30
WAVES = ((4, -3, 3, -2), (0, 1, -1, 2))
POS = {off: 4 * w + t for w in range(2) for t, off in enumerate(WAVES[w])}
ME = POS[0]
BACK = {off: POS[4 if off == 4 else -off] for off in POS}


def iota(shape, dim):
    return lax.broadcasted_iota(jnp.int32, shape, dim)


def mm(a, b):
    return jnp.dot(a, b, preferred_element_type=F32)


def mm_nt(a, b):
    return lax.dot_general(a, b, (((1,), (1,)), ((), ())), preferred_element_type=F32)


def kernel(
    G, C, ELOC, CAPX,
    q_hbm, nl_hbm, pool_hbm, owner_hbm, slot_hbm, len_hbm, res_hbm, wv_hbm, wo_hbm, gain_hbm,
    ids_hbm, gates_hbm, win_hbm, wout_hbm,
    out_ref,
    nl_ref, owner_ref, slot_ref, len_ref, res_ref, gain_ref, ids_ref, gates_ref,
    kc, vt, nlp, q_in, q_all, sml_s, sml_r, perm, perm_t, o_all, o_hm, hv_hm, hv_s, lse_s, hv_r,
    lse_r, hva, xmat, wv, wo, win, wg, wout, xall, xsib, sq_s, sq_r, inv_s, inv_r,
    sel, sel_t, gcol, part, in1, out1, b2, in2, hid, vown, vsib, zsib_s, zsib_r, zs, zr, zown,
    lsem, sent, heard, r_q, r_x, r_hva, r_sib, r_p1, r_p2, r_hid,
):
    g = lax.axis_index("dp")
    k = lax.axis_index("expert")
    core = lax.rem(k, 2)
    chip = lax.div(k, 2)
    sib = k + 1 - 2 * core
    cx = lax.rem(chip, 4)
    cy = lax.div(chip, 4)
    ROWS, H, LAT = q_in.shape
    NS = pool_hbm.shape[0]
    PAGE = pool_hbm.shape[2]
    RH = ROWS * H
    GROUP = C * ROWS
    W = res_ref.shape[1]
    FF = win_hbm.shape[3]
    FH = FF // 2
    ESL = 4 * CAPX
    QR = ESL // 2
    QF = FH // 4
    NR = G * ROWS

    def dp_peer(d):
        half = lax.div(G + 1 - d, 2)
        off = half * (1 - 2 * lax.rem(G + 1 - d, 2))
        return lax.rem(g + off + G, G)

    def at_dp(off):
        return lax.rem(g + off + G, G)

    def ex_peer(d):
        return lax.rem(k + d, C)

    def at_chip(ox, oy):
        x = lax.rem(cx + ox + 4, 4)
        y = lax.rem(cy + oy + 4, 4)
        return x, y, (g, 2 * (4 * y + x) + core)

    s_q, s_sml, s_hv, s_lse, s_hva, s_x, s_fw, s_sq = (sent.at[i] for i in range(8))
    s_inv, s_p1, s_p2, s_hid, s_win, s_wout, s_zsib, s_z = (sent.at[8 + i] for i in range(8))
    r_sml, r_hv, r_lse, r_inv, r_z, r_sq, r_win, r_wout = (heard.at[i] for i in range(8))
    r_fwd, r_zsib = (heard.at[8], heard.at[9]), (heard.at[10], heard.at[11])

    def rcopy(src, dst, ss, rs, dev):
        return pltpu.make_async_remote_copy(
            src_ref=src, dst_ref=dst, send_sem=ss, recv_sem=rs, device_id=dev, device_id_type=MESH
        )

    def sent_all(ref, sem):
        rcopy(ref, ref, sem, sem, exp_dev(sib)).wait_send()

    def heard_all(ref, sem):
        rcopy(ref, ref, sem, sem, exp_dev(sib)).wait_recv()

    def loop(lo, hi, fn):
        lax.fori_loop(lo, hi, lambda i, c: (fn(i), c)[1], 0)

    def exp_dev(kk):
        return (g, kk)

    def dp_dev(j):
        return (j, k)

    locals_ = []
    for s in range(NS):
        locals_.append(
            pltpu.make_async_copy(pool_hbm.at[s], kc.at[:, pl.ds(s * PAGE, PAGE)], lsem.at[0])
        )
    c_q = pltpu.make_async_copy(q_hbm, q_in, lsem.at[1])
    c_win = pltpu.make_async_copy(
        win_hbm.at[:, :, :, pl.ds(pl.multiple_of(core * FH, FH), FH)], win.at[0], lsem.at[2]
    )
    c_wv = pltpu.make_async_copy(wv_hbm, wv, lsem.at[3])
    c_wo = pltpu.make_async_copy(wo_hbm, wo, lsem.at[4])
    c_wout = pltpu.make_async_copy(
        wout_hbm.at[:, :, pl.ds(pl.multiple_of(core * FH, FH), FH)], wout.at[0], lsem.at[5]
    )
    c_q.start()
    small = []
    for i, (a, b) in enumerate(
        (
            (ids_hbm, ids_ref), (gates_hbm, gates_ref), (len_hbm, len_ref), (nl_hbm, nl_ref),
            (owner_hbm, owner_ref), (slot_hbm, slot_ref), (res_hbm, res_ref), (gain_hbm, gain_ref),
        )
    ):
        small.append(pltpu.make_async_copy(a, b, lsem.at[6 + i]))
        small[-1].start()
    for c in locals_:
        c.start()
    for c in (c_win, c_wv, c_wo, c_wout):
        c.start()

    barrier = pltpu.get_barrier_semaphore()

    def sig_dp(d):
        pl.semaphore_signal(barrier, inc=1, device_id=dp_dev(lax.rem(g + d, G)), device_id_type=MESH)

    def sig_ex(d):
        pl.semaphore_signal(barrier, inc=1, device_id=exp_dev(ex_peer(d)), device_id_type=MESH)

    loop(1, G, sig_dp)
    loop(1, C, sig_ex)

    c_q.wait()
    small[2].wait()
    for r in range(ROWS):
        n = len_ref[r]
        li = iota((H, q_all.shape[3] - LAT), 1)
        tail = jnp.where(li == 0, lax.div(n, 32), jnp.where(li == 1, lax.rem(n, 32), 0))
        q_all[g, r] = jnp.concatenate([q_in[r], tail.astype(F32).astype(BF16)], axis=1)
    pl.semaphore_wait(barrier, G - 1 + C - 1)

    def q_copy(src, off, row=None):
        ref = q_all.at[src] if row is None else q_all.at[src, row]
        return rcopy(ref, ref, s_q, r_q.at[src], dp_dev(at_dp(off)))

    for off in (2, -2, 1, -1):
        q_copy(g, off).start()

    for i, c in enumerate(small):
        if i != 2:
            c.wait()
    ids = ids_ref[...]
    gates = gates_ref[...]
    e_iota = iota((G * ELOC, GROUP), 0)
    named = jnp.zeros((G * ELOC, GROUP), F32)
    gval = jnp.zeros((G * ELOC, GROUP), F32)
    for t in range(TOP):
        hit = ids[t : t + 1, :] == e_iota
        named = named + hit.astype(F32)
        gval = gval + jnp.where(hit, gates[t : t + 1, :], 0.0)
    tri = (iota((GROUP, GROUP), 0) < iota((GROUP, GROUP), 1)).astype(BF16)
    rank = mm(named.astype(BF16), tri)
    code = jnp.where(named > 0, rank, -1.0)
    sml_s[...] = jnp.zeros_like(sml_s)
    for j in range(G):
        sml_s[j, 0:ELOC, 0:GROUP] = code[j * ELOC : (j + 1) * ELOC]
        sml_s[j, ELOC : 2 * ELOC, 0:GROUP] = gval[j * ELOC : (j + 1) * ELOC]
    sml_r[ME] = sml_s[g]

    N2 = NR * H
    pr = iota((N2, 1), 0)
    perm[...] = (iota((N2, N2), 1) == lax.rem(pr, NR) * H + lax.div(pr, NR)).astype(BF16)
    perm_t[...] = (iota((N2, N2), 1) == lax.rem(pr, H) * NR + lax.div(pr, H)).astype(BF16)
    nl = nl_ref[...].astype(F32)
    nrow = iota((128, LAT), 0)
    nacc = jnp.zeros((128, LAT), F32)
    for s in range(ROWS):
        nacc = jnp.where(nrow == s, nl[s : s + 1, :], nacc)
    nlp[...] = nacc.astype(BF16)

    other = pl.multiple_of((1 - core) * FH, FH)
    w1 = rcopy(win_hbm.at[:, :, :, pl.ds(other, FH)], win.at[1], s_win, r_win, exp_dev(sib))
    w2 = rcopy(wout_hbm.at[:, :, pl.ds(other, FH)], wout.at[1], s_wout, r_wout, exp_dev(sib))
    w1.start()
    w2.start()

    pltpu.make_async_copy(kc, kc, lsem.at[0]).wait()
    vt[...] = kc[0:KVR, :].T

    scale = (DV + ROPE) ** (-0.5)
    NT = NS * PAGE

    def attend(src, own):
        qx = q_all[src].reshape(RH, q_all.shape[3])
        q = qx[:, 0:LAT]
        sc = mm(q, kc[...]) * scale
        lid = iota((1, NT), 1)
        slot_lane = lax.div(lid, PAGE)
        tpos = lax.rem(lid, PAGE).astype(F32)
        rows = []
        for s in range(ROWS):
            lv = qx[s * H : s * H + 8, LAT : LAT + 2].astype(F32)
            ln = lv[0:1, 0:1] * 32.0 + lv[0:1, 1:2]
            cnt = jnp.zeros((1, NT), F32)
            for p in range(owner_ref.shape[3]):
                here = jnp.where(owner_ref[src, 0, s, p] == g, slot_ref[src, 0, s, p], -1)
                ok = jnp.logical_and(slot_lane == here, tpos + float(p * PAGE) < ln)
                cnt = cnt + ok.astype(F32)
            rows.append(jnp.broadcast_to(cnt, (H, NT)))
        cnt = jnp.concatenate(rows, axis=0)
        scm = jnp.where(cnt > 0, sc, NEG)
        top = jnp.max(scm, axis=1, keepdims=True)
        if own:
            cs = (iota((RH, 128), 1) == lax.div(iota((RH, 128), 0), H)).astype(F32)
            ss = jnp.where(cs > 0, mm_nt(q, nlp[...]) * scale, NEG)
            top = jnp.maximum(top, jnp.max(ss, axis=1, keepdims=True))
        p = cnt * jnp.exp(scm - top)
        den = jnp.sum(p, axis=1, keepdims=True)
        acc = mm(p.astype(BF16), vt[...])
        if own:
            pself = cs * jnp.exp(ss - top)
            den = den + jnp.sum(pself, axis=1, keepdims=True)
            acc = acc + mm(pself.astype(BF16), nlp[:, 0:KVR])
        has = den > 0
        inv_den = jnp.where(has, 1.0 / jnp.where(has, den, 1.0), 0.0)
        lse = jnp.where(has, top + jnp.log(jnp.where(has, den, 1.0)), NEG)
        o_all[pl.ds(pl.multiple_of(src * RH, RH), RH), :] = (acc * inv_den).astype(BF16)
        row = jnp.broadcast_to(lse, (RH, 128)).T[0:1]
        lse_s[src] = jnp.concatenate([row, row], axis=1)

    attend(g, True)

    col = iota((W, 2 * W), 1)
    two = 2 * iota((W, 2 * W), 0)
    pick_g = (col == two).astype(BF16)
    pick_u = (col == two + 1).astype(BF16)

    def split(o, e):
        w = win[o, e].reshape(2 * W, FH)
        wgate = mm(pick_g, w).astype(BF16)
        wup = mm(pick_u, w).astype(BF16)
        for f in range(4):
            wg[e, o, :, 2 * f * QF : (2 * f + 1) * QF] = wgate[:, f * QF : (f + 1) * QF]
            wg[e, o, :, (2 * f + 1) * QF : 2 * (f + 1) * QF] = wup[:, f * QF : (f + 1) * QF]

    c_win.wait()
    loop(0, ELOC, lambda e: split(0, e))

    for i, off in ((0, -2), (1, 2)):
        src = at_dp(off)
        q_copy(src, off).wait_recv()
        q_copy(src, 1 - 2 * i).start()
        q_copy(src, 2 - 4 * i, row=i).start()

    def sml_copy(off, n):
        j = at_dp(off)
        return rcopy(sml_s.at[j], sml_r.at[n], s_sml, r_sml, dp_dev(j))

    others = [4, -3, 3, -2, 2, -1, 1]
    for off in others:
        sml_copy(off, BACK[off]).start()

    def ring(d):
        n = lax.div(d, 2)
        m = jnp.where(n == 0, 2, jnp.where(n == 1, 1, n + 1))
        return at_dp(jnp.where(lax.rem(d, 2) == 0, -m, m))

    def near(d):
        attend(ring(d), False)

    def chunk(d):
        src = ring(d)
        heard_all(q_all.at[src], r_q.at[src])
        attend(src, False)

    loop(0, 2, near)
    loop(2, G - 2, chunk)
    far = at_dp(G // 2)
    heard_all(q_all.at[far], r_q.at[far])
    attend(far, False)

    o_hm[...] = mm(perm[...], o_all[...]).astype(BF16)
    c_wv.wait()
    HB = 16

    def project(b):
        for i in range(HB):
            h = b * HB + i
            at = pl.ds(pl.multiple_of(h * NR, NR), NR)
            hv_hm[at, :] = mm(o_hm[at, :], wv[h]).astype(BF16)

    loop(0, H // HB, project)
    hv_s[...] = mm(perm_t[...], hv_hm[...]).astype(BF16).reshape(G, RH, DV)
    hv_r[g] = hv_s[g]
    lse_r[g] = lse_s[g]

    def send_hv(d):
        j = dp_peer(d)
        rcopy(lse_s.at[j], lse_r.at[g], s_lse, r_lse, dp_dev(j)).start()
        rcopy(hv_s.at[j], hv_r.at[g], s_hv, r_hv, dp_dev(j)).start()

    loop(1, G, send_hv)

    heard_all(win.at[1], r_win)
    loop(0, ELOC, lambda e: split(1, e))
    heard_all(sml_r.at[pl.ds(0, G - 1)], r_sml)
    siota = iota((ESL, 4 * GROUP), 0).astype(F32)
    for w in range(2):
        for e in range(ELOC):
            codes = []
            gvals = []
            for t in range(4):
                cj = sml_r[4 * w + t, e : e + 1, 0:GROUP]
                codes.append(jnp.where(cj >= 0, cj + float(t * CAPX), -1.0))
                gvals.append(sml_r[4 * w + t, ELOC + e : ELOC + e + 1, 0:GROUP])
            hit = siota == jnp.concatenate(codes, axis=1)
            sel[w, e] = hit.astype(F32).astype(BF16)
            gs = jnp.where(hit, jnp.concatenate(gvals, axis=1), 0.0)
            gcol[w, e] = jnp.broadcast_to(jnp.sum(gs, axis=1, keepdims=True), (ESL, 128))
        sel_t[w] = sel[w].reshape(ELOC * ESL, 4 * GROUP).T

    heard_all(lse_r.at[pl.ds(0, G - 1)], r_lse)
    heard_all(hv_r.at[pl.ds(0, G - 1)], r_hv)
    riota = iota((8, 128), 0)
    ls = jnp.full((8, 128), NEG, F32)
    for j in range(G):
        ls = jnp.where(riota == j, lse_r[j], ls)
    wts = jnp.exp(ls - jnp.max(ls, axis=0, keepdims=True))
    wts = wts / jnp.sum(wts, axis=0, keepdims=True)
    wcol = wts.T
    comb = jnp.zeros((RH, DV), F32)
    for j in range(G):
        comb = comb + wcol[0:RH, j : j + 1] * hv_r[j].astype(F32)
    hva[k] = comb.astype(BF16)

    plane = [(2, 2), (2, 1), (2, -1), (1, 2), (-1, 2), (2, 0), (0, 2)]
    plane += [(1, 1), (1, -1), (-1, 1), (-1, -1), (1, 0), (-1, 0), (0, 1), (0, -1)]
    for ox, oy in plane:
        rcopy(hva.at[k], hva.at[k], s_hva, r_hva.at[chip], at_chip(ox, oy)[2]).start()
    rcopy(hva.at[k], hva.at[k], s_hva, r_sib.at[cy], exp_dev(sib)).start()
    for ox, oy in plane[::-1]:
        sx, sy, dev = at_chip(ox, oy)
        c = 4 * sy + sx
        got = hva.at[2 * c + core]
        heard_all(got, r_hva.at[c])
        rcopy(got, got, s_hva, r_sib.at[sy], exp_dev(sib)).start()
    c_wo.wait()
    for off in (0, 1, 3, 2):
        y = lax.rem(cy + off, 4)
        heard_all(hva.at[pl.ds(0, 4)], r_sib.at[y])
        blk = mm(perm[...], hva[pl.ds(8 * y, 8)].reshape(N2, DV)).astype(BF16)
        for h in range(H):
            at = pl.ds(pl.multiple_of(y * NR, NR), NR)
            xmat[at, h * DV : (h + 1) * DV] = blk[h * NR : (h + 1) * NR]
    proj = mm_nt(xmat[...], wo[...])
    resid = (res_ref[...].astype(F32) + proj).astype(BF16).astype(F32)
    xall[1, 0] = (resid * gain_ref[...]).astype(BF16)

    def x_copy(off, n):
        ref = xall.at[n // 4, n % 4]
        return rcopy(xall.at[1, 0], ref, s_x, r_x.at[n], dp_dev(at_dp(off)))

    def fwd(n):
        src, dst = xall.at[n // 4, n % 4], xsib.at[n // 4, n % 4]
        return rcopy(src, dst, s_fw, r_fwd[n // 4], exp_dev(sib))

    for off in others:
        x_copy(off, BACK[off]).start()
    fwd(ME).start()
    sq = jnp.sum(resid * resid, axis=1, keepdims=True)
    sq_row = jnp.broadcast_to(sq, (GROUP, 128)).T[0:1]
    sq_s[...] = jnp.concatenate([sq_row] * (128 // GROUP), axis=1)
    sq_r[k] = sq_s[...]

    def send_sq(d):
        j = ex_peer(d)
        rcopy(sq_s, sq_r.at[k], s_sq, r_sq, exp_dev(j)).start()

    loop(1, C, send_sq)

    def get_x(w):
        for off in sorted(WAVES[w], key=abs):
            if off != 0:
                x_copy(off, POS[off]).wait_recv()
                fwd(POS[off]).start()
        heard_all(xsib.at[w], r_fwd[w])

    place = (cx, cy)

    def along(h, off):
        return at_chip(off, 0)[2] if h == 0 else at_chip(0, off)[2]

    def across(h, off):
        return at_chip(0, off)[2] if h == 0 else at_chip(off, 0)[2]

    def ring1(w, h, slot, src):
        sem = r_p1.at[3 * (2 * w + h) + min(slot, 2)]
        return rcopy(src, in1.at[w, h, slot], s_p1, sem, along(h, 1 if slot in (0, 2, 3) else -1))

    def block(e):
        return pl.ds(pl.multiple_of(e * ESL, 16), ESL)

    def partials(w):
        def step(i):
            e = lax.rem(cx + 2 + 3 * i, 4)
            xo = mm(sel[w, e], xall[w].reshape(4 * GROUP, W)).astype(BF16)
            xs = mm(sel[w, e], xsib[w].reshape(4 * GROUP, W)).astype(BF16)
            for f in range(4):
                cols = slice(2 * f * QF, 2 * (f + 1) * QF)
                both = mm(xo, wg[e, 0, :, cols]) + mm(xs, wg[e, 1, :, cols])
                part[w, f, block(e)] = both.astype(BF16)
            for h in range(2):
                role = lax.rem(e - place[h] + 4, 4)

                @pl.when(role == 2)
                def _():
                    ring1(w, h, 0, part.at[w, 2 * h, block(e)]).start()
                    ring1(w, h, 1, part.at[w, 2 * h + 1, block(e)]).start()

                @pl.when(role == 1)
                def _():
                    ring1(w, h, 2, part.at[w, 2 * h + 1, block(e)]).start()

                @pl.when(role == 3)
                def _():
                    ring1(w, h, 4, part.at[w, 2 * h, block(e)]).start()

        loop(0, 4, step)

    def relay(w):
        for h in range(2):
            for i in range(2):
                to = lax.rem(place[h] + (1, 3)[i], 4)
                ring1(w, h, i, in1.at[w, h, i]).wait_recv()
                passed = part[w, 2 * h + i, block(to)].astype(F32) + in1[w, h, i].astype(F32)
                out1[w, h, i] = passed.astype(BF16)
                ring1(w, h, 3 + 2 * i, out1.at[w, h, i]).start()

    def rows2(p):
        return pl.ds(pl.multiple_of(lax.div(p, 2) * QR, 16), QR)

    def ring2(w, h, off):
        to = lax.rem(place[1 - h] + off, 4)
        src = b2.at[w, h, lax.rem(to, 2), rows2(to)]
        return rcopy(src, in2.at[w, h, 4 - off], s_p2, r_p2.at[2 * w + h], across(h, off))

    def second(w):
        for h in range(2):
            heard_all(in1.at[w, h, pl.ds(2, 4)], r_p1.at[3 * (2 * w + h) + 2])
            for i in range(2):
                own = part[w, 2 * h + i, block(place[h])].astype(F32)
                got = in1[w, h, 4 - 2 * i].astype(F32) + in1[w, h, 3 + 2 * i].astype(F32)
                b2[w, h, i] = (own + got).astype(BF16)
            for off in (2, 1, 3):
                ring2(w, h, off).start()
            p = place[1 - h]
            in2[w, h, 0] = b2[w, h, lax.rem(p, 2), rows2(p)]

    def piece(w, h, x, y):
        p = (x, y)
        at = p[h] * ESL + lax.div(p[1 - h], 2) * QR
        return w, 2 * h + lax.rem(p[1 - h], 2), pl.ds(pl.multiple_of(at, 16), QR)

    around = [(1, 1), (1, -1), (-1, 1), (-1, -1), (1, 0), (-1, 0), (0, 1), (0, -1)]

    def hid_copy(w, h, sx, sy, n, dev):
        ref = hid.at[piece(w, h, sx, sy)]
        return rcopy(ref, ref, s_hid, r_hid.at[9 * w + n], dev)

    def hidden(w):
        irow = jnp.concatenate([inv_r[4 * w + t, 0:1, 0:GROUP] for t in range(4)], axis=1)
        for h in range(2):
            mine = sel[w, place[h], rows2(place[1 - h]), :]
            icol = jnp.sum(mine.astype(F32) * irow, axis=1, keepdims=True)
            heard_all(in2.at[w, h, pl.ds(1, 3)], r_p2.at[2 * w + h])
            tot = in2[w, h, 0].astype(F32)
            for j in range(1, 4):
                tot = tot + in2[w, h, j].astype(F32)
            tot = tot * icol
            ga = tot[:, 0:QF]
            hv = ga / (1.0 + jnp.exp(-ga)) * tot[:, QF : 2 * QF]
            hid[piece(w, h, cx, cy)] = hv.astype(BF16)
            for ox, oy in around:
                n = around.index((-ox, -oy))
                hid_copy(w, h, cx, cy, n, at_chip(ox, oy)[2]).start()

    def spread(w):
        for n, (ox, oy) in enumerate(around):
            sx, sy, _ = at_chip(ox, oy)
            heard_all(hid.at[w, pl.ds(0, 2), pl.ds(0, QR)], r_hid.at[9 * w + n])
            if ox == oy:
                hid_copy(w, int(ox > 0), sx, sy, 8, at_chip(-ox, -oy)[2]).start()
            if ox != 0:
                hid_copy(w, int(ox > 0), sx, sy, 8, at_chip(-ox, 0)[2]).start()
            if oy != 0:
                hid_copy(w, int(oy > 0), sx, sy, 8, at_chip(0, -oy)[2]).start()

    def down(w):
        heard_all(hid.at[w, pl.ds(0, 2), pl.ds(0, 7 * QR)], r_hid.at[9 * w + 8])

        def step(e):
            at = block(e)
            he = jnp.concatenate([hid[w, f, at] for f in range(4)], axis=1)
            gs = gcol[w, e, :, 0:1]
            vsib[w, at, :] = (mm_nt(he, wout[1, e]) * gs).astype(BF16)
            vown[w, at, :] = (mm_nt(he, wout[0, e]) * gs).astype(BF16)

        loop(0, ELOC, step)
        zsib_s[w] = mm(sel_t[w], vsib[w]).astype(BF16)
        zsib_copy(w).start()
        zown[w] = mm(sel_t[w], vown[w])

    def zsib_copy(w):
        return rcopy(zsib_s.at[w], zsib_r.at[w], s_zsib, r_zsib[w], exp_dev(sib))

    def z_copy(off, n):
        ref = zs.at[POS[off] // 4, POS[off] % 4]
        return rcopy(ref, zr.at[n], s_z, r_z, dp_dev(at_dp(off)))

    def give_back(w):
        zsib_copy(w).wait_recv()
        zsum = zown[w] + zsib_r[w].astype(F32)
        zown[w] = zsum
        zs[w] = zsum.astype(BF16).reshape(4, GROUP, W)
        for off in sorted(WAVES[w], key=lambda o: -abs(o)):
            if off != 0:
                z_copy(off, BACK[off]).start()

    get_x(0)
    partials(0)

    heard_all(sq_r.at[pl.ds(0, C - 1)], r_sq)
    inv_s[...] = lax.rsqrt(jnp.sum(sq_r[...], axis=0) / D + EPS)
    inv_r[ME] = inv_s[...]

    def inv_copy(off, n):
        return rcopy(inv_s, inv_r.at[n], s_inv, r_inv, dp_dev(at_dp(off)))

    for off in others:
        inv_copy(off, BACK[off]).start()
    get_x(1)
    partials(1)
    relay(0)
    relay(1)
    second(0)
    second(1)
    heard_all(inv_r.at[pl.ds(0, G - 1)], r_inv)
    hidden(0)
    hidden(1)
    spread(0)
    spread(1)
    c_wout.wait()
    heard_all(wout.at[1], r_wout)
    down(0)
    give_back(0)
    down(1)
    give_back(1)
    total = resid + zown[1, 0:GROUP, :]

    w1.wait_send()
    w2.wait_send()
    seven = pl.ds(0, G - 1)
    sent_all(q_all.at[seven], s_q)
    sent_all(sml_r.at[seven], s_sml)
    sent_all(hv_r.at[seven], s_hv)
    sent_all(lse_r.at[seven], s_lse)
    sent_all(hva.at[pl.ds(0, C - 1)], s_hva)
    sent_all(zr.at[seven], s_x)
    sent_all(zr, s_fw)
    sent_all(sq_r.at[pl.ds(0, C - 1)], s_sq)
    sent_all(inv_r.at[seven], s_inv)
    sent_all(in1, s_p1)
    sent_all(in2.at[:, :, pl.ds(0, 3)], s_p2)
    sent_all(wv.at[pl.ds(0, 30), pl.ds(0, 2 * QR)], s_hid)
    sent_all(zsib_r, s_zsib)

    heard_all(zr.at[seven], r_z)
    for off in others:
        total = total + zr[POS[off]].astype(F32)
    out_ref[...] = total.astype(BF16)
    sent_all(zr.at[seven], s_z)


def body(
    queries, new_latent, pool_pages, page_owner, page_slot, lengths, residual, value_weight,
    output_weight, norm_gain, expert_ids, route_gates, expert_in, expert_out,
):
    G = lax.axis_size("dp")
    C = lax.axis_size("expert")
    ROWS, H, LAT = queries.shape
    NS, _, PAGE = pool_pages.shape
    GROUP, W = residual.shape
    ELOC, _, _, FF = expert_in.shape
    FH = FF // 2
    RH = ROWS * H
    capacity = min(GROUP, (3 * GROUP * TOP + 2 * G * ELOC - 1) // (2 * G * ELOC))
    ESL = 4 * capacity
    SLOTS = ELOC * ESL
    QR, QC = ESL // 2, FF // 4
    N2 = G * RH
    HALF = 4 * GROUP

    def v(shape, dtype=BF16):
        return pltpu.VMEM(shape, dtype)

    dma = lambda n: pltpu.SemaphoreType.DMA((n,))
    scratch = [
        v(new_latent.shape), pltpu.SMEM(page_owner.shape, jnp.int32),
        pltpu.SMEM(page_slot.shape, jnp.int32), pltpu.SMEM(lengths.shape, jnp.int32),
        v((GROUP, W)), v((1, W), F32), v((TOP, GROUP), jnp.int32), v((TOP, GROUP), F32),
        v((LAT, NS * PAGE)), v((NS * PAGE, KVR)), v((128, LAT)), v((ROWS, H, LAT)),
        v((G, ROWS, H, -(-(LAT + 2) // 128) * 128)),
        v((G, 8, 128), F32), v((G, 8, 128), F32), v((N2, N2)), v((N2, N2)),
        v((N2, KVR)), v((N2, KVR)), v((N2, DV)), v((G, RH, DV)), v((G, 1, 128), F32),
        v((G, RH, DV)), v((G, 1, 128), F32),
        v((C, RH, DV)), v((GROUP, H * DV)), v((H, KVR, DV)), v((W, H * DV)),
        v((2, ELOC, W, 2, FH)), v((ELOC, 2, W, FF)), v((2, ELOC, W, FH)),
        v((2, 4, GROUP, W)), v((2, 4, GROUP, W)), v((1, 128), F32), v((C, 1, 128), F32),
        v((1, 128), F32), v((G, 1, 128), F32),
        v((2, ELOC, ESL, HALF)), v((2, HALF, SLOTS)), v((2, ELOC, ESL, 128), F32),
        v((2, 4, SLOTS, QC)), v((2, 2, 6, ESL, QC)), v((2, 2, 2, ESL, QC)), v((2, 2, 2, ESL, QC)),
        v((2, 2, 4, QR, QC)), v((2, 4, SLOTS, QC // 2)), v((2, SLOTS, W)), v((2, SLOTS, W)),
        v((2, HALF, W)), v((2, HALF, W)), v((2, 4, GROUP, W)), v((G, GROUP, W)),
        v((2, HALF, W), F32),
        dma(14), dma(16), dma(12), dma(G), dma(G), dma(C // 2), dma(4), dma(12), dma(4), dma(18),
    ]
    vm = pl.BlockSpec(memory_space=pltpu.VMEM)
    hbm = pl.BlockSpec(memory_space=pl.ANY)
    return pl.pallas_call(
        functools.partial(kernel, G, C, ELOC, capacity),
        out_shape=jax.ShapeDtypeStruct((GROUP, W), BF16),
        in_specs=[hbm] * 14,
        out_specs=vm,
        scratch_shapes=scratch,
        compiler_params=pltpu.CompilerParams(
            collective_id=0, has_side_effects=True, vmem_limit_bytes=56 << 20
        ),
        cost_estimate=pl.CostEstimate(flops=4 << 30, bytes_accessed=16 << 20, transcendentals=1 << 20),
        name="decode_step",
    )(
        queries, new_latent, pool_pages, page_owner, page_slot, lengths, residual, value_weight,
        output_weight.T, norm_gain.reshape(1, W), expert_ids.T, route_gates.T, expert_in,
        jnp.swapaxes(expert_out, 1, 2),
    )


def solution(mesh):
    in_specs = (
        P(("dp", "expert"), None, None),
        P(("dp", "expert"), None),
        P(("dp", "expert"), None, None),
        P(None, "expert", None, None),
        P(None, "expert", None, None),
        P(("dp", "expert")),
        P("dp", "expert"),
        P(),
        P(None, "expert"),
        P("expert"),
        P("dp", None),
        P("dp", None),
        P("dp", "expert", None, None),
        P("dp", None, "expert"),
    )
    return jax.shard_map(
        body, mesh=mesh, in_specs=in_specs, out_specs=P("dp", "expert"), check_vma=False
    )
```

```python
import functools
import jax
import jax.numpy as jnp
from jax import lax
from jax.experimental import pallas as pl
from jax.experimental.pallas import tpu as pltpu
from jax.sharding import PartitionSpec as P

D = 7168
KVR = 512
ROPE = 64
DV = 128
TOP = 8
EPS = 1e-06
MESH = pl.DeviceIdType.MESH
F32 = jnp.float32
BF16 = jnp.bfloat16
NEG = -1e30
WAVES = ((4, -3, 3, -2), (0, 1, -1, 2))
POS = {off: 4 * w + t for w in range(2) for t, off in enumerate(WAVES[w])}
ME = POS[0]
BACK = {off: POS[4 if off == 4 else -off] for off in POS}


def iota(shape, dim):
    return lax.broadcasted_iota(jnp.int32, shape, dim)


def mm(a, b):
    return jnp.dot(a, b, preferred_element_type=F32)


def mm_nt(a, b):
    return lax.dot_general(a, b, (((1,), (1,)), ((), ())), preferred_element_type=F32)


def kernel(
    G, C, ELOC, CAPX,
    q_hbm, nl_hbm, pool_hbm, owner_hbm, slot_hbm, len_hbm, res_hbm, wv_hbm, wo_hbm, gain_hbm,
    ids_hbm, gates_hbm, win_hbm, wout_hbm,
    out_ref,
    nl_ref, owner_ref, slot_ref, len_ref, res_ref, gain_ref, ids_ref, gates_ref,
    kc, vt, nlp, q_in, q_all, sml_s, sml_r, perm, perm_t, o_all, o_hm, hv_hm, hv_s, lse_s, hv_r,
    lse_r, hva, xmat, wv, wo, win, wg, wout, xall, xsib, sq_s, sq_r, inv_s, inv_r,
    sel, sel_g, sel_t, gcol, part, in1, b2, in2, hid, vown, vsib, zsib_s, zsib_r, zs, zr, zown,
    lsem, sent, heard, r_rows, r_q, r_x, r_p1, r_p2, r_hid,
):
    g = lax.axis_index("dp")
    k = lax.axis_index("expert")
    core = lax.rem(k, 2)
    chip = lax.div(k, 2)
    sib = k + 1 - 2 * core
    cx = lax.rem(chip, 4)
    cy = lax.div(chip, 4)
    ROWS, H, LAT = q_in.shape
    NS = pool_hbm.shape[0]
    PAGE = pool_hbm.shape[2]
    RH = ROWS * H
    GROUP = C * ROWS
    W = res_ref.shape[1]
    FF = win_hbm.shape[3]
    FH = FF // 2
    ESL = 4 * CAPX
    QR = ESL // 2
    QF = FH // 4
    NR = G * ROWS

    def dp_peer(d):
        half = lax.div(G + 1 - d, 2)
        off = half * (1 - 2 * lax.rem(G + 1 - d, 2))
        return lax.rem(g + off + G, G)

    def at_dp(off):
        return lax.rem(g + off + G, G)

    def ex_peer(d):
        return lax.rem(k + d, C)

    def at_chip(ox, oy):
        x = lax.rem(cx + ox + 4, 4)
        y = lax.rem(cy + oy + 4, 4)
        return x, y, (g, 2 * (4 * y + x) + core)

    s_q, s_sml, s_hv, s_lse, s_hva, s_x, s_fw, s_sq = (sent.at[i] for i in range(8))
    s_inv, s_p1, s_p2, s_hid, s_win, s_wout, s_zsib, s_z = (sent.at[8 + i] for i in range(8))
    r_sml, r_lse, r_inv, r_z, r_sq, r_win, r_wout = (heard.at[i] for i in range(7))
    r_fwd, r_zsib = (heard.at[8], heard.at[9]), (heard.at[10], heard.at[11])

    def rcopy(src, dst, ss, rs, dev):
        return pltpu.make_async_remote_copy(
            src_ref=src, dst_ref=dst, send_sem=ss, recv_sem=rs, device_id=dev, device_id_type=MESH
        )

    def sent_all(ref, sem):
        rcopy(ref, ref, sem, sem, exp_dev(sib)).wait_send()

    def heard_all(ref, sem):
        rcopy(ref, ref, sem, sem, exp_dev(sib)).wait_recv()

    def loop(lo, hi, fn):
        lax.fori_loop(lo, hi, lambda i, c: (fn(i), c)[1], 0)

    def exp_dev(kk):
        return (g, kk)

    def dp_dev(j):
        return (j, k)

    locals_ = []
    for s in range(NS):
        locals_.append(
            pltpu.make_async_copy(pool_hbm.at[s], kc.at[:, pl.ds(s * PAGE, PAGE)], lsem.at[0])
        )
    c_q = pltpu.make_async_copy(q_hbm, q_in, lsem.at[1])
    c_win = pltpu.make_async_copy(
        win_hbm.at[:, :, :, pl.ds(pl.multiple_of(core * FH, FH), FH)], win.at[0], lsem.at[2]
    )
    c_wv = pltpu.make_async_copy(wv_hbm, wv, lsem.at[3])
    c_wo = pltpu.make_async_copy(wo_hbm, wo, lsem.at[4])
    c_wout = pltpu.make_async_copy(
        wout_hbm.at[:, :, pl.ds(pl.multiple_of(core * FH, FH), FH)], wout.at[0], lsem.at[5]
    )
    c_q.start()
    small = []
    for i, (a, b) in enumerate(
        (
            (ids_hbm, ids_ref), (gates_hbm, gates_ref), (len_hbm, len_ref), (nl_hbm, nl_ref),
            (owner_hbm, owner_ref), (slot_hbm, slot_ref), (res_hbm, res_ref), (gain_hbm, gain_ref),
        )
    ):
        small.append(pltpu.make_async_copy(a, b, lsem.at[6 + i]))
        small[-1].start()
    for c in locals_:
        c.start()
    for c in (c_win, c_wv, c_wo, c_wout):
        c.start()

    barrier = pltpu.get_barrier_semaphore()

    def sig_dp(d):
        pl.semaphore_signal(barrier, inc=1, device_id=dp_dev(lax.rem(g + d, G)), device_id_type=MESH)

    def sig_ex(d):
        pl.semaphore_signal(barrier, inc=1, device_id=exp_dev(ex_peer(d)), device_id_type=MESH)

    loop(1, G, sig_dp)
    loop(1, C, sig_ex)

    c_q.wait()
    small[2].wait()
    for r in range(ROWS):
        n = len_ref[r]
        li = iota((H, q_all.shape[3] - LAT), 1)
        tail = jnp.where(li == 0, lax.div(n, 32), jnp.where(li == 1, lax.rem(n, 32), 0))
        q_all[g, r] = jnp.concatenate([q_in[r], tail.astype(F32).astype(BF16)], axis=1)
    pl.semaphore_wait(barrier, G - 1 + C - 1)

    def q_copy(src, off, row=None):
        ref = q_all.at[src] if row is None else q_all.at[src, row]
        return rcopy(ref, ref, s_q, r_q.at[src], dp_dev(at_dp(off)))

    for off in (2, -2, 1, -1):
        q_copy(g, off).start()

    for i, c in enumerate(small):
        if i != 2:
            c.wait()
    ids = ids_ref[...]
    gates = gates_ref[...]
    e_iota = iota((G * ELOC, GROUP), 0)
    named = jnp.zeros((G * ELOC, GROUP), F32)
    gval = jnp.zeros((G * ELOC, GROUP), F32)
    for t in range(TOP):
        hit = ids[t : t + 1, :] == e_iota
        named = named + hit.astype(F32)
        gval = gval + jnp.where(hit, gates[t : t + 1, :], 0.0)
    tri = (iota((GROUP, GROUP), 0) < iota((GROUP, GROUP), 1)).astype(BF16)
    rank = mm(named.astype(BF16), tri)
    code = jnp.where(named > 0, rank, -1.0)
    sml_s[...] = jnp.zeros_like(sml_s)
    for j in range(G):
        sml_s[j, 0:ELOC, 0:GROUP] = code[j * ELOC : (j + 1) * ELOC]
        sml_s[j, ELOC : 2 * ELOC, 0:GROUP] = gval[j * ELOC : (j + 1) * ELOC]
    sml_r[ME] = sml_s[g]

    N2 = NR * H
    pr = iota((N2, 1), 0)
    perm[...] = (iota((N2, N2), 1) == lax.rem(pr, NR) * H + lax.div(pr, NR)).astype(BF16)
    perm_t[...] = (iota((N2, N2), 1) == lax.rem(pr, H) * NR + lax.div(pr, H)).astype(BF16)
    rr = iota((GROUP, GROUP), 0)
    rc = iota((GROUP, GROUP), 1)
    to_split = (rc == lax.rem(rr, C) * ROWS + lax.div(rr, C)).astype(BF16)
    from_split = (rr == lax.rem(rc, C) * ROWS + lax.div(rc, C)).astype(BF16)
    nl = nl_ref[...].astype(F32)
    nrow = iota((128, LAT), 0)
    nacc = jnp.zeros((128, LAT), F32)
    for s in range(ROWS):
        nacc = jnp.where(nrow == s, nl[s : s + 1, :], nacc)
    nlp[...] = nacc.astype(BF16)

    other = pl.multiple_of((1 - core) * FH, FH)
    w1 = rcopy(win_hbm.at[:, :, :, pl.ds(other, FH)], win.at[1], s_win, r_win, exp_dev(sib))
    w2 = rcopy(wout_hbm.at[:, :, pl.ds(other, FH)], wout.at[1], s_wout, r_wout, exp_dev(sib))
    w1.start()
    w2.start()

    pltpu.make_async_copy(kc, kc, lsem.at[0]).wait()
    vt[...] = kc[0:KVR, :].T

    scale = (DV + ROPE) ** (-0.5)
    NT = NS * PAGE

    def attend(src, own):
        qx = q_all[src].reshape(RH, q_all.shape[3])
        q = qx[:, 0:LAT]
        sc = mm(q, kc[...]) * scale
        lid = iota((1, NT), 1)
        slot_lane = lax.div(lid, PAGE)
        tpos = lax.rem(lid, PAGE).astype(F32)
        rows = []
        for s in range(ROWS):
            lv = qx[s * H : s * H + 8, LAT : LAT + 2].astype(F32)
            ln = lv[0:1, 0:1] * 32.0 + lv[0:1, 1:2]
            cnt = jnp.zeros((1, NT), F32)
            for p in range(owner_ref.shape[3]):
                here = jnp.where(owner_ref[src, 0, s, p] == g, slot_ref[src, 0, s, p], -1)
                ok = jnp.logical_and(slot_lane == here, tpos + float(p * PAGE) < ln)
                cnt = cnt + ok.astype(F32)
            rows.append(jnp.broadcast_to(cnt, (H, NT)))
        cnt = jnp.concatenate(rows, axis=0)
        scm = jnp.where(cnt > 0, sc, NEG)
        top = jnp.max(scm, axis=1, keepdims=True)
        if own:
            cs = (iota((RH, 128), 1) == lax.div(iota((RH, 128), 0), H)).astype(F32)
            ss = jnp.where(cs > 0, mm_nt(q, nlp[...]) * scale, NEG)
            top = jnp.maximum(top, jnp.max(ss, axis=1, keepdims=True))
        p = cnt * jnp.exp(scm - top)
        den = jnp.sum(p, axis=1, keepdims=True)
        acc = mm(p.astype(BF16), vt[...])
        if own:
            pself = cs * jnp.exp(ss - top)
            den = den + jnp.sum(pself, axis=1, keepdims=True)
            acc = acc + mm(pself.astype(BF16), nlp[:, 0:KVR])
        has = den > 0
        inv_den = jnp.where(has, 1.0 / jnp.where(has, den, 1.0), 0.0)
        lse = jnp.where(has, top + jnp.log(jnp.where(has, den, 1.0)), NEG)
        o_all[pl.ds(pl.multiple_of(src * RH, RH), RH), :] = (acc * inv_den).astype(BF16)
        row = jnp.broadcast_to(lse, (RH, 128)).T[0:1]
        lse_s[src] = jnp.concatenate([row, row], axis=1)

    attend(g, True)

    col = iota((W, 2 * W), 1)
    two = 2 * iota((W, 2 * W), 0)
    pick_g = (col == two).astype(BF16)
    pick_u = (col == two + 1).astype(BF16)

    def split(o, e):
        w = win[o, e].reshape(2 * W, FH)
        wgate = mm(pick_g, w).astype(BF16)
        wup = mm(pick_u, w).astype(BF16)
        for f in range(4):
            wg[e, o, :, 2 * f * QF : (2 * f + 1) * QF] = wgate[:, f * QF : (f + 1) * QF]
            wg[e, o, :, (2 * f + 1) * QF : 2 * (f + 1) * QF] = wup[:, f * QF : (f + 1) * QF]

    c_win.wait()
    loop(0, ELOC, lambda e: split(0, e))

    for i, off in ((0, -2), (1, 2)):
        src = at_dp(off)
        q_copy(src, off).wait_recv()
        q_copy(src, 1 - 2 * i).start()
        q_copy(src, 2 - 4 * i, row=i).start()

    def sml_copy(off, n):
        j = at_dp(off)
        return rcopy(sml_s.at[j], sml_r.at[n], s_sml, r_sml, dp_dev(j))

    others = [4, -3, 3, -2, 2, -1, 1]
    for off in others:
        sml_copy(off, BACK[off]).start()

    def ring(d):
        n = lax.div(d, 2)
        m = jnp.where(n == 0, 2, jnp.where(n == 1, 1, n + 1))
        return at_dp(jnp.where(lax.rem(d, 2) == 0, -m, m))

    def near(d):
        attend(ring(d), False)

    def chunk(d):
        src = ring(d)
        heard_all(q_all.at[src], r_q.at[src])
        attend(src, False)

    loop(0, 2, near)
    loop(2, G - 2, chunk)
    far = at_dp(G // 2)
    heard_all(q_all.at[far], r_q.at[far])
    attend(far, False)

    o_hm[...] = mm(perm[...], o_all[...]).astype(BF16)
    c_wv.wait()
    HB = 16

    def project(b):
        for i in range(HB):
            h = b * HB + i
            at = pl.ds(pl.multiple_of(h * NR, NR), NR)
            hv_hm[at, :] = mm(o_hm[at, :], wv[h]).astype(BF16)

    loop(0, H // HB, project)
    hv_s[...] = mm(perm_t[...], hv_hm[...]).astype(BF16).reshape(G, RH, DV)
    hv_r[g] = hv_s[g]
    lse_r[g] = lse_s[g]

    def part_of(r):
        return pl.ds(r * H, H)

    def send_hv(r, d):
        j = dp_peer(d)
        if r == 0:
            rcopy(lse_s.at[j], lse_r.at[g], s_lse, r_lse, dp_dev(j)).start()
        rcopy(
            hv_s.at[j, part_of(r)], hv_r.at[g, part_of(r)], s_hv, r_rows.at[r], dp_dev(j)
        ).start()

    for r in range(ROWS):
        loop(1, G, functools.partial(send_hv, r))

    heard_all(win.at[1], r_win)
    loop(0, ELOC, lambda e: split(1, e))
    heard_all(sml_r.at[pl.ds(0, G - 1)], r_sml)
    siota = iota((ESL, 4 * GROUP), 0).astype(F32)
    codes_in = sml_r[:, :, 0:GROUP].reshape(8 * G, GROUP).astype(BF16)
    split_codes = mm(codes_in, from_split)

    def slots(rows, w, e):
        return jnp.concatenate(
            [jnp.where(c >= 0, c + float(t * CAPX), -1.0) for t, c in enumerate(rows)], axis=1
        )

    for w in range(2):
        for e in range(ELOC):
            ns = [4 * w + t for t in range(4)]
            given = siota == slots([sml_r[n, e : e + 1, 0:GROUP] for n in ns], w, e)
            halved = siota == slots([split_codes[8 * n + e : 8 * n + e + 1] for n in ns], w, e)
            sel[w, e] = halved.astype(F32).astype(BF16)
            sel_g[w, e] = given.astype(F32).astype(BF16)
            gvals = [sml_r[n, ELOC + e : ELOC + e + 1, 0:GROUP] for n in ns]
            gs = jnp.where(given, jnp.concatenate(gvals, axis=1), 0.0)
            gcol[w, e] = jnp.broadcast_to(jnp.sum(gs, axis=1, keepdims=True), (ESL, 128))
        sel_t[w] = sel_g[w].reshape(ELOC * ESL, 4 * GROUP).T
    res_split = mm(to_split, res_ref[...])

    heard_all(lse_r.at[pl.ds(0, G - 1)], r_lse)
    riota = iota((8, 128), 0)
    ls = jnp.full((8, 128), NEG, F32)
    for j in range(G):
        ls = jnp.where(riota == j, lse_r[j], ls)
    wts = jnp.exp(ls - jnp.max(ls, axis=0, keepdims=True))
    wts = wts / jnp.sum(wts, axis=0, keepdims=True)
    wcol = wts.T
    plane = [(2, 2), (2, 1), (2, -1), (1, 2), (-1, 2), (2, 0), (0, 2)]
    plane += [(1, 1), (1, -1), (-1, 1), (-1, -1), (1, 0), (-1, 0), (0, 1), (0, -1)]

    for r in range(ROWS):
        heard_all(hv_r.at[pl.ds(0, G - 1), part_of(0)], r_rows.at[r])
        comb = jnp.zeros((H, DV), F32)
        for j in range(G):
            at = slice(r * H, (r + 1) * H)
            comb = comb + wcol[at, j : j + 1] * hv_r[j, at].astype(F32)
        hva[r, k] = comb.astype(BF16)
        for ox, oy in plane:
            x, y, dev = at_chip(ox, oy)
            for kk in (2 * (4 * y + x) + core, 2 * (4 * y + x) + 1 - core):
                rcopy(hva.at[r, k], hva.at[r, k], s_hva, r_rows.at[ROWS + r], exp_dev(kk)).start()
        rcopy(hva.at[r, k], hva.at[r, k], s_hva, r_rows.at[ROWS + r], exp_dev(sib)).start()
    c_wo.wait()

    def half(r):
        return pl.ds(r * C, C)

    def x_copy(off, n, r):
        ref = xall.at[n // 4, n % 4, half(r)]
        return rcopy(xall.at[1, 0, half(r)], ref, s_x, r_x.at[n], dp_dev(at_dp(off)))

    def fwd(n):
        src, dst = xall.at[n // 4, n % 4], xsib.at[n // 4, n % 4]
        return rcopy(src, dst, s_fw, r_fwd[n // 4], exp_dev(sib))

    resids = []
    for r in range(ROWS):
        heard_all(hva.at[r, pl.ds(0, C - 1)], r_rows.at[ROWS + r])
        for b in range(C // NR):
            blk = mm(perm[...], hva[r, b * NR : (b + 1) * NR].reshape(N2, DV)).astype(BF16)
            for h in range(H):
                xmat[r, b * NR : (b + 1) * NR, h * DV : (h + 1) * DV] = blk[h * NR : (h + 1) * NR]
        proj = mm_nt(xmat[r], wo[...])
        resids.append((res_split[r * C : (r + 1) * C] + proj).astype(BF16).astype(F32))
        xall[1, 0, r * C : (r + 1) * C] = (resids[r] * gain_ref[...]).astype(BF16)
        for off in others:
            x_copy(off, BACK[off], r).start()
    fwd(ME).start()
    resid = jnp.concatenate(resids, axis=0)
    sq = jnp.sum(resid * resid, axis=1, keepdims=True)
    sq_row = jnp.broadcast_to(sq, (GROUP, 128)).T[0:1]
    sq_s[...] = jnp.concatenate([sq_row] * (128 // GROUP), axis=1)
    sq_r[k] = sq_s[...]

    def send_sq(d):
        j = ex_peer(d)
        rcopy(sq_s, sq_r.at[k], s_sq, r_sq, exp_dev(j)).start()

    loop(1, C, send_sq)

    def get_x(w):
        for off in sorted(WAVES[w], key=abs):
            if off != 0:
                n = POS[off]
                heard_all(xall.at[n // 4, n % 4], r_x.at[n])
                fwd(n).start()
        heard_all(xsib.at[w], r_fwd[w])

    place = (cx, cy)

    def along(h, off):
        return at_chip(off, 0)[2] if h == 0 else at_chip(0, off)[2]

    def across(h, off):
        return at_chip(0, off)[2] if h == 0 else at_chip(off, 0)[2]

    def ring1(w, h, role, e):
        ref = part.at[w, pl.ds(2 * h, 2), block(e)]
        dst = in1.at[w, h, role - 1]
        return rcopy(ref, dst, s_p1, r_p1.at[2 * w + h], along(h, role))

    def block(e):
        return pl.ds(pl.multiple_of(e * ESL, 16), ESL)

    def partials(w):
        def step(i):
            e = lax.rem(cx + 2 + 3 * i, 4)
            xo = mm(sel[w, e], xall[w].reshape(4 * GROUP, W)).astype(BF16)
            xs = mm(sel[w, e], xsib[w].reshape(4 * GROUP, W)).astype(BF16)
            for f in range(4):
                cols = slice(2 * f * QF, 2 * (f + 1) * QF)
                both = mm(xo, wg[e, 0, :, cols]) + mm(xs, wg[e, 1, :, cols])
                part[w, f, block(e)] = both.astype(BF16)
            for h in range(2):
                role = lax.rem(e - place[h] + 4, 4)

                @pl.when(role > 0)
                def _():
                    ring1(w, h, role, e).start()

        loop(0, 4, step)

    def rows2(p):
        return pl.ds(pl.multiple_of(lax.div(p, 2) * QR, 16), QR)

    def ring2(w, h, off):
        to = lax.rem(place[1 - h] + off, 4)
        src = b2.at[w, h, lax.rem(to, 2), rows2(to)]
        return rcopy(src, in2.at[w, h, 4 - off], s_p2, r_p2.at[2 * w + h], across(h, off))

    def second(w):
        for h in range(2):
            heard_all(in1.at[w, h], r_p1.at[2 * w + h])
            for i in range(2):
                tot = part[w, 2 * h + i, block(place[h])].astype(F32)
                for j in range(3):
                    tot = tot + in1[w, h, j, i].astype(F32)
                b2[w, h, i] = tot.astype(BF16)
            for off in (2, 1, 3):
                ring2(w, h, off).start()
            p = place[1 - h]
            in2[w, h, 0] = b2[w, h, lax.rem(p, 2), rows2(p)]

    def piece(w, h, x, y):
        p = (x, y)
        at = p[h] * ESL + lax.div(p[1 - h], 2) * QR
        return w, 2 * h + lax.rem(p[1 - h], 2), pl.ds(pl.multiple_of(at, 16), QR)

    def hid_copy(w, h, dev):
        ref = hid.at[piece(w, h, cx, cy)]
        return rcopy(ref, ref, s_hid, r_hid.at[w], dev)

    def hidden(w):
        irow = jnp.concatenate([inv_r[4 * w + t, 0:1, 0:GROUP] for t in range(4)], axis=1)
        for h in range(2):
            mine = sel[w, place[h], rows2(place[1 - h]), :]
            icol = jnp.sum(mine.astype(F32) * irow, axis=1, keepdims=True)
            heard_all(in2.at[w, h, pl.ds(1, 3)], r_p2.at[2 * w + h])
            tot = in2[w, h, 0].astype(F32)
            for j in range(1, 4):
                tot = tot + in2[w, h, j].astype(F32)
            tot = tot * icol
            ga = tot[:, 0:QF]
            hv = ga / (1.0 + jnp.exp(-ga)) * tot[:, QF : 2 * QF]
            hid[piece(w, h, cx, cy)] = hv.astype(BF16)
            for ox, oy in plane:
                hid_copy(w, h, at_chip(ox, oy)[2]).start()

    def down(w):
        heard_all(wv.at[pl.ds(0, 30), pl.ds(0, QR)], r_hid.at[w])

        def step(e):
            at = block(e)
            he = jnp.concatenate([hid[w, f, at] for f in range(4)], axis=1)
            gs = gcol[w, e, :, 0:1]
            vsib[w, at, :] = (mm_nt(he, wout[1, e]) * gs).astype(BF16)
            vown[w, at, :] = (mm_nt(he, wout[0, e]) * gs).astype(BF16)

        loop(0, ELOC, step)
        zsib_s[w] = mm(sel_t[w], vsib[w]).astype(BF16)
        zsib_copy(w).start()
        zown[w] = mm(sel_t[w], vown[w])

    def zsib_copy(w):
        return rcopy(zsib_s.at[w], zsib_r.at[w], s_zsib, r_zsib[w], exp_dev(sib))

    def z_copy(off, n):
        ref = zs.at[POS[off] // 4, POS[off] % 4]
        return rcopy(ref, zr.at[n], s_z, r_z, dp_dev(at_dp(off)))

    def give_back(w):
        zsib_copy(w).wait_recv()
        zsum = zown[w] + zsib_r[w].astype(F32)
        zown[w] = zsum
        zs[w] = zsum.astype(BF16).reshape(4, GROUP, W)
        for off in sorted(WAVES[w], key=lambda o: -abs(o)):
            if off != 0:
                z_copy(off, BACK[off]).start()

    get_x(0)
    partials(0)

    heard_all(sq_r.at[pl.ds(0, C - 1)], r_sq)
    inv_s[...] = lax.rsqrt(jnp.sum(sq_r[...], axis=0) / D + EPS)
    inv_r[ME] = inv_s[...]

    def inv_copy(off, n):
        return rcopy(inv_s, inv_r.at[n], s_inv, r_inv, dp_dev(at_dp(off)))

    for off in others:
        inv_copy(off, BACK[off]).start()
    get_x(1)
    partials(1)
    second(0)
    second(1)
    heard_all(inv_r.at[pl.ds(0, G - 1)], r_inv)
    hidden(0)
    hidden(1)
    c_wout.wait()
    heard_all(wout.at[1], r_wout)
    down(0)
    give_back(0)
    down(1)
    give_back(1)
    total = mm(from_split, resid.astype(BF16)) + zown[1, 0:GROUP, :]

    w1.wait_send()
    w2.wait_send()
    seven = pl.ds(0, G - 1)
    sent_all(q_all.at[seven], s_q)
    sent_all(sml_r.at[seven], s_sml)
    sent_all(hv_r.at[seven], s_hv)
    sent_all(lse_r.at[seven], s_lse)
    sent_all(hva.at[:, pl.ds(0, C - 1)], s_hva)
    sent_all(zr.at[seven], s_x)
    sent_all(zr, s_fw)
    sent_all(sq_r.at[pl.ds(0, C - 1)], s_sq)
    sent_all(inv_r.at[seven], s_inv)
    sent_all(in1, s_p1)
    sent_all(in2.at[:, :, pl.ds(0, 3)], s_p2)
    sent_all(wv.at[pl.ds(0, 30), pl.ds(0, 2 * QR)], s_hid)
    sent_all(zsib_r, s_zsib)

    heard_all(zr.at[seven], r_z)
    for off in others:
        total = total + zr[POS[off]].astype(F32)
    out_ref[...] = total.astype(BF16)
    sent_all(zr.at[seven], s_z)


def body(
    queries, new_latent, pool_pages, page_owner, page_slot, lengths, residual, value_weight,
    output_weight, norm_gain, expert_ids, route_gates, expert_in, expert_out,
):
    G = lax.axis_size("dp")
    C = lax.axis_size("expert")
    ROWS, H, LAT = queries.shape
    NS, _, PAGE = pool_pages.shape
    GROUP, W = residual.shape
    ELOC, _, _, FF = expert_in.shape
    FH = FF // 2
    RH = ROWS * H
    capacity = min(GROUP, (3 * GROUP * TOP + 2 * G * ELOC - 1) // (2 * G * ELOC))
    ESL = 4 * capacity
    SLOTS = ELOC * ESL
    QR, QC = ESL // 2, FF // 4
    N2 = G * RH
    HALF = 4 * GROUP

    def v(shape, dtype=BF16):
        return pltpu.VMEM(shape, dtype)

    dma = lambda n: pltpu.SemaphoreType.DMA((n,))
    scratch = [
        v(new_latent.shape), pltpu.SMEM(page_owner.shape, jnp.int32),
        pltpu.SMEM(page_slot.shape, jnp.int32), pltpu.SMEM(lengths.shape, jnp.int32),
        v((GROUP, W)), v((1, W), F32), v((TOP, GROUP), jnp.int32), v((TOP, GROUP), F32),
        v((LAT, NS * PAGE)), v((NS * PAGE, KVR)), v((128, LAT)), v((ROWS, H, LAT)),
        v((G, ROWS, H, -(-(LAT + 2) // 128) * 128)),
        v((G, 8, 128), F32), v((G, 8, 128), F32), v((N2, N2)), v((N2, N2)),
        v((N2, KVR)), v((N2, KVR)), v((N2, DV)), v((G, RH, DV)), v((G, 1, 128), F32),
        v((G, RH, DV)), v((G, 1, 128), F32),
        v((ROWS, C, H, DV)), v((ROWS, C, H * DV)), v((H, KVR, DV)), v((W, H * DV)),
        v((2, ELOC, W, 2, FH)), v((ELOC, 2, W, FF)), v((2, ELOC, W, FH)),
        v((2, 4, GROUP, W)), v((2, 4, GROUP, W)), v((1, 128), F32), v((C, 1, 128), F32),
        v((1, 128), F32), v((G, 1, 128), F32),
        v((2, ELOC, ESL, HALF)), v((2, ELOC, ESL, HALF)), v((2, HALF, SLOTS)), v((2, ELOC, ESL, 128), F32),
        v((2, 4, SLOTS, QC)), v((2, 2, 3, 2, ESL, QC)), v((2, 2, 2, ESL, QC)),
        v((2, 2, 4, QR, QC)), v((2, 4, SLOTS, QC // 2)), v((2, SLOTS, W)), v((2, SLOTS, W)),
        v((2, HALF, W)), v((2, HALF, W)), v((2, 4, GROUP, W)), v((G, GROUP, W)),
        v((2, HALF, W), F32),
        dma(14), dma(16), dma(12), dma(2 * ROWS), dma(G), dma(G), dma(4), dma(4), dma(2),
    ]
    vm = pl.BlockSpec(memory_space=pltpu.VMEM)
    hbm = pl.BlockSpec(memory_space=pl.ANY)
    return pl.pallas_call(
        functools.partial(kernel, G, C, ELOC, capacity),
        out_shape=jax.ShapeDtypeStruct((GROUP, W), BF16),
        in_specs=[hbm] * 14,
        out_specs=vm,
        scratch_shapes=scratch,
        compiler_params=pltpu.CompilerParams(
            collective_id=0, has_side_effects=True, vmem_limit_bytes=56 << 20
        ),
        cost_estimate=pl.CostEstimate(flops=4 << 30, bytes_accessed=16 << 20, transcendentals=1 << 20),
        name="decode_step",
    )(
        queries, new_latent, pool_pages, page_owner, page_slot, lengths, residual, value_weight,
        output_weight.T, norm_gain.reshape(1, W), expert_ids.T, route_gates.T, expert_in,
        jnp.swapaxes(expert_out, 1, 2),
    )


def solution(mesh):
    in_specs = (
        P(("dp", "expert"), None, None),
        P(("dp", "expert"), None),
        P(("dp", "expert"), None, None),
        P(None, "expert", None, None),
        P(None, "expert", None, None),
        P(("dp", "expert")),
        P("dp", "expert"),
        P(),
        P(None, "expert"),
        P("expert"),
        P("dp", None),
        P("dp", None),
        P("dp", "expert", None, None),
        P("dp", None, "expert"),
    )
    return jax.shard_map(
        body, mesh=mesh, in_specs=in_specs, out_specs=P("dp", "expert"), check_vma=False
    )
```

```python
import functools
import jax
import jax.numpy as jnp
from jax import lax
from jax.experimental import pallas as pl
from jax.experimental.pallas import tpu as pltpu
from jax.sharding import PartitionSpec as P

D = 7168
KVR = 512
ROPE = 64
DV = 128
TOP = 8
EPS = 1e-06
MESH = pl.DeviceIdType.MESH
F32 = jnp.float32
BF16 = jnp.bfloat16
NEG = -1e30
WAVES = ((4, -3, 3, -2), (0, 1, -1, 2))
POS = {off: 4 * w + t for w in range(2) for t, off in enumerate(WAVES[w])}
ME = POS[0]
BACK = {off: POS[4 if off == 4 else -off] for off in POS}


def iota(shape, dim):
    return lax.broadcasted_iota(jnp.int32, shape, dim)


def mm(a, b):
    return jnp.dot(a, b, preferred_element_type=F32)


def mm_nt(a, b):
    return lax.dot_general(a, b, (((1,), (1,)), ((), ())), preferred_element_type=F32)


def kernel(
    G, C, ELOC, CAPX,
    q_hbm, nl_hbm, pool_hbm, owner_hbm, slot_hbm, len_hbm, res_hbm, wv_hbm, wo_hbm, gain_hbm,
    ids_hbm, gates_hbm, win_hbm, wout_hbm,
    out_ref,
    nl_ref, owner_ref, slot_ref, len_ref, res_ref, gain_ref, ids_ref, gates_ref,
    kc, vt, nlp, q_in, q_all, sml_s, sml_r, perm, perm_t, o_all, o_hm, hv_hm, hv_s, lse_s, hv_r,
    lse_r, hva, xmat, wv, wo, wot, win, wg, wout, woutt, xall, xsib, sq_s, sq_r, inv_s, inv_r,
    sel, sel_g, sel_t, gcol, part, in1, out1, b2, in2, hid, vown, vsib, zsib_s, zsib_r, zs, zr, zown,
    lsem, sent, heard, r_rows, r_q, r_x, r_p1, r_p2, r_hid,
):
    g = lax.axis_index("dp")
    k = lax.axis_index("expert")
    core = lax.rem(k, 2)
    chip = lax.div(k, 2)
    sib = k + 1 - 2 * core
    cx = lax.rem(chip, 4)
    cy = lax.div(chip, 4)
    ROWS, H, LAT = q_in.shape
    NS = pool_hbm.shape[0]
    PAGE = pool_hbm.shape[2]
    RH = ROWS * H
    GROUP = C * ROWS
    W = res_ref.shape[1]
    FF = win_hbm.shape[3]
    FH = FF // 2
    ESL = 4 * CAPX
    QR = ESL // 2
    QF = FH // 4
    NR = G * ROWS

    def dp_peer(d):
        half = lax.div(G + 1 - d, 2)
        off = half * (1 - 2 * lax.rem(G + 1 - d, 2))
        return lax.rem(g + off + G, G)

    def at_dp(off):
        return lax.rem(g + off + G, G)

    def ex_peer(d):
        return lax.rem(k + d, C)

    def at_chip(ox, oy):
        x = lax.rem(cx + ox + 4, 4)
        y = lax.rem(cy + oy + 4, 4)
        return x, y, (g, 2 * (4 * y + x) + core)

    s_q, s_sml, s_hv, s_lse, s_hva, s_x, s_fw, s_sq = (sent.at[i] for i in range(8))
    s_inv, s_p1, s_p2, s_hid, s_win, s_wout, s_zsib, s_z = (sent.at[8 + i] for i in range(8))
    r_sml, r_lse, r_inv, r_z, r_sq, r_win, r_wout = (heard.at[i] for i in range(7))
    r_fwd, r_zsib = (heard.at[8], heard.at[9]), (heard.at[10], heard.at[11])

    def rcopy(src, dst, ss, rs, dev):
        return pltpu.make_async_remote_copy(
            src_ref=src, dst_ref=dst, send_sem=ss, recv_sem=rs, device_id=dev, device_id_type=MESH
        )

    def sent_all(ref, sem):
        rcopy(ref, ref, sem, sem, exp_dev(sib)).wait_send()

    def heard_all(ref, sem):
        rcopy(ref, ref, sem, sem, exp_dev(sib)).wait_recv()

    def loop(lo, hi, fn):
        lax.fori_loop(lo, hi, lambda i, c: (fn(i), c)[1], 0)

    def exp_dev(kk):
        return (g, kk)

    def dp_dev(j):
        return (j, k)

    locals_ = []
    for s in range(NS):
        locals_.append(
            pltpu.make_async_copy(pool_hbm.at[s], kc.at[:, pl.ds(s * PAGE, PAGE)], lsem.at[0])
        )
    c_q = pltpu.make_async_copy(q_hbm, q_in, lsem.at[1])
    c_win = pltpu.make_async_copy(
        win_hbm.at[:, :, :, pl.ds(pl.multiple_of(core * FH, FH), FH)], win.at[0], lsem.at[2]
    )
    c_wv = pltpu.make_async_copy(wv_hbm, wv, lsem.at[3])
    c_wo = pltpu.make_async_copy(wo_hbm, wo, lsem.at[4])
    c_wout = pltpu.make_async_copy(
        wout_hbm.at[:, :, pl.ds(pl.multiple_of(core * FH, FH), FH)], wout.at[0], lsem.at[5]
    )
    c_q.start()
    small = []
    for i, (a, b) in enumerate(
        (
            (ids_hbm, ids_ref), (gates_hbm, gates_ref), (len_hbm, len_ref), (nl_hbm, nl_ref),
            (owner_hbm, owner_ref), (slot_hbm, slot_ref), (res_hbm, res_ref), (gain_hbm, gain_ref),
        )
    ):
        small.append(pltpu.make_async_copy(a, b, lsem.at[6 + i]))
        small[-1].start()
    for c in locals_:
        c.start()
    for c in (c_win, c_wv, c_wo, c_wout):
        c.start()

    barrier = pltpu.get_barrier_semaphore()

    def sig_dp(d):
        pl.semaphore_signal(barrier, inc=1, device_id=dp_dev(lax.rem(g + d, G)), device_id_type=MESH)

    def sig_ex(d):
        pl.semaphore_signal(barrier, inc=1, device_id=exp_dev(ex_peer(d)), device_id_type=MESH)

    loop(1, G, sig_dp)
    loop(1, C, sig_ex)

    c_q.wait()
    small[2].wait()
    for r in range(ROWS):
        n = len_ref[r]
        li = iota((H, q_all.shape[3] - LAT), 1)
        tail = jnp.where(li == 0, lax.div(n, 32), jnp.where(li == 1, lax.rem(n, 32), 0))
        q_all[g, r] = jnp.concatenate([q_in[r], tail.astype(F32).astype(BF16)], axis=1)
    pl.semaphore_wait(barrier, G - 1 + C - 1)

    def q_copy(src, off, row=None):
        ref = q_all.at[src] if row is None else q_all.at[src, row]
        return rcopy(ref, ref, s_q, r_q.at[src], dp_dev(at_dp(off)))

    for off in (2, -2, 1, -1):
        q_copy(g, off).start()

    for i, c in enumerate(small):
        if i != 2:
            c.wait()
    ids = ids_ref[...]
    gates = gates_ref[...]
    e_iota = iota((G * ELOC, GROUP), 0)
    named = jnp.zeros((G * ELOC, GROUP), F32)
    gval = jnp.zeros((G * ELOC, GROUP), F32)
    for t in range(TOP):
        hit = ids[t : t + 1, :] == e_iota
        named = named + hit.astype(F32)
        gval = gval + jnp.where(hit, gates[t : t + 1, :], 0.0)
    tri = (iota((GROUP, GROUP), 0) < iota((GROUP, GROUP), 1)).astype(BF16)
    rank = mm(named.astype(BF16), tri)
    code = jnp.where(named > 0, rank, -1.0)
    sml_s[...] = jnp.zeros_like(sml_s)
    for j in range(G):
        sml_s[j, 0:ELOC, 0:GROUP] = code[j * ELOC : (j + 1) * ELOC]
        sml_s[j, ELOC : 2 * ELOC, 0:GROUP] = gval[j * ELOC : (j + 1) * ELOC]
    sml_r[ME] = sml_s[g]

    N2 = NR * H
    pr = iota((N2, 1), 0)
    perm[...] = (iota((N2, N2), 1) == lax.rem(pr, NR) * H + lax.div(pr, NR)).astype(BF16)
    perm_t[...] = (iota((N2, N2), 1) == lax.rem(pr, H) * NR + lax.div(pr, H)).astype(BF16)
    rr = iota((GROUP, GROUP), 0)
    rc = iota((GROUP, GROUP), 1)
    to_split = (rc == lax.rem(rr, C) * ROWS + lax.div(rr, C)).astype(BF16)
    from_split = (rr == lax.rem(rc, C) * ROWS + lax.div(rc, C)).astype(BF16)
    nl = nl_ref[...].astype(F32)
    nrow = iota((128, LAT), 0)
    nacc = jnp.zeros((128, LAT), F32)
    for s in range(ROWS):
        nacc = jnp.where(nrow == s, nl[s : s + 1, :], nacc)
    nlp[...] = nacc.astype(BF16)

    other = pl.multiple_of((1 - core) * FH, FH)
    w1 = rcopy(win_hbm.at[:, :, :, pl.ds(other, FH)], win.at[1], s_win, r_win, exp_dev(sib))
    w2 = rcopy(wout_hbm.at[:, :, pl.ds(other, FH)], wout.at[1], s_wout, r_wout, exp_dev(sib))
    w1.start()
    w2.start()

    pltpu.make_async_copy(kc, kc, lsem.at[0]).wait()
    vt[...] = kc[0:KVR, :].T

    scale = (DV + ROPE) ** (-0.5)
    NT = NS * PAGE

    def attend(src, own):
        qx = q_all[src].reshape(RH, q_all.shape[3])
        q = qx[:, 0:LAT]
        sc = mm(q, kc[...]) * scale
        lid = iota((1, NT), 1)
        slot_lane = lax.div(lid, PAGE)
        tpos = lax.rem(lid, PAGE).astype(F32)
        rows = []
        for s in range(ROWS):
            lv = qx[s * H : s * H + 8, LAT : LAT + 2].astype(F32)
            ln = lv[0:1, 0:1] * 32.0 + lv[0:1, 1:2]
            cnt = jnp.zeros((1, NT), F32)
            for p in range(owner_ref.shape[3]):
                here = jnp.where(owner_ref[src, 0, s, p] == g, slot_ref[src, 0, s, p], -1)
                ok = jnp.logical_and(slot_lane == here, tpos + float(p * PAGE) < ln)
                cnt = cnt + ok.astype(F32)
            rows.append(jnp.broadcast_to(cnt, (H, NT)))
        cnt = jnp.concatenate(rows, axis=0)
        scm = jnp.where(cnt > 0, sc, NEG)
        top = jnp.max(scm, axis=1, keepdims=True)
        if own:
            cs = (iota((RH, 128), 1) == lax.div(iota((RH, 128), 0), H)).astype(F32)
            ss = jnp.where(cs > 0, mm_nt(q, nlp[...]) * scale, NEG)
            top = jnp.maximum(top, jnp.max(ss, axis=1, keepdims=True))
        p = cnt * jnp.exp(scm - top)
        den = jnp.sum(p, axis=1, keepdims=True)
        acc = mm(p.astype(BF16), vt[...])
        if own:
            pself = cs * jnp.exp(ss - top)
            den = den + jnp.sum(pself, axis=1, keepdims=True)
            acc = acc + mm(pself.astype(BF16), nlp[:, 0:KVR])
        has = den > 0
        inv_den = jnp.where(has, 1.0 / jnp.where(has, den, 1.0), 0.0)
        lse = jnp.where(has, top + jnp.log(jnp.where(has, den, 1.0)), NEG)
        o_all[pl.ds(pl.multiple_of(src * RH, RH), RH), :] = (acc * inv_den).astype(BF16)
        row = jnp.broadcast_to(lse, (RH, 128)).T[0:1]
        lse_s[src] = jnp.concatenate([row, row], axis=1)

    attend(g, True)

    col = iota((W, 2 * W), 1)
    two = 2 * iota((W, 2 * W), 0)
    pick_g = (col == two).astype(BF16)
    pick_u = (col == two + 1).astype(BF16)

    def split(o, e):
        w = win[o, e].reshape(2 * W, FH)
        wgate = mm(pick_g, w).astype(BF16)
        wup = mm(pick_u, w).astype(BF16)
        for f in range(4):
            wg[e, o, :, 2 * f * QF : (2 * f + 1) * QF] = wgate[:, f * QF : (f + 1) * QF]
            wg[e, o, :, (2 * f + 1) * QF : 2 * (f + 1) * QF] = wup[:, f * QF : (f + 1) * QF]

    c_win.wait()
    loop(0, ELOC, lambda e: split(0, e))

    c_wo.wait()
    wot[...] = wo[...].T

    for i, off in ((0, -2), (1, 2)):
        src = at_dp(off)
        q_copy(src, off).wait_recv()
        q_copy(src, 1 - 2 * i).start()
        q_copy(src, 2 - 4 * i, row=i).start()

    def sml_copy(off, n):
        j = at_dp(off)
        return rcopy(sml_s.at[j], sml_r.at[n], s_sml, r_sml, dp_dev(j))

    others = [4, -3, 3, -2, 2, -1, 1]
    for off in others:
        sml_copy(off, BACK[off]).start()

    def ring(d):
        n = lax.div(d, 2)
        m = jnp.where(n == 0, 2, jnp.where(n == 1, 1, n + 1))
        return at_dp(jnp.where(lax.rem(d, 2) == 0, -m, m))

    def near(d):
        attend(ring(d), False)

    def chunk(d):
        src = ring(d)
        heard_all(q_all.at[src], r_q.at[src])
        attend(src, False)

    loop(0, 2, near)
    loop(2, G - 2, chunk)
    far = at_dp(G // 2)
    heard_all(q_all.at[far], r_q.at[far])
    attend(far, False)

    o_hm[...] = mm(perm[...], o_all[...]).astype(BF16)
    c_wv.wait()
    HB = 16

    def project(b):
        for i in range(HB):
            h = b * HB + i
            at = pl.ds(pl.multiple_of(h * NR, NR), NR)
            hv_hm[at, :] = mm(o_hm[at, :], wv[h]).astype(BF16)

    loop(0, H // HB, project)
    hv_s[...] = mm(perm_t[...], hv_hm[...]).astype(BF16).reshape(G, RH, DV)
    hv_r[g] = hv_s[g]
    lse_r[g] = lse_s[g]

    def part_of(r):
        return pl.ds(r * H, H)

    def send_hv(r, d):
        j = dp_peer(d)
        if r == 0:
            rcopy(lse_s.at[j], lse_r.at[g], s_lse, r_lse, dp_dev(j)).start()
        rcopy(
            hv_s.at[j, part_of(r)], hv_r.at[g, part_of(r)], s_hv, r_rows.at[r], dp_dev(j)
        ).start()

    for r in range(ROWS):
        loop(1, G, functools.partial(send_hv, r))

    heard_all(win.at[1], r_win)
    loop(0, ELOC, lambda e: split(1, e))
    heard_all(sml_r.at[pl.ds(0, G - 1)], r_sml)
    siota = iota((ESL, 4 * GROUP), 0).astype(F32)
    codes_in = sml_r[:, :, 0:GROUP].reshape(8 * G, GROUP).astype(BF16)
    split_codes = mm(codes_in, from_split)

    def slots(rows, w, e):
        return jnp.concatenate(
            [jnp.where(c >= 0, c + float(t * CAPX), -1.0) for t, c in enumerate(rows)], axis=1
        )

    for w in range(2):
        for e in range(ELOC):
            ns = [4 * w + t for t in range(4)]
            given = siota == slots([sml_r[n, e : e + 1, 0:GROUP] for n in ns], w, e)
            halved = siota == slots([split_codes[8 * n + e : 8 * n + e + 1] for n in ns], w, e)
            sel[w, e] = halved.astype(F32).astype(BF16)
            sel_g[w, e] = given.astype(F32).astype(BF16)
            gvals = [sml_r[n, ELOC + e : ELOC + e + 1, 0:GROUP] for n in ns]
            gs = jnp.where(given, jnp.concatenate(gvals, axis=1), 0.0)
            gcol[w, e] = jnp.broadcast_to(jnp.sum(gs, axis=1, keepdims=True), (ESL, 128))
        sel_t[w] = sel_g[w].reshape(ELOC * ESL, 4 * GROUP).T
    res_split = mm(to_split, res_ref[...])

    heard_all(lse_r.at[pl.ds(0, G - 1)], r_lse)
    riota = iota((8, 128), 0)
    ls = jnp.full((8, 128), NEG, F32)
    for j in range(G):
        ls = jnp.where(riota == j, lse_r[j], ls)
    wts = jnp.exp(ls - jnp.max(ls, axis=0, keepdims=True))
    wts = wts / jnp.sum(wts, axis=0, keepdims=True)
    wcol = wts.T
    plane = [(2, 2), (2, 1), (2, -1), (1, 2), (-1, 2), (2, 0), (0, 2)]
    plane += [(1, 1), (1, -1), (-1, 1), (-1, -1), (1, 0), (-1, 0), (0, 1), (0, -1)]

    for r in range(ROWS):
        heard_all(hv_r.at[pl.ds(0, G - 1), part_of(0)], r_rows.at[r])
        comb = jnp.zeros((H, DV), F32)
        for j in range(G):
            at = slice(r * H, (r + 1) * H)
            comb = comb + wcol[at, j : j + 1] * hv_r[j, at].astype(F32)
        hva[r, k] = comb.astype(BF16)
        for ox, oy in plane:
            x, y, dev = at_chip(ox, oy)
            for kk in (2 * (4 * y + x) + core, 2 * (4 * y + x) + 1 - core):
                rcopy(hva.at[r, k], hva.at[r, k], s_hva, r_rows.at[ROWS + r], exp_dev(kk)).start()
        rcopy(hva.at[r, k], hva.at[r, k], s_hva, r_rows.at[ROWS + r], exp_dev(sib)).start()

    def half(r):
        return pl.ds(r * C, C)

    def x_copy(off, n, r):
        ref = xall.at[n // 4, n % 4, half(r)]
        return rcopy(xall.at[1, 0, half(r)], ref, s_x, r_x.at[n], dp_dev(at_dp(off)))

    def fwd(n):
        src, dst = xall.at[n // 4, n % 4], xsib.at[n // 4, n % 4]
        return rcopy(src, dst, s_fw, r_fwd[n // 4], exp_dev(sib))

    c_wout.wait()
    heard_all(wout.at[1], r_wout)
    for o in range(2):
        for e in range(ELOC):
            woutt[o, e] = wout[o, e].T

    resids = []
    for r in range(ROWS):
        heard_all(hva.at[r, pl.ds(0, C - 1)], r_rows.at[ROWS + r])
        both = [hva[r, b * NR : (b + 1) * NR].reshape(N2, DV) for b in range(C // NR)]
        blk = mm(perm[...], jnp.concatenate(both, axis=1)).astype(BF16)
        for b in range(C // NR):
            for h in range(H):
                xmat[r, b * NR : (b + 1) * NR, h * DV : (h + 1) * DV] = blk[
                    h * NR : (h + 1) * NR, b * DV : (b + 1) * DV
                ]
        proj = mm(xmat[r], wot[...])
        resids.append((res_split[r * C : (r + 1) * C] + proj).astype(BF16).astype(F32))
        xall[1, 0, r * C : (r + 1) * C] = (resids[r] * gain_ref[...]).astype(BF16)
        for off in others:
            x_copy(off, BACK[off], r).start()
    fwd(ME).start()
    resid = jnp.concatenate(resids, axis=0)
    sq = jnp.sum(resid * resid, axis=1, keepdims=True)
    sq_row = jnp.broadcast_to(sq, (GROUP, 128)).T[0:1]
    sq_s[...] = jnp.concatenate([sq_row] * (128 // GROUP), axis=1)
    sq_r[k] = sq_s[...]

    def send_sq(d):
        j = ex_peer(d)
        rcopy(sq_s, sq_r.at[k], s_sq, r_sq, exp_dev(j)).start()

    loop(1, C, send_sq)

    def get_x(w):
        for off in sorted(WAVES[w], key=abs):
            if off != 0:
                n = POS[off]
                heard_all(xall.at[n // 4, n % 4], r_x.at[n])
                fwd(n).start()
        heard_all(xsib.at[w], r_fwd[w])

    place = (cx, cy)

    def along(h, off):
        return at_chip(off, 0)[2] if h == 0 else at_chip(0, off)[2]

    def across(h, off):
        return at_chip(0, off)[2] if h == 0 else at_chip(off, 0)[2]

    def ring1(w, h, slot, src):
        sem = r_p1.at[3 * (2 * w + h) + min(slot, 2)]
        return rcopy(src, in1.at[w, h, slot], s_p1, sem, along(h, 1 if slot in (0, 2, 3) else -1))

    def block(e):
        return pl.ds(pl.multiple_of(e * ESL, 16), ESL)

    def partials(w):
        def step(i):
            e = lax.rem(cx + 2 + 3 * i, 4)
            xo = mm(sel[w, e], xall[w].reshape(4 * GROUP, W)).astype(BF16)
            xs = mm(sel[w, e], xsib[w].reshape(4 * GROUP, W)).astype(BF16)
            for f in range(4):
                cols = slice(2 * f * QF, 2 * (f + 1) * QF)
                both = mm(xo, wg[e, 0, :, cols]) + mm(xs, wg[e, 1, :, cols])
                part[w, f, block(e)] = both.astype(BF16)
            for h in range(2):
                role = lax.rem(e - place[h] + 4, 4)

                @pl.when(role == 2)
                def _():
                    ring1(w, h, 0, part.at[w, 2 * h, block(e)]).start()
                    ring1(w, h, 1, part.at[w, 2 * h + 1, block(e)]).start()

                @pl.when(role == 1)
                def _():
                    ring1(w, h, 2, part.at[w, 2 * h + 1, block(e)]).start()

                @pl.when(role == 3)
                def _():
                    ring1(w, h, 4, part.at[w, 2 * h, block(e)]).start()

        loop(0, 4, step)

    def relay(w):
        for h in range(2):
            for i in range(2):
                to = lax.rem(place[h] + (1, 3)[i], 4)
                ring1(w, h, i, in1.at[w, h, i]).wait_recv()
                passed = part[w, 2 * h + i, block(to)].astype(F32) + in1[w, h, i].astype(F32)
                out1[w, h, i] = passed.astype(BF16)
                ring1(w, h, 3 + 2 * i, out1.at[w, h, i]).start()

    def rows2(p):
        return pl.ds(pl.multiple_of(lax.div(p, 2) * QR, 16), QR)

    def ring2(w, h, off):
        to = lax.rem(place[1 - h] + off, 4)
        src = b2.at[w, h, lax.rem(to, 2), rows2(to)]
        return rcopy(src, in2.at[w, h, 4 - off], s_p2, r_p2.at[2 * w + h], across(h, off))

    def second(w):
        for h in range(2):
            heard_all(in1.at[w, h, pl.ds(2, 4)], r_p1.at[3 * (2 * w + h) + 2])
            for i in range(2):
                own = part[w, 2 * h + i, block(place[h])].astype(F32)
                got = in1[w, h, 4 - 2 * i].astype(F32) + in1[w, h, 3 + 2 * i].astype(F32)
                b2[w, h, i] = (own + got).astype(BF16)
            for off in (2, 1, 3):
                ring2(w, h, off).start()
            p = place[1 - h]
            in2[w, h, 0] = b2[w, h, lax.rem(p, 2), rows2(p)]

    def piece(w, h, x, y):
        p = (x, y)
        at = p[h] * ESL + lax.div(p[1 - h], 2) * QR
        return w, 2 * h + lax.rem(p[1 - h], 2), pl.ds(pl.multiple_of(at, 16), QR)

    def hid_copy(w, h, dev):
        ref = hid.at[piece(w, h, cx, cy)]
        return rcopy(ref, ref, s_hid, r_hid.at[w], dev)

    def hidden(w):
        irow = jnp.concatenate([inv_r[4 * w + t, 0:1, 0:GROUP] for t in range(4)], axis=1)
        for h in range(2):
            mine = sel[w, place[h], rows2(place[1 - h]), :]
            icol = jnp.sum(mine.astype(F32) * irow, axis=1, keepdims=True)
            heard_all(in2.at[w, h, pl.ds(1, 3)], r_p2.at[2 * w + h])
            tot = in2[w, h, 0].astype(F32)
            for j in range(1, 4):
                tot = tot + in2[w, h, j].astype(F32)
            tot = tot * icol
            ga = tot[:, 0:QF]
            hv = ga / (1.0 + jnp.exp(-ga)) * tot[:, QF : 2 * QF]
            hid[piece(w, h, cx, cy)] = hv.astype(BF16)
            for ox, oy in plane:
                hid_copy(w, h, at_chip(ox, oy)[2]).start()

    def down(w):
        heard_all(wv.at[pl.ds(0, 30), pl.ds(0, QR)], r_hid.at[w])

        def out(o, into):
            for e in range(ELOC):
                at = slice(e * ESL, (e + 1) * ESL)
                he = jnp.concatenate([hid[w, f, at] for f in range(4)], axis=1)
                into[w, at, :] = (mm(he, woutt[o, e]) * gcol[w, e, :, 0:1]).astype(BF16)

        out(1, vsib)
        zsib_s[w] = mm(sel_t[w], vsib[w]).astype(BF16)
        zsib_copy(w).start()
        out(0, vown)
        zown[w] = mm(sel_t[w], vown[w])

    def zsib_copy(w):
        return rcopy(zsib_s.at[w], zsib_r.at[w], s_zsib, r_zsib[w], exp_dev(sib))

    def z_copy(off, n):
        ref = zs.at[POS[off] // 4, POS[off] % 4]
        return rcopy(ref, zr.at[n], s_z, r_z, dp_dev(at_dp(off)))

    def give_back(w):
        zsib_copy(w).wait_recv()
        zsum = zown[w] + zsib_r[w].astype(F32)
        zown[w] = zsum
        zs[w] = zsum.astype(BF16).reshape(4, GROUP, W)
        for off in sorted(WAVES[w], key=lambda o: -abs(o)):
            if off != 0:
                z_copy(off, BACK[off]).start()

    get_x(0)
    partials(0)

    heard_all(sq_r.at[pl.ds(0, C - 1)], r_sq)
    inv_s[...] = lax.rsqrt(jnp.sum(sq_r[...], axis=0) / D + EPS)
    inv_r[ME] = inv_s[...]

    def inv_copy(off, n):
        return rcopy(inv_s, inv_r.at[n], s_inv, r_inv, dp_dev(at_dp(off)))

    for off in others:
        inv_copy(off, BACK[off]).start()
    get_x(1)
    partials(1)
    relay(0)
    relay(1)
    second(0)
    second(1)
    heard_all(inv_r.at[pl.ds(0, G - 1)], r_inv)
    hidden(0)
    hidden(1)
    down(0)
    give_back(0)
    down(1)
    give_back(1)
    total = mm(from_split, resid.astype(BF16)) + zown[1, 0:GROUP, :]

    w1.wait_send()
    w2.wait_send()
    seven = pl.ds(0, G - 1)
    sent_all(q_all.at[seven], s_q)
    sent_all(sml_r.at[seven], s_sml)
    sent_all(hv_r.at[seven], s_hv)
    sent_all(lse_r.at[seven], s_lse)
    sent_all(hva.at[:, pl.ds(0, C - 1)], s_hva)
    sent_all(zr.at[seven], s_x)
    sent_all(zr, s_fw)
    sent_all(sq_r.at[pl.ds(0, C - 1)], s_sq)
    sent_all(inv_r.at[seven], s_inv)
    sent_all(in1, s_p1)
    sent_all(in2.at[:, :, pl.ds(0, 3)], s_p2)
    sent_all(wv.at[pl.ds(0, 30), pl.ds(0, 2 * QR)], s_hid)
    sent_all(zsib_r, s_zsib)

    heard_all(zr.at[seven], r_z)
    for off in others:
        total = total + zr[POS[off]].astype(F32)
    out_ref[...] = total.astype(BF16)
    sent_all(zr.at[seven], s_z)


def body(
    queries, new_latent, pool_pages, page_owner, page_slot, lengths, residual, value_weight,
    output_weight, norm_gain, expert_ids, route_gates, expert_in, expert_out,
):
    G = lax.axis_size("dp")
    C = lax.axis_size("expert")
    ROWS, H, LAT = queries.shape
    NS, _, PAGE = pool_pages.shape
    GROUP, W = residual.shape
    ELOC, _, _, FF = expert_in.shape
    FH = FF // 2
    RH = ROWS * H
    capacity = min(GROUP, (3 * GROUP * TOP + 2 * G * ELOC - 1) // (2 * G * ELOC))
    ESL = 4 * capacity
    SLOTS = ELOC * ESL
    QR, QC = ESL // 2, FF // 4
    N2 = G * RH
    HALF = 4 * GROUP

    def v(shape, dtype=BF16):
        return pltpu.VMEM(shape, dtype)

    dma = lambda n: pltpu.SemaphoreType.DMA((n,))
    scratch = [
        v(new_latent.shape), pltpu.SMEM(page_owner.shape, jnp.int32),
        pltpu.SMEM(page_slot.shape, jnp.int32), pltpu.SMEM(lengths.shape, jnp.int32),
        v((GROUP, W)), v((1, W), F32), v((TOP, GROUP), jnp.int32), v((TOP, GROUP), F32),
        v((LAT, NS * PAGE)), v((NS * PAGE, KVR)), v((128, LAT)), v((ROWS, H, LAT)),
        v((G, ROWS, H, -(-(LAT + 2) // 128) * 128)),
        v((G, 8, 128), F32), v((G, 8, 128), F32), v((N2, N2)), v((N2, N2)),
        v((N2, KVR)), v((N2, KVR)), v((N2, DV)), v((G, RH, DV)), v((G, 1, 128), F32),
        v((G, RH, DV)), v((G, 1, 128), F32),
        v((ROWS, C, H, DV)), v((ROWS, C, H * DV)), v((H, KVR, DV)), v((W, H * DV)), v((H * DV, W)),
        v((2, ELOC, W, 2, FH)), v((ELOC, 2, W, FF)), v((2, ELOC, W, FH)), v((2, ELOC, FH, W)),
        v((2, 4, GROUP, W)), v((2, 4, GROUP, W)), v((1, 128), F32), v((C, 1, 128), F32),
        v((1, 128), F32), v((G, 1, 128), F32),
        v((2, ELOC, ESL, HALF)), v((2, ELOC, ESL, HALF)), v((2, HALF, SLOTS)), v((2, ELOC, ESL, 128), F32),
        v((2, 4, SLOTS, QC)), v((2, 2, 6, ESL, QC)), v((2, 2, 2, ESL, QC)), v((2, 2, 2, ESL, QC)),
        v((2, 2, 4, QR, QC)), v((2, 4, SLOTS, QC // 2)), v((2, SLOTS, W)), v((2, SLOTS, W)),
        v((2, HALF, W)), v((2, HALF, W)), v((2, 4, GROUP, W)), v((G, GROUP, W)),
        v((2, HALF, W), F32),
        dma(14), dma(16), dma(12), dma(2 * ROWS), dma(G), dma(G), dma(12), dma(4), dma(2),
    ]
    vm = pl.BlockSpec(memory_space=pltpu.VMEM)
    hbm = pl.BlockSpec(memory_space=pl.ANY)
    return pl.pallas_call(
        functools.partial(kernel, G, C, ELOC, capacity),
        out_shape=jax.ShapeDtypeStruct((GROUP, W), BF16),
        in_specs=[hbm] * 14,
        out_specs=vm,
        scratch_shapes=scratch,
        compiler_params=pltpu.CompilerParams(
            collective_id=0, has_side_effects=True, vmem_limit_bytes=56 << 20
        ),
        cost_estimate=pl.CostEstimate(flops=4 << 30, bytes_accessed=16 << 20, transcendentals=1 << 20),
        name="decode_step",
    )(
        queries, new_latent, pool_pages, page_owner, page_slot, lengths, residual, value_weight,
        output_weight.T, norm_gain.reshape(1, W), expert_ids.T, route_gates.T, expert_in,
        jnp.swapaxes(expert_out, 1, 2),
    )


def solution(mesh):
    in_specs = (
        P(("dp", "expert"), None, None),
        P(("dp", "expert"), None),
        P(("dp", "expert"), None, None),
        P(None, "expert", None, None),
        P(None, "expert", None, None),
        P(("dp", "expert")),
        P("dp", "expert"),
        P(),
        P(None, "expert"),
        P("expert"),
        P("dp", None),
        P("dp", None),
        P("dp", "expert", None, None),
        P("dp", None, "expert"),
    )
    return jax.shard_map(
        body, mesh=mesh, in_specs=in_specs, out_specs=P("dp", "expert"), check_vma=False
    )
```

```python
import functools
import jax
import jax.numpy as jnp
from jax import lax
from jax.experimental import pallas as pl
from jax.experimental.pallas import tpu as pltpu
from jax.sharding import PartitionSpec as P

D = 7168
KVR = 512
ROPE = 64
DV = 128
TOP = 8
EPS = 1e-06
MESH = pl.DeviceIdType.MESH
F32 = jnp.float32
BF16 = jnp.bfloat16
NEG = -1e30
WAVES = ((4, -3, 3, -2), (0, 1, -1, 2))
POS = {off: 4 * w + t for w in range(2) for t, off in enumerate(WAVES[w])}
ME = POS[0]
BACK = {off: POS[4 if off == 4 else -off] for off in POS}


def iota(shape, dim):
    return lax.broadcasted_iota(jnp.int32, shape, dim)


def mm(a, b):
    return jnp.dot(a, b, preferred_element_type=F32)


def mm_nt(a, b):
    return lax.dot_general(a, b, (((1,), (1,)), ((), ())), preferred_element_type=F32)


def kernel(
    G, C, ELOC, CAPX,
    q_hbm, nl_hbm, pool_hbm, owner_hbm, slot_hbm, len_hbm, res_hbm, wv_hbm, wo_hbm, gain_hbm,
    ids_hbm, gates_hbm, win_hbm, wout_hbm,
    out_ref,
    nl_ref, owner_ref, slot_ref, len_ref, res_ref, gain_ref, ids_ref, gates_ref,
    kc, vt, nlp, q_in, q_main, q_rope, len_r, sml_s, sml_r, perm, perm_t, o_all, o_hm, hv_hm, hv_s, lse_s, hv_r,
    lse_r, hva, xmat, wv, wo, wot, win, wg, wout, woutt, xall, xsib, sq_s, sq_r, inv_s, inv_r,
    sel, sel_g, sel_t, gcol, part, in1, out1, b2, in2, hid, vown, vsib, zsib_s, zsib_r, zs, zr, zown,
    lsem, sent, heard, r_rows, r_q, r_rope, r_x, r_p1, r_p2, r_hid,
):
    g = lax.axis_index("dp")
    k = lax.axis_index("expert")
    core = lax.rem(k, 2)
    chip = lax.div(k, 2)
    sib = k + 1 - 2 * core
    cx = lax.rem(chip, 4)
    cy = lax.div(chip, 4)
    ROWS, H, LAT = q_in.shape
    NS = pool_hbm.shape[0]
    PAGE = pool_hbm.shape[2]
    RH = ROWS * H
    GROUP = C * ROWS
    W = res_ref.shape[1]
    FF = win_hbm.shape[3]
    FH = FF // 2
    ESL = 4 * CAPX
    QR = ESL // 2
    QF = FH // 4
    NR = G * ROWS

    def dp_peer(d):
        half = lax.div(G + 1 - d, 2)
        off = half * (1 - 2 * lax.rem(G + 1 - d, 2))
        return lax.rem(g + off + G, G)

    def at_dp(off):
        return lax.rem(g + off + G, G)

    def ex_peer(d):
        return lax.rem(k + d, C)

    def at_chip(ox, oy):
        x = lax.rem(cx + ox + 4, 4)
        y = lax.rem(cy + oy + 4, 4)
        return x, y, (g, 2 * (4 * y + x) + core)

    s_q, s_sml, s_hv, s_lse, s_hva, s_x, s_fw, s_sq = (sent.at[i] for i in range(8))
    s_inv, s_p1, s_p2, s_hid, s_win, s_wout, s_zsib, s_z = (sent.at[8 + i] for i in range(8))
    r_sml, r_lse, r_inv, r_z, r_sq, r_win, r_wout = (heard.at[i] for i in range(7))
    s_rope, s_len, r_len = sent.at[16], sent.at[17], heard.at[12]
    r_fwd, r_zsib = (heard.at[8], heard.at[9]), (heard.at[10], heard.at[11])

    def rcopy(src, dst, ss, rs, dev):
        return pltpu.make_async_remote_copy(
            src_ref=src, dst_ref=dst, send_sem=ss, recv_sem=rs, device_id=dev, device_id_type=MESH
        )

    def sent_all(ref, sem):
        rcopy(ref, ref, sem, sem, exp_dev(sib)).wait_send()

    def heard_all(ref, sem):
        rcopy(ref, ref, sem, sem, exp_dev(sib)).wait_recv()

    def loop(lo, hi, fn):
        lax.fori_loop(lo, hi, lambda i, c: (fn(i), c)[1], 0)

    def exp_dev(kk):
        return (g, kk)

    def dp_dev(j):
        return (j, k)

    locals_ = []
    for s in range(NS):
        locals_.append(
            pltpu.make_async_copy(pool_hbm.at[s], kc.at[:, pl.ds(s * PAGE, PAGE)], lsem.at[0])
        )
    c_q = pltpu.make_async_copy(q_hbm, q_in, lsem.at[1])
    c_win = pltpu.make_async_copy(
        win_hbm.at[:, :, :, pl.ds(pl.multiple_of(core * FH, FH), FH)], win.at[0], lsem.at[2]
    )
    c_wv = pltpu.make_async_copy(wv_hbm, wv, lsem.at[3])
    c_wo = pltpu.make_async_copy(wo_hbm, wo, lsem.at[4])
    c_wout = pltpu.make_async_copy(
        wout_hbm.at[:, :, pl.ds(pl.multiple_of(core * FH, FH), FH)], wout.at[0], lsem.at[5]
    )
    c_q.start()
    small = []
    for i, (a, b) in enumerate(
        (
            (ids_hbm, ids_ref), (gates_hbm, gates_ref), (len_hbm, len_ref), (nl_hbm, nl_ref),
            (owner_hbm, owner_ref), (slot_hbm, slot_ref), (res_hbm, res_ref), (gain_hbm, gain_ref),
        )
    ):
        small.append(pltpu.make_async_copy(a, b, lsem.at[6 + i]))
        small[-1].start()
    for c in locals_:
        c.start()
    for c in (c_win, c_wv, c_wo, c_wout):
        c.start()

    barrier = pltpu.get_barrier_semaphore()

    def sig_dp(d):
        pl.semaphore_signal(barrier, inc=1, device_id=dp_dev(lax.rem(g + d, G)), device_id_type=MESH)

    def sig_ex(d):
        pl.semaphore_signal(barrier, inc=1, device_id=exp_dev(ex_peer(d)), device_id_type=MESH)

    loop(1, G, sig_dp)
    loop(1, C, sig_ex)

    c_q.wait()
    small[2].wait()
    q_main[g] = q_in[:, :, 0:KVR]
    q_rope[g] = jnp.concatenate([q_in[r, :, KVR:LAT] for r in range(ROWS)], axis=1)
    lane = iota((1, 128), 1)
    lens = jnp.zeros((1, 128), F32)
    for r in range(ROWS):
        lens = jnp.where(lane == r, len_ref[r].astype(F32), lens)
    len_r[g] = lens
    pl.semaphore_wait(barrier, G - 1 + C - 1)

    def q_copy(src, off):
        ref = q_main.at[src]
        return rcopy(ref, ref, s_q, r_q.at[src], dp_dev(at_dp(off)))

    def rope_copy(src, off):
        ref = q_rope.at[src]
        return rcopy(ref, ref, s_rope, r_rope.at[src], dp_dev(at_dp(off)))

    def len_copy(off):
        ref = len_r.at[g]
        return rcopy(ref, ref, s_len, r_len, dp_dev(at_dp(off)))

    others = [4, -3, 3, -2, 2, -1, 1]
    for off in others:
        len_copy(off).start()
    def send_q(off):
        q_copy(g, off).start()
        rope_copy(g, off).start()

    send_q(2)
    send_q(-2)

    for i, c in enumerate(small):
        if i != 2:
            c.wait()
    ids = ids_ref[...]
    gates = gates_ref[...]
    e_iota = iota((G * ELOC, GROUP), 0)
    named = jnp.zeros((G * ELOC, GROUP), F32)
    gval = jnp.zeros((G * ELOC, GROUP), F32)
    for t in range(TOP):
        hit = ids[t : t + 1, :] == e_iota
        named = named + hit.astype(F32)
        gval = gval + jnp.where(hit, gates[t : t + 1, :], 0.0)
    tri = (iota((GROUP, GROUP), 0) < iota((GROUP, GROUP), 1)).astype(BF16)
    rank = mm(named.astype(BF16), tri)
    code = jnp.where(named > 0, rank, -1.0)
    sml_s[...] = jnp.zeros_like(sml_s)
    for j in range(G):
        sml_s[j, 0:ELOC, 0:GROUP] = code[j * ELOC : (j + 1) * ELOC]
        sml_s[j, ELOC : 2 * ELOC, 0:GROUP] = gval[j * ELOC : (j + 1) * ELOC]
    sml_r[ME] = sml_s[g]

    N2 = NR * H
    pr = iota((N2, 1), 0)
    perm[...] = (iota((N2, N2), 1) == lax.rem(pr, NR) * H + lax.div(pr, NR)).astype(BF16)
    perm_t[...] = (iota((N2, N2), 1) == lax.rem(pr, H) * NR + lax.div(pr, H)).astype(BF16)
    rr = iota((GROUP, GROUP), 0)
    rc = iota((GROUP, GROUP), 1)
    to_split = (rc == lax.rem(rr, C) * ROWS + lax.div(rr, C)).astype(BF16)
    from_split = (rr == lax.rem(rc, C) * ROWS + lax.div(rc, C)).astype(BF16)
    nl = nl_ref[...].astype(F32)
    nrow = iota((128, LAT), 0)
    nacc = jnp.zeros((128, LAT), F32)
    for s in range(ROWS):
        nacc = jnp.where(nrow == s, nl[s : s + 1, :], nacc)
    nlp[...] = nacc.astype(BF16)

    other = pl.multiple_of((1 - core) * FH, FH)
    w1 = rcopy(win_hbm.at[:, :, :, pl.ds(other, FH)], win.at[1], s_win, r_win, exp_dev(sib))
    w2 = rcopy(wout_hbm.at[:, :, pl.ds(other, FH)], wout.at[1], s_wout, r_wout, exp_dev(sib))
    w1.start()
    w2.start()

    pltpu.make_async_copy(kc, kc, lsem.at[0]).wait()
    vt[...] = kc[0:KVR, :].T

    scale = (DV + ROPE) ** (-0.5)
    NT = NS * PAGE

    def attend(src, own):
        q = q_main[src].reshape(RH, KVR)
        ropes = q_rope[src]
        qr = jnp.concatenate([ropes[:, r * ROPE : (r + 1) * ROPE] for r in range(ROWS)], axis=0)
        sc = (mm(q, kc[0:KVR, :]) + mm(qr, kc[KVR:LAT, :])) * scale
        lid = iota((1, NT), 1)
        slot_lane = lax.div(lid, PAGE)
        tpos = lax.rem(lid, PAGE).astype(F32)
        rows = []
        for s in range(ROWS):
            ln = len_r[src][0:1, s : s + 1]
            cnt = jnp.zeros((1, NT), F32)
            for p in range(owner_ref.shape[3]):
                here = jnp.where(owner_ref[src, 0, s, p] == g, slot_ref[src, 0, s, p], -1)
                ok = jnp.logical_and(slot_lane == here, tpos + float(p * PAGE) < ln)
                cnt = cnt + ok.astype(F32)
            rows.append(jnp.broadcast_to(cnt, (H, NT)))
        cnt = jnp.concatenate(rows, axis=0)
        scm = jnp.where(cnt > 0, sc, NEG)
        top = jnp.max(scm, axis=1, keepdims=True)
        if own:
            cs = (iota((RH, 128), 1) == lax.div(iota((RH, 128), 0), H)).astype(F32)
            ss = (mm_nt(q, nlp[:, 0:KVR]) + mm_nt(qr, nlp[:, KVR:LAT])) * scale
            ss = jnp.where(cs > 0, ss, NEG)
            top = jnp.maximum(top, jnp.max(ss, axis=1, keepdims=True))
        p = cnt * jnp.exp(scm - top)
        den = jnp.sum(p, axis=1, keepdims=True)
        acc = mm(p.astype(BF16), vt[...])
        if own:
            pself = cs * jnp.exp(ss - top)
            den = den + jnp.sum(pself, axis=1, keepdims=True)
            acc = acc + mm(pself.astype(BF16), nlp[:, 0:KVR])
        has = den > 0
        inv_den = jnp.where(has, 1.0 / jnp.where(has, den, 1.0), 0.0)
        lse = jnp.where(has, top + jnp.log(jnp.where(has, den, 1.0)), NEG)
        o_all[pl.ds(pl.multiple_of(src * RH, RH), RH), :] = (acc * inv_den).astype(BF16)
        row = jnp.broadcast_to(lse, (RH, 128)).T[0:1]
        lse_s[src] = jnp.concatenate([row, row], axis=1)

    attend(g, True)

    send_q(1)
    send_q(-1)

    col = iota((W, 2 * W), 1)
    two = 2 * iota((W, 2 * W), 0)
    pick_g = (col == two).astype(BF16)
    pick_u = (col == two + 1).astype(BF16)

    def split(o, e):
        w = win[o, e].reshape(2 * W, FH)
        wgate = mm(pick_g, w).astype(BF16)
        wup = mm(pick_u, w).astype(BF16)
        for f in range(4):
            wg[e, o, :, 2 * f * QF : (2 * f + 1) * QF] = wgate[:, f * QF : (f + 1) * QF]
            wg[e, o, :, (2 * f + 1) * QF : 2 * (f + 1) * QF] = wup[:, f * QF : (f + 1) * QF]

    c_win.wait()
    loop(0, ELOC, lambda e: split(0, e))

    c_wo.wait()
    wot[...] = wo[...].T

    for i, off in ((0, -2), (1, 2)):
        src = at_dp(off)
        heard_all(q_main.at[src], r_q.at[src])
        heard_all(q_rope.at[src], r_rope.at[src])
        q_copy(src, 1 - 2 * i).start()
        rope_copy(src, 1 - 2 * i).start()
        row = q_main.at[src, i]
        rcopy(row, row, s_q, r_q.at[src], dp_dev(at_dp(2 - 4 * i))).start()
        if i == 0:
            rope_copy(src, 2).start()
    heard_all(len_r.at[pl.ds(0, G - 1)], r_len)

    def sml_copy(off, n):
        j = at_dp(off)
        return rcopy(sml_s.at[j], sml_r.at[n], s_sml, r_sml, dp_dev(j))

    for off in others:
        sml_copy(off, BACK[off]).start()

    def ring(d):
        n = lax.div(d, 2)
        m = jnp.where(n == 0, 2, jnp.where(n == 1, 1, n + 1))
        return at_dp(jnp.where(lax.rem(d, 2) == 0, -m, m))

    def near(d):
        attend(ring(d), False)

    def chunk(d):
        src = ring(d)
        heard_all(q_main.at[src], r_q.at[src])
        heard_all(q_rope.at[src], r_rope.at[src])
        attend(src, False)

    loop(0, 2, near)
    loop(2, G - 2, chunk)
    far = at_dp(G // 2)
    heard_all(q_main.at[far], r_q.at[far])
    heard_all(q_rope.at[far], r_rope.at[far])
    attend(far, False)

    o_hm[...] = mm(perm[...], o_all[...]).astype(BF16)
    c_wv.wait()
    HB = 16

    def project(b):
        for i in range(HB):
            h = b * HB + i
            at = pl.ds(pl.multiple_of(h * NR, NR), NR)
            hv_hm[at, :] = mm(o_hm[at, :], wv[h]).astype(BF16)

    loop(0, H // HB, project)
    hv_s[...] = mm(perm_t[...], hv_hm[...]).astype(BF16).reshape(G, RH, DV)
    hv_r[g] = hv_s[g]
    lse_r[g] = lse_s[g]

    def part_of(r):
        return pl.ds(r * H, H)

    def send_hv(r, d):
        j = dp_peer(d)
        if r == 0:
            rcopy(lse_s.at[j], lse_r.at[g], s_lse, r_lse, dp_dev(j)).start()
        rcopy(
            hv_s.at[j, part_of(r)], hv_r.at[g, part_of(r)], s_hv, r_rows.at[r], dp_dev(j)
        ).start()

    for r in range(ROWS):
        loop(1, G, functools.partial(send_hv, r))

    heard_all(win.at[1], r_win)
    loop(0, ELOC, lambda e: split(1, e))
    heard_all(sml_r.at[pl.ds(0, G - 1)], r_sml)
    siota = iota((ESL, 4 * GROUP), 0).astype(F32)
    codes_in = sml_r[:, :, 0:GROUP].reshape(8 * G, GROUP).astype(BF16)
    split_codes = mm(codes_in, from_split)

    def slots(rows, w, e):
        return jnp.concatenate(
            [jnp.where(c >= 0, c + float(t * CAPX), -1.0) for t, c in enumerate(rows)], axis=1
        )

    for w in range(2):
        for e in range(ELOC):
            ns = [4 * w + t for t in range(4)]
            given = siota == slots([sml_r[n, e : e + 1, 0:GROUP] for n in ns], w, e)
            halved = siota == slots([split_codes[8 * n + e : 8 * n + e + 1] for n in ns], w, e)
            sel[w, e] = halved.astype(F32).astype(BF16)
            sel_g[w, e] = given.astype(F32).astype(BF16)
            gvals = [sml_r[n, ELOC + e : ELOC + e + 1, 0:GROUP] for n in ns]
            gs = jnp.where(given, jnp.concatenate(gvals, axis=1), 0.0)
            gcol[w, e] = jnp.broadcast_to(jnp.sum(gs, axis=1, keepdims=True), (ESL, 128))
        sel_t[w] = sel_g[w].reshape(ELOC * ESL, 4 * GROUP).T
    res_split = mm(to_split, res_ref[...])

    heard_all(lse_r.at[pl.ds(0, G - 1)], r_lse)
    riota = iota((8, 128), 0)
    ls = jnp.full((8, 128), NEG, F32)
    for j in range(G):
        ls = jnp.where(riota == j, lse_r[j], ls)
    wts = jnp.exp(ls - jnp.max(ls, axis=0, keepdims=True))
    wts = wts / jnp.sum(wts, axis=0, keepdims=True)
    wcol = wts.T
    plane = [(2, 2), (2, 1), (2, -1), (1, 2), (-1, 2), (2, 0), (0, 2)]
    plane += [(1, 1), (1, -1), (-1, 1), (-1, -1), (1, 0), (-1, 0), (0, 1), (0, -1)]

    for r in range(ROWS):
        heard_all(hv_r.at[pl.ds(0, G - 1), part_of(0)], r_rows.at[r])
        comb = jnp.zeros((H, DV), F32)
        for j in range(G):
            at = slice(r * H, (r + 1) * H)
            comb = comb + wcol[at, j : j + 1] * hv_r[j, at].astype(F32)
        hva[r, k] = comb.astype(BF16)
        for ox, oy in plane:
            x, y, dev = at_chip(ox, oy)
            for kk in (2 * (4 * y + x) + core, 2 * (4 * y + x) + 1 - core):
                rcopy(hva.at[r, k], hva.at[r, k], s_hva, r_rows.at[ROWS + r], exp_dev(kk)).start()
        rcopy(hva.at[r, k], hva.at[r, k], s_hva, r_rows.at[ROWS + r], exp_dev(sib)).start()

    def half(r):
        return pl.ds(r * C, C)

    def x_copy(off, n, r):
        ref = xall.at[n // 4, n % 4, half(r)]
        return rcopy(xall.at[1, 0, half(r)], ref, s_x, r_x.at[n], dp_dev(at_dp(off)))

    def fwd(n):
        src, dst = xall.at[n // 4, n % 4], xsib.at[n // 4, n % 4]
        return rcopy(src, dst, s_fw, r_fwd[n // 4], exp_dev(sib))

    c_wout.wait()
    heard_all(wout.at[1], r_wout)
    for o in range(2):
        for e in range(ELOC):
            woutt[o, e] = wout[o, e].T

    resids = []
    for r in range(ROWS):
        heard_all(hva.at[r, pl.ds(0, C - 1)], r_rows.at[ROWS + r])
        both = [hva[r, b * NR : (b + 1) * NR].reshape(N2, DV) for b in range(C // NR)]
        blk = mm(perm[...], jnp.concatenate(both, axis=1)).astype(BF16)
        for b in range(C // NR):
            for h in range(H):
                xmat[r, b * NR : (b + 1) * NR, h * DV : (h + 1) * DV] = blk[
                    h * NR : (h + 1) * NR, b * DV : (b + 1) * DV
                ]
        proj = mm(xmat[r], wot[...])
        resids.append((res_split[r * C : (r + 1) * C] + proj).astype(BF16).astype(F32))
        xall[1, 0, r * C : (r + 1) * C] = (resids[r] * gain_ref[...]).astype(BF16)
        for off in others:
            x_copy(off, BACK[off], r).start()
    fwd(ME).start()
    resid = jnp.concatenate(resids, axis=0)
    sq = jnp.sum(resid * resid, axis=1, keepdims=True)
    sq_row = jnp.broadcast_to(sq, (GROUP, 128)).T[0:1]
    sq_s[...] = jnp.concatenate([sq_row] * (128 // GROUP), axis=1)
    sq_r[k] = sq_s[...]

    def send_sq(d):
        j = ex_peer(d)
        rcopy(sq_s, sq_r.at[k], s_sq, r_sq, exp_dev(j)).start()

    loop(1, C, send_sq)

    def get_x(w):
        for off in sorted(WAVES[w], key=abs):
            if off != 0:
                n = POS[off]
                heard_all(xall.at[n // 4, n % 4], r_x.at[n])
                fwd(n).start()
        heard_all(xsib.at[w], r_fwd[w])

    place = (cx, cy)

    def along(h, off):
        return at_chip(off, 0)[2] if h == 0 else at_chip(0, off)[2]

    def across(h, off):
        return at_chip(0, off)[2] if h == 0 else at_chip(off, 0)[2]

    def ring1(w, h, slot, src):
        sem = r_p1.at[3 * (2 * w + h) + min(slot, 2)]
        return rcopy(src, in1.at[w, h, slot], s_p1, sem, along(h, 1 if slot in (0, 2, 3) else -1))

    def block(e):
        return pl.ds(pl.multiple_of(e * ESL, 16), ESL)

    def partials(w):
        def step(i):
            e = lax.rem(cx + 2 + 3 * i, 4)
            xo = mm(sel[w, e], xall[w].reshape(4 * GROUP, W)).astype(BF16)
            xs = mm(sel[w, e], xsib[w].reshape(4 * GROUP, W)).astype(BF16)
            for f in range(4):
                cols = slice(2 * f * QF, 2 * (f + 1) * QF)
                both = mm(xo, wg[e, 0, :, cols]) + mm(xs, wg[e, 1, :, cols])
                part[w, f, block(e)] = both.astype(BF16)
            for h in range(2):
                role = lax.rem(e - place[h] + 4, 4)

                @pl.when(role == 2)
                def _():
                    ring1(w, h, 0, part.at[w, 2 * h, block(e)]).start()
                    ring1(w, h, 1, part.at[w, 2 * h + 1, block(e)]).start()

                @pl.when(role == 1)
                def _():
                    ring1(w, h, 2, part.at[w, 2 * h + 1, block(e)]).start()

                @pl.when(role == 3)
                def _():
                    ring1(w, h, 4, part.at[w, 2 * h, block(e)]).start()

        loop(0, 4, step)

    def relay(w):
        for h in range(2):
            for i in range(2):
                to = lax.rem(place[h] + (1, 3)[i], 4)
                ring1(w, h, i, in1.at[w, h, i]).wait_recv()
                passed = part[w, 2 * h + i, block(to)].astype(F32) + in1[w, h, i].astype(F32)
                out1[w, h, i] = passed.astype(BF16)
                ring1(w, h, 3 + 2 * i, out1.at[w, h, i]).start()

    def rows2(p):
        return pl.ds(pl.multiple_of(lax.div(p, 2) * QR, 16), QR)

    def ring2(w, h, off):
        to = lax.rem(place[1 - h] + off, 4)
        src = b2.at[w, h, lax.rem(to, 2), rows2(to)]
        return rcopy(src, in2.at[w, h, 4 - off], s_p2, r_p2.at[2 * w + h], across(h, off))

    def second(w):
        for h in range(2):
            heard_all(in1.at[w, h, pl.ds(2, 4)], r_p1.at[3 * (2 * w + h) + 2])
            for i in range(2):
                own = part[w, 2 * h + i, block(place[h])].astype(F32)
                got = in1[w, h, 4 - 2 * i].astype(F32) + in1[w, h, 3 + 2 * i].astype(F32)
                b2[w, h, i] = (own + got).astype(BF16)
            for off in (2, 1, 3):
                ring2(w, h, off).start()
            p = place[1 - h]
            in2[w, h, 0] = b2[w, h, lax.rem(p, 2), rows2(p)]

    def piece(w, h, x, y):
        p = (x, y)
        at = p[h] * ESL + lax.div(p[1 - h], 2) * QR
        return w, 2 * h + lax.rem(p[1 - h], 2), pl.ds(pl.multiple_of(at, 16), QR)

    def hid_copy(w, h, dev):
        ref = hid.at[piece(w, h, cx, cy)]
        return rcopy(ref, ref, s_hid, r_hid.at[w], dev)

    def hidden(w):
        irow = jnp.concatenate([inv_r[4 * w + t, 0:1, 0:GROUP] for t in range(4)], axis=1)
        for h in range(2):
            mine = sel[w, place[h], rows2(place[1 - h]), :]
            icol = jnp.sum(mine.astype(F32) * irow, axis=1, keepdims=True)
            heard_all(in2.at[w, h, pl.ds(1, 3)], r_p2.at[2 * w + h])
            tot = in2[w, h, 0].astype(F32)
            for j in range(1, 4):
                tot = tot + in2[w, h, j].astype(F32)
            tot = tot * icol
            ga = tot[:, 0:QF]
            hv = ga / (1.0 + jnp.exp(-ga)) * tot[:, QF : 2 * QF]
            hid[piece(w, h, cx, cy)] = hv.astype(BF16)
            for ox, oy in plane:
                hid_copy(w, h, at_chip(ox, oy)[2]).start()

    def down(w):
        heard_all(wv.at[pl.ds(0, 30), pl.ds(0, QR)], r_hid.at[w])

        def out(o, into):
            for e in range(ELOC):
                at = slice(e * ESL, (e + 1) * ESL)
                he = jnp.concatenate([hid[w, f, at] for f in range(4)], axis=1)
                into[w, at, :] = (mm(he, woutt[o, e]) * gcol[w, e, :, 0:1]).astype(BF16)

        out(1, vsib)
        zsib_s[w] = mm(sel_t[w], vsib[w]).astype(BF16)
        zsib_copy(w).start()
        out(0, vown)
        zown[w] = mm(sel_t[w], vown[w])

    def zsib_copy(w):
        return rcopy(zsib_s.at[w], zsib_r.at[w], s_zsib, r_zsib[w], exp_dev(sib))

    def z_copy(off, n):
        ref = zs.at[POS[off] // 4, POS[off] % 4]
        return rcopy(ref, zr.at[n], s_z, r_z, dp_dev(at_dp(off)))

    def give_back(w):
        zsib_copy(w).wait_recv()
        zsum = zown[w] + zsib_r[w].astype(F32)
        zown[w] = zsum
        zs[w] = zsum.astype(BF16).reshape(4, GROUP, W)
        for off in sorted(WAVES[w], key=lambda o: -abs(o)):
            if off != 0:
                z_copy(off, BACK[off]).start()

    get_x(0)
    partials(0)

    heard_all(sq_r.at[pl.ds(0, C - 1)], r_sq)
    inv_s[...] = lax.rsqrt(jnp.sum(sq_r[...], axis=0) / D + EPS)
    inv_r[ME] = inv_s[...]

    def inv_copy(off, n):
        return rcopy(inv_s, inv_r.at[n], s_inv, r_inv, dp_dev(at_dp(off)))

    for off in others:
        inv_copy(off, BACK[off]).start()
    get_x(1)
    partials(1)
    relay(0)
    relay(1)
    second(0)
    second(1)
    heard_all(inv_r.at[pl.ds(0, G - 1)], r_inv)
    hidden(0)
    hidden(1)
    down(0)
    give_back(0)
    down(1)
    give_back(1)
    total = mm(from_split, resid.astype(BF16)) + zown[1, 0:GROUP, :]

    w1.wait_send()
    w2.wait_send()
    seven = pl.ds(0, G - 1)
    sent_all(q_main.at[seven], s_q)
    sent_all(q_rope.at[seven], s_rope)
    sent_all(len_r.at[seven], s_len)
    sent_all(sml_r.at[seven], s_sml)
    sent_all(hv_r.at[seven], s_hv)
    sent_all(lse_r.at[seven], s_lse)
    sent_all(hva.at[:, pl.ds(0, C - 1)], s_hva)
    sent_all(zr.at[seven], s_x)
    sent_all(zr, s_fw)
    sent_all(sq_r.at[pl.ds(0, C - 1)], s_sq)
    sent_all(inv_r.at[seven], s_inv)
    sent_all(in1, s_p1)
    sent_all(in2.at[:, :, pl.ds(0, 3)], s_p2)
    sent_all(wv.at[pl.ds(0, 30), pl.ds(0, 2 * QR)], s_hid)
    sent_all(zsib_r, s_zsib)

    heard_all(zr.at[seven], r_z)
    for off in others:
        total = total + zr[POS[off]].astype(F32)
    out_ref[...] = total.astype(BF16)
    sent_all(zr.at[seven], s_z)


def body(
    queries, new_latent, pool_pages, page_owner, page_slot, lengths, residual, value_weight,
    output_weight, norm_gain, expert_ids, route_gates, expert_in, expert_out,
):
    G = lax.axis_size("dp")
    C = lax.axis_size("expert")
    ROWS, H, LAT = queries.shape
    NS, _, PAGE = pool_pages.shape
    GROUP, W = residual.shape
    ELOC, _, _, FF = expert_in.shape
    FH = FF // 2
    RH = ROWS * H
    capacity = min(GROUP, (3 * GROUP * TOP + 2 * G * ELOC - 1) // (2 * G * ELOC))
    ESL = 4 * capacity
    SLOTS = ELOC * ESL
    QR, QC = ESL // 2, FF // 4
    N2 = G * RH
    HALF = 4 * GROUP

    def v(shape, dtype=BF16):
        return pltpu.VMEM(shape, dtype)

    dma = lambda n: pltpu.SemaphoreType.DMA((n,))
    scratch = [
        v(new_latent.shape), pltpu.SMEM(page_owner.shape, jnp.int32),
        pltpu.SMEM(page_slot.shape, jnp.int32), pltpu.SMEM(lengths.shape, jnp.int32),
        v((GROUP, W)), v((1, W), F32), v((TOP, GROUP), jnp.int32), v((TOP, GROUP), F32),
        v((LAT, NS * PAGE)), v((NS * PAGE, KVR)), v((128, LAT)), v((ROWS, H, LAT)),
        v((G, ROWS, H, KVR)), v((G, H, ROWS * ROPE)), v((G, 1, 128), F32),
        v((G, 8, 128), F32), v((G, 8, 128), F32), v((N2, N2)), v((N2, N2)),
        v((N2, KVR)), v((N2, KVR)), v((N2, DV)), v((G, RH, DV)), v((G, 1, 128), F32),
        v((G, RH, DV)), v((G, 1, 128), F32),
        v((ROWS, C, H, DV)), v((ROWS, C, H * DV)), v((H, KVR, DV)), v((W, H * DV)), v((H * DV, W)),
        v((2, ELOC, W, 2, FH)), v((ELOC, 2, W, FF)), v((2, ELOC, W, FH)), v((2, ELOC, FH, W)),
        v((2, 4, GROUP, W)), v((2, 4, GROUP, W)), v((1, 128), F32), v((C, 1, 128), F32),
        v((1, 128), F32), v((G, 1, 128), F32),
        v((2, ELOC, ESL, HALF)), v((2, ELOC, ESL, HALF)), v((2, HALF, SLOTS)), v((2, ELOC, ESL, 128), F32),
        v((2, 4, SLOTS, QC)), v((2, 2, 6, ESL, QC)), v((2, 2, 2, ESL, QC)), v((2, 2, 2, ESL, QC)),
        v((2, 2, 4, QR, QC)), v((2, 4, SLOTS, QC // 2)), v((2, SLOTS, W)), v((2, SLOTS, W)),
        v((2, HALF, W)), v((2, HALF, W)), v((2, 4, GROUP, W)), v((G, GROUP, W)),
        v((2, HALF, W), F32),
        dma(14), dma(18), dma(13), dma(2 * ROWS), dma(G), dma(G), dma(G), dma(12), dma(4), dma(2),
    ]
    vm = pl.BlockSpec(memory_space=pltpu.VMEM)
    hbm = pl.BlockSpec(memory_space=pl.ANY)
    return pl.pallas_call(
        functools.partial(kernel, G, C, ELOC, capacity),
        out_shape=jax.ShapeDtypeStruct((GROUP, W), BF16),
        in_specs=[hbm] * 14,
        out_specs=vm,
        scratch_shapes=scratch,
        compiler_params=pltpu.CompilerParams(
            collective_id=0, has_side_effects=True, vmem_limit_bytes=56 << 20
        ),
        cost_estimate=pl.CostEstimate(flops=4 << 30, bytes_accessed=16 << 20, transcendentals=1 << 20),
        name="decode_step",
    )(
        queries, new_latent, pool_pages, page_owner, page_slot, lengths, residual, value_weight,
        output_weight.T, norm_gain.reshape(1, W), expert_ids.T, route_gates.T, expert_in,
        jnp.swapaxes(expert_out, 1, 2),
    )


def solution(mesh):
    in_specs = (
        P(("dp", "expert"), None, None),
        P(("dp", "expert"), None),
        P(("dp", "expert"), None, None),
        P(None, "expert", None, None),
        P(None, "expert", None, None),
        P(("dp", "expert")),
        P("dp", "expert"),
        P(),
        P(None, "expert"),
        P("expert"),
        P("dp", None),
        P("dp", None),
        P("dp", "expert", None, None),
        P("dp", None, "expert"),
    )
    return jax.shard_map(
        body, mesh=mesh, in_specs=in_specs, out_specs=P("dp", "expert"), check_vma=False
    )
```

```python
import functools
import jax
import jax.numpy as jnp
from jax import lax
from jax.experimental import pallas as pl
from jax.experimental.pallas import tpu as pltpu
from jax.sharding import PartitionSpec as P

D = 7168
KVR = 512
ROPE = 64
DV = 128
TOP = 8
EPS = 1e-06
MESH = pl.DeviceIdType.MESH
F32 = jnp.float32
BF16 = jnp.bfloat16
NEG = -1e30
WAVES = ((4, -3, 3, -2), (0, 1, -1, 2))
POS = {off: 4 * w + t for w in range(2) for t, off in enumerate(WAVES[w])}
ME = POS[0]
BACK = {off: POS[4 if off == 4 else -off] for off in POS}


def iota(shape, dim):
    return lax.broadcasted_iota(jnp.int32, shape, dim)


def mm(a, b):
    return jnp.dot(a, b, preferred_element_type=F32)


def mm_nt(a, b):
    return lax.dot_general(a, b, (((1,), (1,)), ((), ())), preferred_element_type=F32)


def kernel(
    G, C, ELOC, CAPX,
    q_hbm, nl_hbm, pool_hbm, owner_hbm, slot_hbm, len_hbm, res_hbm, wv_hbm, wo_hbm, gain_hbm,
    ids_hbm, gates_hbm, win_hbm, wout_hbm,
    out_ref,
    nl_ref, owner_ref, slot_ref, len_ref, res_ref, gain_ref, ids_ref, gates_ref,
    kc, vt, nlp, q_in, q_main, q_rope, len_r, sml_s, sml_r, perm, perm_t, o_all, o_hm, hv_hm, hv_s, lse_s, hv_r,
    lse_r, hva, xmat, wv, wo, wot, win, wg, wout, woutt, xall, xsib, sq_s, sq_r, inv_s, inv_r,
    sel, sel_g, sel_t, gcol, part, in1, out1, b2, in2, hid, vown, vsib, zsib_s, zsib_r, zs, zr, zown,
    lsem, sent, heard, r_rows, r_q, r_rope, r_x, r_p1, r_p2, r_hid,
):
    g = lax.axis_index("dp")
    k = lax.axis_index("expert")
    core = lax.rem(k, 2)
    chip = lax.div(k, 2)
    sib = k + 1 - 2 * core
    cx = lax.rem(chip, 4)
    cy = lax.div(chip, 4)
    ROWS, H, LAT = q_in.shape
    NS = pool_hbm.shape[0]
    PAGE = pool_hbm.shape[2]
    RH = ROWS * H
    GROUP = C * ROWS
    W = res_ref.shape[1]
    FF = win_hbm.shape[3]
    FH = FF // 2
    ESL = 4 * CAPX
    QR = ESL // 2
    QF = FH // 4
    NR = G * ROWS

    def dp_peer(d):
        half = lax.div(G + 1 - d, 2)
        off = half * (1 - 2 * lax.rem(G + 1 - d, 2))
        return lax.rem(g + off + G, G)

    def at_dp(off):
        return lax.rem(g + off + G, G)

    def ex_peer(d):
        return lax.rem(k + d, C)

    def at_chip(ox, oy):
        x = lax.rem(cx + ox + 4, 4)
        y = lax.rem(cy + oy + 4, 4)
        return x, y, (g, 2 * (4 * y + x) + core)

    s_q, s_sml, s_hv, s_lse, s_hva, s_x, s_fw, s_sq = (sent.at[i] for i in range(8))
    s_inv, s_p1, s_p2, s_hid, s_win, s_wout, s_zsib, s_z = (sent.at[8 + i] for i in range(8))
    r_sml, r_lse, r_inv, r_z, r_sq, r_win, r_wout = (heard.at[i] for i in range(7))
    s_rope, s_len, r_len = sent.at[16], sent.at[17], heard.at[12]
    r_fwd, r_zsib = (heard.at[8], heard.at[9]), (heard.at[10], heard.at[11])

    def rcopy(src, dst, ss, rs, dev):
        return pltpu.make_async_remote_copy(
            src_ref=src, dst_ref=dst, send_sem=ss, recv_sem=rs, device_id=dev, device_id_type=MESH
        )

    def sent_all(ref, sem):
        rcopy(ref, ref, sem, sem, exp_dev(sib)).wait_send()

    def heard_all(ref, sem):
        rcopy(ref, ref, sem, sem, exp_dev(sib)).wait_recv()

    def loop(lo, hi, fn):
        lax.fori_loop(lo, hi, lambda i, c: (fn(i), c)[1], 0)

    def exp_dev(kk):
        return (g, kk)

    def dp_dev(j):
        return (j, k)

    locals_ = []
    for s in range(NS):
        locals_.append(
            pltpu.make_async_copy(pool_hbm.at[s], kc.at[:, pl.ds(s * PAGE, PAGE)], lsem.at[0])
        )
    c_q = pltpu.make_async_copy(q_hbm, q_in, lsem.at[1])
    c_win = pltpu.make_async_copy(
        win_hbm.at[:, :, :, pl.ds(pl.multiple_of(core * FH, FH), FH)], win.at[0], lsem.at[2]
    )
    c_wv = pltpu.make_async_copy(wv_hbm, wv, lsem.at[3])
    c_wo = pltpu.make_async_copy(wo_hbm, wo, lsem.at[4])
    c_wout = pltpu.make_async_copy(
        wout_hbm.at[:, :, pl.ds(pl.multiple_of(core * FH, FH), FH)], wout.at[0], lsem.at[5]
    )
    c_q.start()
    small = []
    for i, (a, b) in enumerate(
        (
            (ids_hbm, ids_ref), (gates_hbm, gates_ref), (len_hbm, len_ref), (nl_hbm, nl_ref),
            (owner_hbm, owner_ref), (slot_hbm, slot_ref), (res_hbm, res_ref), (gain_hbm, gain_ref),
        )
    ):
        small.append(pltpu.make_async_copy(a, b, lsem.at[6 + i]))
        small[-1].start()
    for c in locals_:
        c.start()
    for c in (c_win, c_wv, c_wo, c_wout):
        c.start()

    barrier = pltpu.get_barrier_semaphore()

    def sig_dp(d):
        pl.semaphore_signal(barrier, inc=1, device_id=dp_dev(lax.rem(g + d, G)), device_id_type=MESH)

    def sig_ex(d):
        pl.semaphore_signal(barrier, inc=1, device_id=exp_dev(ex_peer(d)), device_id_type=MESH)

    loop(0, C - 1, lambda d: sig_ex(1 + lax.rem(d + C // 2 - 1, C - 1)))
    loop(1, G, sig_dp)

    c_q.wait()
    small[2].wait()
    q_main[g] = q_in[:, :, 0:KVR]
    q_rope[g] = jnp.concatenate([q_in[r, :, KVR:LAT] for r in range(ROWS)], axis=1)
    lane = iota((1, 128), 1)
    lens = jnp.zeros((1, 128), F32)
    for r in range(ROWS):
        lens = jnp.where(lane == r, len_ref[r].astype(F32), lens)
    len_r[g] = lens
    pl.semaphore_wait(barrier, G - 1 + C - 1)

    def q_copy(src, off):
        ref = q_main.at[src]
        return rcopy(ref, ref, s_q, r_q.at[src], dp_dev(at_dp(off)))

    def rope_copy(src, off):
        ref = q_rope.at[src]
        return rcopy(ref, ref, s_rope, r_rope.at[src], dp_dev(at_dp(off)))

    def len_copy(off):
        ref = len_r.at[g]
        return rcopy(ref, ref, s_len, r_len, dp_dev(at_dp(off)))

    others = [4, -3, 3, -2, 2, -1, 1]
    for off in others:
        len_copy(off).start()
    def send_q(off):
        q_copy(g, off).start()
        rope_copy(g, off).start()

    send_q(2)
    send_q(-2)

    for i, c in enumerate(small):
        if i != 2:
            c.wait()
    ids = ids_ref[...]
    gates = gates_ref[...]
    e_iota = iota((G * ELOC, GROUP), 0)
    named = jnp.zeros((G * ELOC, GROUP), F32)
    gval = jnp.zeros((G * ELOC, GROUP), F32)
    for t in range(TOP):
        hit = ids[t : t + 1, :] == e_iota
        named = named + hit.astype(F32)
        gval = gval + jnp.where(hit, gates[t : t + 1, :], 0.0)
    tri = (iota((GROUP, GROUP), 0) < iota((GROUP, GROUP), 1)).astype(BF16)
    rank = mm(named.astype(BF16), tri)
    code = jnp.where(named > 0, rank, -1.0)
    sml_s[...] = jnp.zeros_like(sml_s)
    for j in range(G):
        sml_s[j, 0:ELOC, 0:GROUP] = code[j * ELOC : (j + 1) * ELOC]
        sml_s[j, ELOC : 2 * ELOC, 0:GROUP] = gval[j * ELOC : (j + 1) * ELOC]
    sml_r[ME] = sml_s[g]

    N2 = NR * H
    pr = iota((N2, 1), 0)
    perm[...] = (iota((N2, N2), 1) == lax.rem(pr, NR) * H + lax.div(pr, NR)).astype(BF16)
    perm_t[...] = (iota((N2, N2), 1) == lax.rem(pr, H) * NR + lax.div(pr, H)).astype(BF16)
    rr = iota((GROUP, GROUP), 0)
    rc = iota((GROUP, GROUP), 1)
    to_split = (rc == lax.rem(rr, C) * ROWS + lax.div(rr, C)).astype(BF16)
    from_split = (rr == lax.rem(rc, C) * ROWS + lax.div(rc, C)).astype(BF16)
    nl = nl_ref[...].astype(F32)
    nrow = iota((128, LAT), 0)
    nacc = jnp.zeros((128, LAT), F32)
    for s in range(ROWS):
        nacc = jnp.where(nrow == s, nl[s : s + 1, :], nacc)
    nlp[...] = nacc.astype(BF16)

    other = pl.multiple_of((1 - core) * FH, FH)
    w1 = rcopy(win_hbm.at[:, :, :, pl.ds(other, FH)], win.at[1], s_win, r_win, exp_dev(sib))
    w2 = rcopy(wout_hbm.at[:, :, pl.ds(other, FH)], wout.at[1], s_wout, r_wout, exp_dev(sib))
    w1.start()
    w2.start()

    pltpu.make_async_copy(kc, kc, lsem.at[0]).wait()
    vt[...] = kc[0:KVR, :].T

    scale = (DV + ROPE) ** (-0.5)
    NT = NS * PAGE

    def attend(src, own):
        q = q_main[src].reshape(RH, KVR)
        ropes = q_rope[src]
        qr = jnp.concatenate([ropes[:, r * ROPE : (r + 1) * ROPE] for r in range(ROWS)], axis=0)
        sc = (mm(q, kc[0:KVR, :]) + mm(qr, kc[KVR:LAT, :])) * scale
        lid = iota((1, NT), 1)
        slot_lane = lax.div(lid, PAGE)
        tpos = lax.rem(lid, PAGE).astype(F32)
        rows = []
        for s in range(ROWS):
            ln = len_r[src][0:1, s : s + 1]
            cnt = jnp.zeros((1, NT), F32)
            for p in range(owner_ref.shape[3]):
                here = jnp.where(owner_ref[src, 0, s, p] == g, slot_ref[src, 0, s, p], -1)
                ok = jnp.logical_and(slot_lane == here, tpos + float(p * PAGE) < ln)
                cnt = cnt + ok.astype(F32)
            rows.append(jnp.broadcast_to(cnt, (H, NT)))
        cnt = jnp.concatenate(rows, axis=0)
        scm = jnp.where(cnt > 0, sc, NEG)
        top = jnp.max(scm, axis=1, keepdims=True)
        if own:
            cs = (iota((RH, 128), 1) == lax.div(iota((RH, 128), 0), H)).astype(F32)
            ss = (mm_nt(q, nlp[:, 0:KVR]) + mm_nt(qr, nlp[:, KVR:LAT])) * scale
            ss = jnp.where(cs > 0, ss, NEG)
            top = jnp.maximum(top, jnp.max(ss, axis=1, keepdims=True))
        p = cnt * jnp.exp(scm - top)
        den = jnp.sum(p, axis=1, keepdims=True)
        acc = mm(p.astype(BF16), vt[...])
        if own:
            pself = cs * jnp.exp(ss - top)
            den = den + jnp.sum(pself, axis=1, keepdims=True)
            acc = acc + mm(pself.astype(BF16), nlp[:, 0:KVR])
        has = den > 0
        inv_den = jnp.where(has, 1.0 / jnp.where(has, den, 1.0), 0.0)
        lse = jnp.where(has, top + jnp.log(jnp.where(has, den, 1.0)), NEG)
        o_all[pl.ds(pl.multiple_of(src * RH, RH), RH), :] = (acc * inv_den).astype(BF16)
        row = jnp.broadcast_to(lse, (RH, 128)).T[0:1]
        lse_s[src] = jnp.concatenate([row, row], axis=1)

    attend(g, True)

    send_q(1)
    send_q(-1)

    col = iota((W, 2 * W), 1)
    two = 2 * iota((W, 2 * W), 0)
    pick_g = (col == two).astype(BF16)
    pick_u = (col == two + 1).astype(BF16)

    def split(o, e):
        w = win[o, e].reshape(2 * W, FH)
        wgate = mm(pick_g, w).astype(BF16)
        wup = mm(pick_u, w).astype(BF16)
        for f in range(4):
            wg[e, o, :, 2 * f * QF : (2 * f + 1) * QF] = wgate[:, f * QF : (f + 1) * QF]
            wg[e, o, :, (2 * f + 1) * QF : 2 * (f + 1) * QF] = wup[:, f * QF : (f + 1) * QF]

    c_wo.wait()
    wot[...] = wo[...].T

    for i, off in ((0, -2), (1, 2)):
        src = at_dp(off)
        heard_all(q_main.at[src], r_q.at[src])
        heard_all(q_rope.at[src], r_rope.at[src])
        q_copy(src, 1 - 2 * i).start()
        rope_copy(src, 1 - 2 * i).start()
        row = q_main.at[src, i]
        rcopy(row, row, s_q, r_q.at[src], dp_dev(at_dp(2 - 4 * i))).start()
        if i == 0:
            rope_copy(src, 2).start()
    heard_all(len_r.at[pl.ds(0, G - 1)], r_len)

    def sml_copy(off, n):
        j = at_dp(off)
        return rcopy(sml_s.at[j], sml_r.at[n], s_sml, r_sml, dp_dev(j))

    for off in others:
        sml_copy(off, BACK[off]).start()

    def ring(d):
        n = lax.div(d, 2)
        m = jnp.where(n == 0, 2, jnp.where(n == 1, 1, n + 1))
        return at_dp(jnp.where(lax.rem(d, 2) == 0, -m, m))

    def near(d):
        attend(ring(d), False)

    def chunk(d):
        src = ring(d)
        heard_all(q_main.at[src], r_q.at[src])
        heard_all(q_rope.at[src], r_rope.at[src])
        attend(src, False)

    loop(0, 2, near)
    loop(2, G - 2, chunk)
    far = at_dp(G // 2)
    heard_all(q_main.at[far], r_q.at[far])
    heard_all(q_rope.at[far], r_rope.at[far])
    attend(far, False)

    o_hm[...] = mm(perm[...], o_all[...]).astype(BF16)
    c_wv.wait()
    HB = 32

    def project(b):
        for i in range(HB):
            h = b * HB + i
            at = pl.ds(pl.multiple_of(h * NR, NR), NR)
            hv_hm[at, :] = mm(o_hm[at, :], wv[h]).astype(BF16)

    loop(0, H // HB, project)
    hv_s[...] = mm(perm_t[...], hv_hm[...]).astype(BF16).reshape(G, RH, DV)
    hv_r[g] = hv_s[g]
    lse_r[g] = lse_s[g]

    def part_of(r):
        return pl.ds(r * H, H)

    def send_hv(r, d):
        j = dp_peer(d)
        if r == 0:
            rcopy(lse_s.at[j], lse_r.at[g], s_lse, r_lse, dp_dev(j)).start()
        rcopy(
            hv_s.at[j, part_of(r)], hv_r.at[g, part_of(r)], s_hv, r_rows.at[r], dp_dev(j)
        ).start()

    for r in range(ROWS):
        loop(1, G, functools.partial(send_hv, r))

    heard_all(win.at[1], r_win)
    loop(0, ELOC, lambda e: split(1, e))
    heard_all(sml_r.at[pl.ds(0, G - 1)], r_sml)
    siota = iota((ESL, 4 * GROUP), 0).astype(F32)
    codes_in = sml_r[:, :, 0:GROUP].reshape(8 * G, GROUP).astype(BF16)
    split_codes = mm(codes_in, from_split)

    def slots(rows, w, e):
        return jnp.concatenate(
            [jnp.where(c >= 0, c + float(t * CAPX), -1.0) for t, c in enumerate(rows)], axis=1
        )

    for w in range(2):
        for e in range(ELOC):
            ns = [4 * w + t for t in range(4)]
            given = siota == slots([sml_r[n, e : e + 1, 0:GROUP] for n in ns], w, e)
            halved = siota == slots([split_codes[8 * n + e : 8 * n + e + 1] for n in ns], w, e)
            sel[w, e] = halved.astype(F32).astype(BF16)
            sel_g[w, e] = given.astype(F32).astype(BF16)
            gvals = [sml_r[n, ELOC + e : ELOC + e + 1, 0:GROUP] for n in ns]
            gs = jnp.where(given, jnp.concatenate(gvals, axis=1), 0.0)
            gcol[w, e] = jnp.broadcast_to(jnp.sum(gs, axis=1, keepdims=True), (ESL, 128))
        sel_t[w] = sel_g[w].reshape(ELOC * ESL, 4 * GROUP).T
    res_split = mm(to_split, res_ref[...])

    heard_all(lse_r.at[pl.ds(0, G - 1)], r_lse)
    riota = iota((8, 128), 0)
    ls = jnp.full((8, 128), NEG, F32)
    for j in range(G):
        ls = jnp.where(riota == j, lse_r[j], ls)
    wts = jnp.exp(ls - jnp.max(ls, axis=0, keepdims=True))
    wts = wts / jnp.sum(wts, axis=0, keepdims=True)
    wcol = wts.T
    plane = [(2, 2), (2, 1), (2, -1), (1, 2), (-1, 2), (2, 0), (0, 2)]
    plane += [(1, 1), (1, -1), (-1, 1), (-1, -1), (1, 0), (-1, 0), (0, 1), (0, -1)]

    for r in range(ROWS):
        heard_all(hv_r.at[pl.ds(0, G - 1), part_of(0)], r_rows.at[r])
        comb = jnp.zeros((H, DV), F32)
        for j in range(G):
            at = slice(r * H, (r + 1) * H)
            comb = comb + wcol[at, j : j + 1] * hv_r[j, at].astype(F32)
        hva[r, k] = comb.astype(BF16)
        for ox, oy in plane:
            x, y, dev = at_chip(ox, oy)
            for kk in (2 * (4 * y + x) + core, 2 * (4 * y + x) + 1 - core):
                rcopy(hva.at[r, k], hva.at[r, k], s_hva, r_rows.at[ROWS + r], exp_dev(kk)).start()
        rcopy(hva.at[r, k], hva.at[r, k], s_hva, r_rows.at[ROWS + r], exp_dev(sib)).start()

    def half(r):
        return pl.ds(r * C, C)

    def x_copy(off, n, r):
        ref = xall.at[n // 4, n % 4, half(r)]
        return rcopy(xall.at[1, 0, half(r)], ref, s_x, r_x.at[n], dp_dev(at_dp(off)))

    def fwd(n):
        src, dst = xall.at[n // 4, n % 4], xsib.at[n // 4, n % 4]
        return rcopy(src, dst, s_fw, r_fwd[n // 4], exp_dev(sib))

    c_win.wait()
    loop(0, ELOC, lambda e: split(0, e))

    c_wout.wait()
    heard_all(wout.at[1], r_wout)
    for o in range(2):
        for e in range(ELOC):
            woutt[o, e] = wout[o, e].T

    resids = []
    for r in range(ROWS):
        heard_all(hva.at[r, pl.ds(0, C - 1)], r_rows.at[ROWS + r])
        both = [hva[r, b * NR : (b + 1) * NR].reshape(N2, DV) for b in range(C // NR)]
        blk = mm(perm[...], jnp.concatenate(both, axis=1)).astype(BF16)
        for b in range(C // NR):
            for h in range(H):
                xmat[r, b * NR : (b + 1) * NR, h * DV : (h + 1) * DV] = blk[
                    h * NR : (h + 1) * NR, b * DV : (b + 1) * DV
                ]
        proj = mm(xmat[r], wot[...])
        resids.append((res_split[r * C : (r + 1) * C] + proj).astype(BF16).astype(F32))
        xall[1, 0, r * C : (r + 1) * C] = (resids[r] * gain_ref[...]).astype(BF16)
        for off in others:
            x_copy(off, BACK[off], r).start()
    fwd(ME).start()
    resid = jnp.concatenate(resids, axis=0)
    sq = jnp.sum(resid * resid, axis=1, keepdims=True)
    sq_row = jnp.broadcast_to(sq, (GROUP, 128)).T[0:1]
    sq_s[...] = jnp.concatenate([sq_row] * (128 // GROUP), axis=1)
    sq_r[k] = sq_s[...]

    def send_sq(d):
        j = ex_peer(d)
        rcopy(sq_s, sq_r.at[k], s_sq, r_sq, exp_dev(j)).start()

    loop(1, C, send_sq)

    def get_x(w):
        for off in sorted(WAVES[w], key=abs):
            if off != 0:
                n = POS[off]
                heard_all(xall.at[n // 4, n % 4], r_x.at[n])
                fwd(n).start()
        heard_all(xsib.at[w], r_fwd[w])

    place = (cx, cy)

    def along(h, off):
        return at_chip(off, 0)[2] if h == 0 else at_chip(0, off)[2]

    def across(h, off):
        return at_chip(0, off)[2] if h == 0 else at_chip(off, 0)[2]

    def ring1(w, h, slot, src):
        sem = r_p1.at[3 * (2 * w + h) + min(slot, 2)]
        return rcopy(src, in1.at[w, h, slot], s_p1, sem, along(h, 1 if slot in (0, 2, 3) else -1))

    def block(e):
        return pl.ds(pl.multiple_of(e * ESL, 16), ESL)

    def partials(w):
        def step(i):
            e = lax.rem(cx + 2 + 3 * i, 4)
            xo = mm(sel[w, e], xall[w].reshape(4 * GROUP, W)).astype(BF16)
            xs = mm(sel[w, e], xsib[w].reshape(4 * GROUP, W)).astype(BF16)
            for f in range(4):
                cols = slice(2 * f * QF, 2 * (f + 1) * QF)
                both = mm(xo, wg[e, 0, :, cols]) + mm(xs, wg[e, 1, :, cols])
                part[w, f, block(e)] = both.astype(BF16)
            for h in range(2):
                role = lax.rem(e - place[h] + 4, 4)

                @pl.when(role == 2)
                def _():
                    ring1(w, h, 0, part.at[w, 2 * h, block(e)]).start()
                    ring1(w, h, 1, part.at[w, 2 * h + 1, block(e)]).start()

                @pl.when(role == 1)
                def _():
                    ring1(w, h, 2, part.at[w, 2 * h + 1, block(e)]).start()

                @pl.when(role == 3)
                def _():
                    ring1(w, h, 4, part.at[w, 2 * h, block(e)]).start()

        loop(0, 4, step)

    def relay(w):
        for h in range(2):
            for i in range(2):
                to = lax.rem(place[h] + (1, 3)[i], 4)
                ring1(w, h, i, in1.at[w, h, i]).wait_recv()
                passed = part[w, 2 * h + i, block(to)].astype(F32) + in1[w, h, i].astype(F32)
                out1[w, h, i] = passed.astype(BF16)
                ring1(w, h, 3 + 2 * i, out1.at[w, h, i]).start()

    def rows2(p):
        return pl.ds(pl.multiple_of(lax.div(p, 2) * QR, 16), QR)

    def ring2(w, h, off):
        to = lax.rem(place[1 - h] + off, 4)
        src = b2.at[w, h, lax.rem(to, 2), rows2(to)]
        return rcopy(src, in2.at[w, h, 4 - off], s_p2, r_p2.at[2 * w + h], across(h, off))

    def second(w):
        for h in range(2):
            heard_all(in1.at[w, h, pl.ds(2, 4)], r_p1.at[3 * (2 * w + h) + 2])
            for i in range(2):
                own = part[w, 2 * h + i, block(place[h])].astype(F32)
                got = in1[w, h, 4 - 2 * i].astype(F32) + in1[w, h, 3 + 2 * i].astype(F32)
                b2[w, h, i] = (own + got).astype(BF16)
            for off in (2, 1, 3):
                ring2(w, h, off).start()
            p = place[1 - h]
            in2[w, h, 0] = b2[w, h, lax.rem(p, 2), rows2(p)]

    def piece(w, h, x, y):
        p = (x, y)
        at = p[h] * ESL + lax.div(p[1 - h], 2) * QR
        return w, 2 * h + lax.rem(p[1 - h], 2), pl.ds(pl.multiple_of(at, 16), QR)

    def hid_copy(w, h, dev):
        ref = hid.at[piece(w, h, cx, cy)]
        return rcopy(ref, ref, s_hid, r_hid.at[w], dev)

    def hidden(w):
        irow = jnp.concatenate([inv_r[4 * w + t, 0:1, 0:GROUP] for t in range(4)], axis=1)
        for h in range(2):
            mine = sel[w, place[h], rows2(place[1 - h]), :]
            icol = jnp.sum(mine.astype(F32) * irow, axis=1, keepdims=True)
            heard_all(in2.at[w, h, pl.ds(1, 3)], r_p2.at[2 * w + h])
            tot = in2[w, h, 0].astype(F32)
            for j in range(1, 4):
                tot = tot + in2[w, h, j].astype(F32)
            tot = tot * icol
            ga = tot[:, 0:QF]
            hv = ga / (1.0 + jnp.exp(-ga)) * tot[:, QF : 2 * QF]
            hid[piece(w, h, cx, cy)] = hv.astype(BF16)
            for ox, oy in plane:
                hid_copy(w, h, at_chip(ox, oy)[2]).start()

    def down(w):
        heard_all(wv.at[pl.ds(0, 30), pl.ds(0, QR)], r_hid.at[w])

        def out(o, into):
            for e in range(ELOC):
                at = slice(e * ESL, (e + 1) * ESL)
                he = jnp.concatenate([hid[w, f, at] for f in range(4)], axis=1)
                into[w, at, :] = (mm(he, woutt[o, e]) * gcol[w, e, :, 0:1]).astype(BF16)

        out(1, vsib)
        zsib_s[w] = mm(sel_t[w], vsib[w]).astype(BF16)
        zsib_copy(w).start()
        out(0, vown)
        zown[w] = mm(sel_t[w], vown[w])

    def zsib_copy(w):
        return rcopy(zsib_s.at[w], zsib_r.at[w], s_zsib, r_zsib[w], exp_dev(sib))

    def z_copy(off, n):
        ref = zs.at[POS[off] // 4, POS[off] % 4]
        return rcopy(ref, zr.at[n], s_z, r_z, dp_dev(at_dp(off)))

    def give_back(w):
        zsib_copy(w).wait_recv()
        zsum = zown[w] + zsib_r[w].astype(F32)
        zown[w] = zsum
        zs[w] = zsum.astype(BF16).reshape(4, GROUP, W)
        for off in sorted(WAVES[w], key=lambda o: -abs(o)):
            if off != 0:
                z_copy(off, BACK[off]).start()

    get_x(0)
    partials(0)

    heard_all(sq_r.at[pl.ds(0, C - 1)], r_sq)
    inv_s[...] = lax.rsqrt(jnp.sum(sq_r[...], axis=0) / D + EPS)
    inv_r[ME] = inv_s[...]

    def inv_copy(off, n):
        return rcopy(inv_s, inv_r.at[n], s_inv, r_inv, dp_dev(at_dp(off)))

    for off in others:
        inv_copy(off, BACK[off]).start()
    get_x(1)
    partials(1)
    relay(0)
    relay(1)
    second(0)
    second(1)
    heard_all(inv_r.at[pl.ds(0, G - 1)], r_inv)
    hidden(0)
    hidden(1)
    down(0)
    give_back(0)
    down(1)
    give_back(1)
    total = mm(from_split, resid.astype(BF16)) + zown[1, 0:GROUP, :]

    w1.wait_send()
    w2.wait_send()
    seven = pl.ds(0, G - 1)
    sent_all(q_main.at[seven], s_q)
    sent_all(q_rope.at[seven], s_rope)
    sent_all(len_r.at[seven], s_len)
    sent_all(sml_r.at[seven], s_sml)
    sent_all(hv_r.at[seven], s_hv)
    sent_all(lse_r.at[seven], s_lse)
    sent_all(hva.at[:, pl.ds(0, C - 1)], s_hva)
    sent_all(zr.at[seven], s_x)
    sent_all(zr, s_fw)
    sent_all(sq_r.at[pl.ds(0, C - 1)], s_sq)
    sent_all(inv_r.at[seven], s_inv)
    sent_all(in1, s_p1)
    sent_all(in2.at[:, :, pl.ds(0, 3)], s_p2)
    sent_all(wv.at[pl.ds(0, 30), pl.ds(0, 2 * QR)], s_hid)
    sent_all(zsib_r, s_zsib)

    heard_all(zr.at[seven], r_z)
    for off in others:
        total = total + zr[POS[off]].astype(F32)
    out_ref[...] = total.astype(BF16)
    sent_all(zr.at[seven], s_z)


def body(
    queries, new_latent, pool_pages, page_owner, page_slot, lengths, residual, value_weight,
    output_weight, norm_gain, expert_ids, route_gates, expert_in, expert_out,
):
    G = lax.axis_size("dp")
    C = lax.axis_size("expert")
    ROWS, H, LAT = queries.shape
    NS, _, PAGE = pool_pages.shape
    GROUP, W = residual.shape
    ELOC, _, _, FF = expert_in.shape
    FH = FF // 2
    RH = ROWS * H
    capacity = min(GROUP, (3 * GROUP * TOP + 2 * G * ELOC - 1) // (2 * G * ELOC))
    ESL = 4 * capacity
    SLOTS = ELOC * ESL
    QR, QC = ESL // 2, FF // 4
    N2 = G * RH
    HALF = 4 * GROUP

    def v(shape, dtype=BF16):
        return pltpu.VMEM(shape, dtype)

    dma = lambda n: pltpu.SemaphoreType.DMA((n,))
    scratch = [
        v(new_latent.shape), pltpu.SMEM(page_owner.shape, jnp.int32),
        pltpu.SMEM(page_slot.shape, jnp.int32), pltpu.SMEM(lengths.shape, jnp.int32),
        v((GROUP, W)), v((1, W), F32), v((TOP, GROUP), jnp.int32), v((TOP, GROUP), F32),
        v((LAT, NS * PAGE)), v((NS * PAGE, KVR)), v((128, LAT)), v((ROWS, H, LAT)),
        v((G, ROWS, H, KVR)), v((G, H, ROWS * ROPE)), v((G, 1, 128), F32),
        v((G, 8, 128), F32), v((G, 8, 128), F32), v((N2, N2)), v((N2, N2)),
        v((N2, KVR)), v((N2, KVR)), v((N2, DV)), v((G, RH, DV)), v((G, 1, 128), F32),
        v((G, RH, DV)), v((G, 1, 128), F32),
        v((ROWS, C, H, DV)), v((ROWS, C, H * DV)), v((H, KVR, DV)), v((W, H * DV)), v((H * DV, W)),
        v((2, ELOC, W, 2, FH)), v((ELOC, 2, W, FF)), v((2, ELOC, W, FH)), v((2, ELOC, FH, W)),
        v((2, 4, GROUP, W)), v((2, 4, GROUP, W)), v((1, 128), F32), v((C, 1, 128), F32),
        v((1, 128), F32), v((G, 1, 128), F32),
        v((2, ELOC, ESL, HALF)), v((2, ELOC, ESL, HALF)), v((2, HALF, SLOTS)), v((2, ELOC, ESL, 128), F32),
        v((2, 4, SLOTS, QC)), v((2, 2, 6, ESL, QC)), v((2, 2, 2, ESL, QC)), v((2, 2, 2, ESL, QC)),
        v((2, 2, 4, QR, QC)), v((2, 4, SLOTS, QC // 2)), v((2, SLOTS, W)), v((2, SLOTS, W)),
        v((2, HALF, W)), v((2, HALF, W)), v((2, 4, GROUP, W)), v((G, GROUP, W)),
        v((2, HALF, W), F32),
        dma(14), dma(18), dma(13), dma(2 * ROWS), dma(G), dma(G), dma(G), dma(12), dma(4), dma(2),
    ]
    vm = pl.BlockSpec(memory_space=pltpu.VMEM)
    hbm = pl.BlockSpec(memory_space=pl.ANY)
    return pl.pallas_call(
        functools.partial(kernel, G, C, ELOC, capacity),
        out_shape=jax.ShapeDtypeStruct((GROUP, W), BF16),
        in_specs=[hbm] * 14,
        out_specs=vm,
        scratch_shapes=scratch,
        compiler_params=pltpu.CompilerParams(
            collective_id=0, has_side_effects=True, vmem_limit_bytes=56 << 20
        ),
        cost_estimate=pl.CostEstimate(flops=4 << 30, bytes_accessed=16 << 20, transcendentals=1 << 20),
        name="decode_step",
    )(
        queries, new_latent, pool_pages, page_owner, page_slot, lengths, residual, value_weight,
        output_weight.T, norm_gain.reshape(1, W), expert_ids.T, route_gates.T, expert_in,
        jnp.swapaxes(expert_out, 1, 2),
    )


def solution(mesh):
    in_specs = (
        P(("dp", "expert"), None, None),
        P(("dp", "expert"), None),
        P(("dp", "expert"), None, None),
        P(None, "expert", None, None),
        P(None, "expert", None, None),
        P(("dp", "expert")),
        P("dp", "expert"),
        P(),
        P(None, "expert"),
        P("expert"),
        P("dp", None),
        P("dp", None),
        P("dp", "expert", None, None),
        P("dp", None, "expert"),
    )
    return jax.shard_map(
        body, mesh=mesh, in_specs=in_specs, out_specs=P("dp", "expert"), check_vma=False
    )
```
